128 devices in a mesh: pair: 2 (over z_hi), dp: 64 (over x, y, z_lo, core).
Axes of the slice: x: 4, y: 4, z: 4 (z_hi: 2, z_lo: 2; z = z_hi * 2 + z_lo), core: 2. Of those that a mesh axis runs over, the one named last changes fastest.
Arguments:
- tokens: bfloat16 [2, 512, 128, 768], P('pair', 'dp'), may hold values from -6 to 6
- cotangent: bfloat16 [2, 512, 128, 768], P('pair', 'dp'), may hold values from -6 to 6
- span_counts: int32 [2, 64], P('pair', 'dp'), may hold values from 1 to 8, as said below
- single_flags: int32 [2, 512], P('pair', 'dp'), may hold values from 0 to 1, as said below
- partner_slots: int32 [2, 512], P('pair', 'dp'), may hold values from 0 to 7, as said below
- w_qkv: bfloat16 [768, 2304], P(('pair', 'dp')), may hold values from -0.3125 to 0.3125
- b_query: bfloat16 [768], P(('pair', 'dp')), may hold values from -3 to 3
- b_value: bfloat16 [768], P(('pair', 'dp')), may hold values from -3 to 3
- w_out: bfloat16 [768, 768], P(('pair', 'dp')), may hold values from -0.4375 to 0.4375
- b_out: bfloat16 [768], P(('pair', 'dp')), may hold values from -3 to 3
- gain_attn: bfloat16 [768], P(('pair', 'dp')), may hold values from 0.5 to 1.5
- shift_attn: bfloat16 [768], P(('pair', 'dp')), may hold values from -3 to 3
- w_in: bfloat16 [768, 3072], P(('pair', 'dp')), may hold values from -0.21875 to 0.21875
- b_in: bfloat16 [3072], P(('pair', 'dp')), may hold values from -3 to 3
- w_down: bfloat16 [3072, 768], P(('pair', 'dp')), may hold values from -0.109375 to 0.109375
- b_down: bfloat16 [768], P(('pair', 'dp')), may hold values from -3 to 3
- gain_ffn: bfloat16 [768], P(('pair', 'dp')), may hold values from 0.5 to 1.5
- shift_ffn: bfloat16 [768], P(('pair', 'dp')), may hold values from -3 to 3
Outputs:
- mixed: bfloat16 [2, 512, 128, 768], P('pair', 'dp')
- grad_tokens: bfloat16 [2, 512, 128, 768], P('pair', 'dp')
- grad_w_qkv: float32 [768, 2304], P(('pair', 'dp'))
- grad_b_query: float32 [768], P(('pair', 'dp'))
- grad_b_value: float32 [768], P(('pair', 'dp'))
- grad_w_out: float32 [768, 768], P(('pair', 'dp'))
- grad_b_out: float32 [768], P(('pair', 'dp'))
- grad_gain_attn: float32 [768], P(('pair', 'dp'))
- grad_shift_attn: float32 [768], P(('pair', 'dp'))
- grad_w_in: float32 [768, 3072], P(('pair', 'dp'))
- grad_b_in: float32 [3072], P(('pair', 'dp'))
- grad_w_down: float32 [3072, 768], P(('pair', 'dp'))
- grad_b_down: float32 [768], P(('pair', 'dp'))
- grad_gain_ffn: float32 [768], P(('pair', 'dp'))
- grad_shift_ffn: float32 [768], P(('pair', 'dp'))
The draws below stay inside these ranges and needn't reach their ends.
Inputs may be any that keep to these rules, and one draw needn't show every extreme that they name: `span_counts`: live slots of a device are slots 0 to count - 1; in every draw some device holds 8 live spans. `single_flags`: 1 only for a live span whose document has a single span; 0 for paired spans and empty slots; both sides of a dp index hold equally many paired spans. `partner_slots`: for a paired span, the slot of its partner on the other side at the same dp index, whose partner is it again; for any other slot, the slot itself.
All inputs are finite; a program needn't handle non-finite values.
Results may differ from the reference program's by a relative error of at most 0.015.
The reference program's roundings to bfloat16 on the way count: a program that leaves them out, or rounds other values in their place, can miss the bound.
Values may be sent and summed in bfloat16 or wider, within the bound.
No kernel may reach another device: no remote copies, remote signals or barrier semaphores. Data moves between devices by JAX's collectives and lax.ppermute only.
A program may use at most 192 MiB of HBM per device.

```python
import jax
import jax.numpy as jnp
from jax import lax

D = 768
HEADS = 12
HEAD_DIM = 64
FF = 3072
SPAN_LEN = 128
SPANS = 8
SIDES = 2
SPANS_ALL = 512


def span_plan(key):
    ndp = SPANS_ALL // SPANS
    key_pairs, key_star, key_single, key_rank = jax.random.split(key, 4)
    pairs = jax.random.randint(key_pairs, (ndp,), 1, SPANS + 1)
    star = jax.random.randint(key_star, (), 0, ndp)
    pairs = jnp.where(jnp.arange(ndp) == star, SPANS, pairs)
    singles = jax.random.randint(key_single, (2, ndp), 0, SPANS + 1)
    singles = jnp.minimum(singles, SPANS - pairs[None, :])
    counts = pairs[None, :] + singles
    slot = jnp.arange(SPANS, dtype=jnp.int32)
    scores = jax.random.randint(key_rank, (2, ndp, SPANS), 0, 1 << 20)
    scores = jnp.where(slot[None, None, :] < counts[:, :, None], scores, (1 << 20) + slot[None, None, :])
    order = jnp.argsort(scores, axis=-1, stable=True).astype(jnp.int32)
    rank = jnp.argsort(order, axis=-1, stable=True).astype(jnp.int32)
    paired = rank < pairs[None, :, None]
    live = slot[None, None, :] < counts[:, :, None]
    flags = jnp.where(live & jnp.logical_not(paired), 1, 0).astype(jnp.int32)
    other = jnp.take_along_axis(order[::-1], rank, axis=-1)
    partner = jnp.where(paired, other, slot[None, None, :]).astype(jnp.int32)
    return (counts.astype(jnp.int32), flags.reshape(2, SPANS_ALL), partner.reshape(2, SPANS_ALL))


def draw_span_counts(key, part):
    counts, flags, partner = span_plan(key)
    return counts


def draw_single_flags(key, part):
    counts, flags, partner = span_plan(key)
    return flags


def draw_partner_slots(key, part):
    counts, flags, partner = span_plan(key)
    return partner


def steps_of(own_key, extent, cuts, smallest, high):
    level, own = 1.0, jax.random.fold_in(own_key, 6)
    for dim, blocks in cuts:
        steps = jnp.exp(jax.random.uniform(jax.random.fold_in(own, dim), (blocks,), jnp.float32, smallest / len(cuts), high / len(cuts)))
        level = level * jnp.repeat(steps, extent[dim] // blocks).reshape([-1 if axis == dim else 1 for axis in range(len(extent))])
    return level


def bell_draw(key, shape, spread, limit, cuts=(), kind=jnp.bfloat16):
    values = spread * jax.random.normal(key, shape, jnp.float32)
    if cuts:
        values = values * steps_of(key, shape, cuts, -0.22, 0.18)
    return jnp.clip(values, -limit, limit).astype(kind)


def setup_inputs(seed: int = 0) -> dict:
    seeds = jax.random.split(jax.random.key(seed), 19)
    return {
        "tokens": bell_draw(seeds[0], (SIDES, SPANS_ALL, SPAN_LEN, D), 1.0, 6.0, ((0, 2), (1, 64))),
        "cotangent": bell_draw(seeds[1], (SIDES, SPANS_ALL, SPAN_LEN, D), 1.0, 6.0, ((0, 2), (1, 64))),
        "span_counts": draw_span_counts(jax.random.fold_in(seeds[18], 71), 0),
        "single_flags": draw_single_flags(jax.random.fold_in(seeds[18], 71), 0),
        "partner_slots": draw_partner_slots(jax.random.fold_in(seeds[18], 71), 0),
        "w_qkv": bell_draw(seeds[5], (D, 3 * D), (D // 2) ** -0.5, 0.3125, ((0, 128),)),
        "b_query": bell_draw(seeds[6], (D,), 0.5, 3.0, ((0, 128),)),
        "b_value": bell_draw(seeds[7], (D,), 0.5, 3.0, ((0, 128),)),
        "w_out": bell_draw(seeds[8], (D, D), (D // 4) ** -0.5, 0.4375, ((0, 128),)),
        "b_out": bell_draw(seeds[9], (D,), 0.5, 3.0, ((0, 128),)),
        "gain_attn": jnp.clip(1.0 + 0.1 * jax.random.normal(seeds[10], (D,), jnp.float32), 0.5, 1.5).astype(jnp.bfloat16),
        "shift_attn": bell_draw(seeds[11], (D,), 0.5, 3.0, ((0, 128),)),
        "w_in": bell_draw(seeds[12], (D, FF), D ** -0.5, 0.21875, ((0, 128),)),
        "b_in": bell_draw(seeds[13], (FF,), 0.5, 3.0, ((0, 128),)),
        "w_down": bell_draw(seeds[14], (FF, D), FF ** -0.5, 0.109375, ((0, 128),)),
        "b_down": bell_draw(seeds[15], (D,), 0.5, 3.0, ((0, 128),)),
        "gain_ffn": jnp.clip(1.0 + 0.1 * jax.random.normal(seeds[16], (D,), jnp.float32), 0.5, 1.5).astype(jnp.bfloat16),
        "shift_ffn": bell_draw(seeds[17], (D,), 0.5, 3.0, ((0, 128),)),
    }


@jax.custom_vjp
def low(v):
    return lax.optimization_barrier(v.astype(jnp.bfloat16)).astype(jnp.float32)

@jax.custom_vjp
def low_back(v):
    return v

def low_keep(v):
    return (low(v), None)

def low_pass(kept, grad):
    return (grad,)

def back_keep(v):
    return (v, None)

def back_low(kept, grad):
    return (low(grad),)
low.defvjp(low_keep, low_pass)
low_back.defvjp(back_keep, back_low)
epsilon = 1e-12
contrast_weight = 8.0
logit_scale = 0.0625

def layer_norm(resid, gain, shift):
    centered = resid - lax.optimization_barrier(jnp.mean(resid, axis=-1, keepdims=True))
    variance = lax.optimization_barrier(jnp.mean(centered * centered, axis=-1, keepdims=True))
    return centered * lax.rsqrt(variance + epsilon) * gain + shift

def gelu_exact(upper):
    return 0.5 * upper * (1.0 + jax.scipy.special.erf(upper * 0.7071067811865476))

def block(params, stretch_x, valid, keep, partner):
    w_qkv, b_query, b_value, w_out, b_out, gain_attn, shift_attn, w_in, b_in, w_down, b_down, gain_ffn, shift_ffn = params
    highest = lax.Precision.HIGHEST
    rows = stretch_x.reshape(-1, D)
    bias = jnp.concatenate([b_query, jnp.zeros_like(b_query), b_value])
    qkv = low(low_back(jnp.dot(rows, w_qkv, precision=highest) + bias))
    qkv = qkv.reshape(-1, SPAN_LEN, 3, HEADS, HEAD_DIM)
    query, keyed, valued = (qkv[:, :, 0], qkv[:, :, 1], qkv[:, :, 2])
    scores = low_back(jnp.einsum('sqhd,skhd->shqk', query, keyed, precision=highest) * HEAD_DIM ** (-0.5))
    probs = jax.nn.softmax(scores, axis=-1)
    heads_out = jnp.einsum('shqk,skhd->sqhd', low(probs), valued, precision=highest).reshape(-1, D)
    heads_out = low(low_back(heads_out))
    attn = low_back(jnp.dot(heads_out, w_out, precision=highest) + b_out)
    hidden_one = layer_norm(rows + attn, gain_attn, shift_attn)
    upper = low_back(jnp.dot(low(hidden_one), w_in, precision=highest) + b_in)
    active = low(gelu_exact(upper))
    down = low_back(jnp.dot(active, w_down, precision=highest) + b_down)
    final = layer_norm(hidden_one + down, gain_ffn, shift_ffn).reshape(stretch_x.shape)
    result = final * valid[..., None, None]
    first = final[:, :, :, 0, :]
    sent = low(low_back(first)) * keep[..., None]
    received = sent[::-1]
    logits = jnp.einsum('bgsd,bgtd->bgst', first, received, precision=highest) * logit_scale
    totals = jax.nn.logsumexp(logits, axis=-1)
    picked = jnp.take_along_axis(logits, partner[..., None], axis=-1)[..., 0]
    loss = contrast_weight * jnp.sum(keep * (totals - picked))
    return (result, loss)

def reference(tokens, cotangent, span_counts, single_flags, partner_slots, w_qkv, b_query, b_value, w_out, b_out, gain_attn, shift_attn, w_in, b_in, w_down, b_down, gain_ffn, shift_ffn):
    ndp = SPANS_ALL // SPANS
    group = max(1, 4096 // (2 * SPANS * SPAN_LEN))
    group = min(group, ndp)
    while ndp % group != 0:
        group = group - 1
    groups = ndp // group
    slot = jnp.arange(SPANS, dtype=jnp.int32)
    valid = (slot[None, None, :] < span_counts[:, :, None]).astype(jnp.float32)
    flags = single_flags.reshape(2, ndp, SPANS).astype(jnp.float32)
    keep = valid * (1.0 - flags)
    partner = partner_slots.reshape(2, ndp, SPANS).astype(jnp.int32)

    def grouped(arr):
        shaped = arr.reshape((2, groups, group) + arr.shape[2:])
        return jnp.moveaxis(shaped, 1, 0)
    x_groups = grouped(tokens.astype(jnp.float32).reshape(2, ndp, SPANS, SPAN_LEN, D))
    cot_groups = grouped(cotangent.astype(jnp.float32).reshape(2, ndp, SPANS, SPAN_LEN, D))
    valid_groups = grouped(valid)
    keep_groups = grouped(keep)
    partner_groups = grouped(partner)
    params = tuple((w.astype(jnp.float32) for w in (w_qkv, b_query, b_value, w_out, b_out, gain_attn, shift_attn, w_in, b_in, w_down, b_down, gain_ffn, shift_ffn)))
    saved_block = jax.checkpoint(block)

    def forward(x_all, weights):

        def step(total, items):
            stretch_x, valid_b, keep_b, partner_b = items
            result, loss = saved_block(weights, stretch_x, valid_b, keep_b, partner_b)
            return (total + loss, result)
        total, results = lax.scan(step, jnp.zeros((), jnp.float32), (x_all, valid_groups, keep_groups, partner_groups))
        return (results, total)
    (results, total), pull = jax.vjp(forward, x_groups, params)
    grad_x, grads = pull((cot_groups, jnp.ones((), jnp.float32)))

    def ungroup(arr):
        return jnp.moveaxis(arr, 0, 1).reshape(2, SPANS_ALL, SPAN_LEN, D)
    return (ungroup(results).astype(jnp.bfloat16), ungroup(grad_x).astype(jnp.bfloat16), grads[0], grads[1], grads[2], grads[3], grads[4], grads[5], grads[6], grads[7], grads[8], grads[9], grads[10], grads[11], grads[12])
```

```python
import functools

import jax
import jax.numpy as jnp
from jax import lax
from jax.experimental import pallas as pl
from jax.experimental.pallas import tpu as pltpu
from jax.sharding import PartitionSpec as P

HEADS = 12
HEAD_DIM = 64


epsilon = 1e-12
contrast_weight = 8.0
logit_scale = 0.0625

def from_partner(value, axis, bit):
    mask = 2**bit
    pairs = [(source, source ^ mask) for source in range(lax.axis_size(axis))]
    return lax.ppermute(value, axis, pairs)


def layer_norm(resid, gain, shift):
    centered = resid - jnp.mean(resid, axis=-1, keepdims=True)
    variance = jnp.mean(centered * centered, axis=-1, keepdims=True)
    return centered * lax.rsqrt(variance + epsilon) * gain + shift


def gelu_exact(upper):
    return 0.5 * upper * (1.0 + jax.scipy.special.erf(upper * 0.7071067811865476))


def contrast(first, received, keep, partner):
    logits = jnp.dot(first, received.T, precision=lax.Precision.HIGHEST) * logit_scale
    totals = jax.nn.logsumexp(logits, axis=-1)
    picked = jnp.take_along_axis(logits, partner[:, None], axis=-1)[:, 0]
    return contrast_weight * jnp.sum(keep * (totals - picked))


def outer_sum(left, right):
    return jnp.einsum("ti,to->io", left, right, preferred_element_type=jnp.float32)


AXES = ("pair", "dp")
UNIT = 48


def device_index(p, a, yh, yl, z, c):
    return ((((p * 4 + a) * 2 + yh) * 2 + yl) * 2 + z) * 2 + c


def all_places():
    return [
        (p, a, yh, yl, z, c)
        for p in range(2)
        for a in range(4)
        for yh in range(2)
        for yl in range(2)
        for z in range(2)
        for c in range(2)
    ]


def moved(place, stage, r):
    p, a, yh, yl, z, c = place
    if (stage == 0) == (c == 0):
        return (p ^ (r & 1), a, yh ^ (r >> 1), yl, z, c)
    return (p, (a + r) % 4, yh, yl, z, c)


def stage_pairs(stage, r, back=False):
    pairs = [(device_index(*moved(q, stage, r)), device_index(*q)) for q in all_places()]
    return [(t, s) for s, t in pairs] if back else pairs


def core_pairs():
    return [(d, d ^ 1) for d in range(128)]


def octets():
    return [[8 * g + k for k in range(8)] for g in range(16)]


def send(value, pairs):
    return lax.ppermute(value, AXES, pairs)


def exchange_octet(value):
    return lax.all_to_all(value, AXES, 0, 0, axis_index_groups=octets(), tiled=True)


def my_units():
    me = lax.axis_index("pair") * 64 + lax.axis_index("dp")
    c, yh, a, p = me & 1, (me >> 3) & 1, (me >> 4) & 3, me >> 6
    i = jnp.arange(16, dtype=jnp.int32)
    late, early = i >> 2, i & 3
    zero = (p ^ (early & 1)) * 8 + ((a + late) & 3) * 2 + (yh ^ (early >> 1))
    one = (p ^ (late & 1)) * 8 + ((a + early) & 3) * 2 + (yh ^ (late >> 1))
    return c, jnp.stack([zero, one]).astype(jnp.int32)


WIDE = (1152, 128, 384)
FIRST = sum(WIDE)
SECOND = 3072


def gather_stage(block, stage):
    return jnp.stack([block] + [send(block, stage_pairs(stage, r)) for r in (1, 2, 3)])


def gather_pieces(block):
    early = gather_stage(block, 0)
    mine = [early] + [send(early, stage_pairs(1, r)) for r in (1, 2, 3)]
    theirs = [send(piece, core_pairs()) for piece in mine]
    return mine, theirs


def place_kernel(layout, n_out, place, *refs):
    pieces, outs, sems = refs[:8], refs[8 : 8 + n_out], refs[8 + n_out]
    core = place[0]
    for side in range(2):
        half = core if side == 0 else 1 - core
        for k in range(16):
            unit = place[1 + half * 16 + k]
            block = pieces[4 * side + k // 4].at[k % 4]
            for n, (first, width, times) in enumerate(layout):
                to = pl.ds(pl.multiple_of(half * width, 128), width)
                for j in range(times):
                    pltpu.make_async_copy(
                        block.at[:, pl.ds(first + j * width, width)],
                        outs[n].at[pl.ds(pl.multiple_of((unit * times + j) * UNIT, 16), UNIT), to],
                        sems.at[side, n],
                    ).start()
    for side in range(2):
        half = core if side == 0 else 1 - core
        for n, (first, width, times) in enumerate(layout):
            whole = outs[n].at[:, pl.ds(pl.multiple_of(half * width, 128), width)]
            pltpu.make_async_copy(whole, whole, sems.at[side, n]).wait()


def place_weights(place, mine, theirs, layout):
    shapes = [jax.ShapeDtypeStruct((768 * t, 2 * w), jnp.bfloat16) for _, w, t in layout]
    return pl.pallas_call(
        functools.partial(place_kernel, layout, len(layout)),
        out_shape=shapes,
        in_specs=[pl.BlockSpec(memory_space=pltpu.SMEM)] + [pl.BlockSpec(memory_space=pl.ANY)] * 8,
        out_specs=[pl.BlockSpec(memory_space=pltpu.VMEM)] * len(layout),
        scratch_shapes=[pltpu.SemaphoreType.DMA((2, len(layout)))],
        compiler_params=pltpu.CompilerParams(vmem_limit_bytes=40 * 2**20),
    )(place, *mine, *theirs)


def split_kernel(layout, total, place, *refs):
    n_in = len(layout)
    grads, outs, sems = refs[:n_in], refs[n_in : n_in + 2], refs[n_in + 2]
    core = place[0]
    for side in range(2):
        half = core if side == 0 else 1 - core
        for k in range(16):
            unit = place[1 + half * 16 + k]
            for n, (first, width, times) in enumerate(layout):
                here = pl.ds(pl.multiple_of(half * width, 128), width)
                for j in range(times):
                    pltpu.make_async_copy(
                        grads[n].at[pl.ds(pl.multiple_of((unit * times + j) * UNIT, 16), UNIT), here],
                        outs[side].at[k, :, pl.ds(first + j * width, width)],
                        sems.at[side],
                    ).start()
    for side in range(2):
        pltpu.make_async_copy(outs[side], outs[side], sems.at[side]).wait()


def split_grads(place, grads, layout):
    total = sum(w * t for _, w, t in layout)
    shape = jax.ShapeDtypeStruct((16, UNIT, total), jnp.bfloat16)
    return pl.pallas_call(
        functools.partial(split_kernel, layout, total),
        out_shape=[shape, shape],
        in_specs=[pl.BlockSpec(memory_space=pltpu.SMEM)] + [pl.BlockSpec(memory_space=pltpu.VMEM)] * len(grads),
        out_specs=[pl.BlockSpec(memory_space=pl.ANY)] * 2,
        scratch_shapes=[pltpu.SemaphoreType.DMA((2,))],
        compiler_params=pltpu.CompilerParams(vmem_limit_bytes=40 * 2**20),
    )(place, *grads)


def add_low(parts):
    total = parts[0].astype(jnp.float32)
    for part in parts[1:]:
        total = total + part.astype(jnp.float32)
    return total.astype(jnp.bfloat16)


def scatter_stage(blocks, stage):
    return add_low([blocks[0]] + [send(blocks[r], stage_pairs(stage, r, True)) for r in (1, 2, 3)])


def scatter_pieces(mine, theirs):
    total = add_low([mine, send(theirs, core_pairs())])
    total = total.reshape(4, 4, UNIT, -1)
    return scatter_stage(scatter_stage(total, 1), 0)


LAYOUT_ONE = ((0, 1152, 1), (1152, 128, 1), (1280, 384, 1))
LAYOUT_TWO = ((0, 1536, 1), (1536, 384, 4))


def halves(value):
    width = value.shape[1] // 2
    return value[:, :width], value[:, width:]


def per_device(
    tokens,
    cotangent,
    span_counts,
    single_flags,
    partner_slots,
    w_qkv,
    b_query,
    b_value,
    w_out,
    b_out,
    gain_attn,
    shift_attn,
    w_in,
    b_in,
    w_down,
    b_down,
    gain_ffn,
    shift_ffn,
):
    spans = tokens.shape[1]
    span_len = tokens.shape[2]
    width = tokens.shape[3]
    f32 = jnp.float32
    bf16 = jnp.bfloat16
    scale = HEAD_DIM ** (-0.5)
    core, units = my_units()
    place = jnp.concatenate([core[None], units.reshape(-1)]).astype(jnp.int32)
    vectors = jnp.concatenate(
        [
            jnp.stack([b_query, b_value, b_out, gain_attn, shift_attn, b_down, gain_ffn, shift_ffn], axis=1),
            b_in.reshape(6, 4),
            jnp.zeros((6, 116), bf16),
        ],
        axis=1,
    )
    packed = []
    for h in range(2):
        packed.append(
            jnp.concatenate(
                [
                    halves(w_qkv)[h],
                    vectors,
                    halves(w_out)[h],
                    halves(w_in)[h],
                    halves(w_down)[h].reshape(6, 1536),
                ],
                axis=1,
            )
        )
    rows48 = exchange_octet(jnp.stack(packed * 4))
    one = rows48[:, :, :FIRST].reshape(UNIT, FIRST)
    two_in = rows48[:, :, FIRST : FIRST + 1536].reshape(UNIT, 1536)
    two_down = rows48[:, :, FIRST + 1536 :].reshape(4, UNIT, 384).transpose(1, 0, 2).reshape(UNIT, 1536)
    two = jnp.concatenate([two_in, two_down], axis=1)
    fw_qkv, fvectors, fw_out = place_weights(place, *gather_pieces(one), LAYOUT_ONE)
    fw_in, fw_down = place_weights(place, *gather_pieces(two), LAYOUT_TWO)
    fvectors = fvectors[:, :12]
    fb_query, fb_value, fb_out, fgain_attn, fshift_attn, fb_down, fgain_ffn, fshift_ffn = [
        fvectors[:, i] for i in range(8)
    ]
    fb_in = fvectors[:, 8:12].reshape(-1)
    slot = jnp.arange(spans, dtype=jnp.int32)
    live = (slot < span_counts[0, 0]).astype(f32)
    keep = live * (1.0 - single_flags[0].astype(f32))
    partner = partner_slots[0]
    rows = tokens.reshape(-1, width)
    bias = jnp.concatenate([fb_query.astype(f32), jnp.zeros((width,), f32), fb_value.astype(f32)])
    qkv = (jnp.dot(rows, fw_qkv, preferred_element_type=f32) + bias).astype(bf16)
    qkv_heads = qkv.reshape(spans, span_len, 3, HEADS, HEAD_DIM)
    query, keyed, valued = (qkv_heads[:, :, 0], qkv_heads[:, :, 1], qkv_heads[:, :, 2])
    scores = jnp.einsum("sqhd,skhd->shqk", query, keyed, preferred_element_type=f32) * scale
    totals = jax.nn.logsumexp(scores, axis=-1)
    probs_low = jnp.exp(scores - totals[..., None]).astype(bf16)
    heads_out = jnp.einsum("shqk,skhd->sqhd", probs_low, valued, preferred_element_type=f32)
    heads_out = heads_out.reshape(-1, width).astype(bf16)
    attn = jnp.dot(heads_out, fw_out, preferred_element_type=f32) + fb_out.astype(f32)
    hidden_one, norm_one_pull = jax.vjp(
        layer_norm, rows.astype(f32) + attn, fgain_attn.astype(f32), fshift_attn.astype(f32)
    )
    hidden_low = hidden_one.astype(bf16)
    upper = jnp.dot(hidden_low, fw_in, preferred_element_type=f32) + fb_in.astype(f32)
    active_f, gelu_pull = jax.vjp(gelu_exact, upper)
    active = active_f.astype(bf16)
    down = jnp.dot(active, fw_down, preferred_element_type=f32) + fb_down.astype(f32)
    final, norm_two_pull = jax.vjp(
        layer_norm, hidden_one + down, fgain_ffn.astype(f32), fshift_ffn.astype(f32)
    )
    final_grid = final.reshape(spans, span_len, width)
    mixed = (final_grid * live[:, None, None]).astype(bf16)
    first = final_grid[:, 0, :]
    sent = (first.astype(bf16).astype(f32) * keep[:, None]).astype(bf16)
    received = from_partner(sent, "pair", 0)
    loss_value, loss_pull = jax.vjp(
        lambda mine, theirs: contrast(mine, theirs, keep, partner), first, received.astype(f32)
    )
    dfirst, dreceived = loss_pull(jnp.ones((), f32))
    returned = from_partner(dreceived.astype(bf16), "pair", 0)
    dsent = returned.astype(f32) * keep[:, None]
    bw_qkv, bw_out, bw_in, bw_down = fw_qkv, fw_out, fw_in, fw_down
    dfinal = cotangent.reshape(spans, span_len, width).astype(f32) * live[:, None, None]
    dfinal = dfinal.at[:, 0, :].add(dfirst + dsent)
    dres2, dgain_ffn, dshift_ffn = norm_two_pull(dfinal.reshape(-1, width))
    ddown = dres2.astype(bf16)
    db_down = jnp.sum(ddown.astype(f32), axis=0)
    dw_down = outer_sum(active, ddown)
    dactive = jnp.dot(ddown, bw_down.T, preferred_element_type=f32)
    (dupper_f,) = gelu_pull(dactive)
    dupper = dupper_f.astype(bf16)
    db_in = jnp.sum(dupper.astype(f32), axis=0)
    dw_in = outer_sum(hidden_low, dupper)
    dhidden = dres2 + jnp.dot(dupper, bw_in.T, preferred_element_type=f32)
    dres1, dgain_attn, dshift_attn = norm_one_pull(dhidden)
    dattn = dres1.astype(bf16)
    db_out = jnp.sum(dattn.astype(f32), axis=0)
    dw_out = outer_sum(heads_out, dattn)
    dheads = jnp.dot(dattn, bw_out.T, preferred_element_type=f32).astype(bf16)
    dheads = dheads.reshape(spans, span_len, HEADS, HEAD_DIM)
    again_scores = jnp.einsum("sqhd,skhd->shqk", query, keyed, preferred_element_type=f32) * scale
    probs = jnp.exp(again_scores - totals[..., None])
    dprobs = jnp.einsum("sqhd,skhd->shqk", dheads, valued, preferred_element_type=f32)
    dvalue = jnp.einsum("shqk,sqhd->skhd", probs.astype(bf16), dheads, preferred_element_type=f32)
    inner = jnp.sum(probs * dprobs, axis=-1, keepdims=True)
    dscores = (probs * (dprobs - inner)).astype(bf16)
    dquery = jnp.einsum("shqk,skhd->sqhd", dscores, keyed, preferred_element_type=f32) * scale
    dkey = jnp.einsum("shqk,sqhd->skhd", dscores, query, preferred_element_type=f32) * scale
    dqkv = jnp.stack([dquery, dkey, dvalue], axis=2).reshape(-1, 3 * width).astype(bf16)
    dqkv_f = dqkv.astype(f32)
    db_query = jnp.sum(dqkv_f[:, :width], axis=0)
    db_value = jnp.sum(dqkv_f[:, 2 * width :], axis=0)
    dw_qkv = outer_sum(rows, dqkv)
    grad_rows = dres1 + jnp.dot(dqkv, bw_qkv.T, preferred_element_type=f32)
    grad_tokens = grad_rows.reshape(tokens.shape).astype(bf16)
    dvectors = jnp.stack(
        [db_query, db_value, db_out, dgain_attn, dshift_attn, db_down, dgain_ffn, dshift_ffn], axis=1
    )
    dvectors = jnp.concatenate(
        [dvectors, db_in.reshape(768, 4), jnp.zeros((768, 244), f32)], axis=1
    ).astype(bf16)
    two = scatter_pieces(*split_grads(place, [dw_in.astype(bf16), dw_down.astype(bf16)], LAYOUT_TWO))
    one = scatter_pieces(
        *split_grads(place, [dw_qkv.astype(bf16), dvectors, dw_out.astype(bf16)], LAYOUT_ONE)
    )
    two_down = two[:, 1536:].reshape(UNIT, 4, 384).transpose(1, 0, 2).reshape(8, 6, 1536)
    back = jnp.concatenate([one.reshape(8, 6, FIRST), two[:, :1536].reshape(8, 6, 1536), two_down], axis=2)
    back = exchange_octet(back).reshape(4, 2, 6, -1)
    sums = jnp.sum(back.astype(f32), axis=0)

    def joined(first, width):
        return jnp.concatenate([sums[0, :, first : first + width], sums[1, :, first : first + width]], axis=1)

    own = sums[0, :, 1152:1164]
    own_down = jnp.concatenate([sums[h, :, FIRST + 1536 :].reshape(24, 384) for h in range(2)], axis=1)
    return (
        mixed.reshape(tokens.shape),
        grad_tokens,
        joined(0, 1152),
        own[:, 0],
        own[:, 1],
        joined(1280, 384),
        own[:, 2],
        own[:, 3],
        own[:, 4],
        joined(FIRST, 1536),
        own[:, 8:12].reshape(24),
        own_down,
        own[:, 5],
        own[:, 6],
        own[:, 7],
    )


def solution(mesh):
    return jax.shard_map(
        per_device,
        mesh=mesh,
        in_specs=(
            P("pair", "dp", None, None),
            P("pair", "dp", None, None),
            P("pair", "dp"),
            P("pair", "dp"),
            P("pair", "dp"),
            P(("pair", "dp"), None),
            P(("pair", "dp")),
            P(("pair", "dp")),
            P(("pair", "dp"), None),
            P(("pair", "dp")),
            P(("pair", "dp")),
            P(("pair", "dp")),
            P(("pair", "dp"), None),
            P(("pair", "dp")),
            P(("pair", "dp"), None),
            P(("pair", "dp")),
            P(("pair", "dp")),
            P(("pair", "dp")),
        ),
        out_specs=(
            P("pair", "dp", None, None),
            P("pair", "dp", None, None),
            P(("pair", "dp"), None),
            P(("pair", "dp")),
            P(("pair", "dp")),
            P(("pair", "dp"), None),
            P(("pair", "dp")),
            P(("pair", "dp")),
            P(("pair", "dp")),
            P(("pair", "dp"), None),
            P(("pair", "dp")),
            P(("pair", "dp"), None),
            P(("pair", "dp")),
            P(("pair", "dp")),
            P(("pair", "dp")),
        ),
        check_vma=False,
    )
```

```python
import functools

import jax
import jax.numpy as jnp
import ml_dtypes
import numpy as np
from jax import lax
from jax.experimental import pallas as pl
from jax.experimental.pallas import tpu as pltpu
from jax.sharding import PartitionSpec as P

HEADS = 12
HEAD_DIM = 64


epsilon = 1e-12
contrast_weight = 8.0
logit_scale = 0.0625


AXES = ("pair", "dp")
UNIT = 48


def device_index(p, a, yh, yl, z, c):
    return ((((p * 4 + a) * 2 + yh) * 2 + yl) * 2 + z) * 2 + c


def all_places():
    return [
        (p, a, yh, yl, z, c)
        for p in range(2)
        for a in range(4)
        for yh in range(2)
        for yl in range(2)
        for z in range(2)
        for c in range(2)
    ]


def moved(place, stage, r):
    p, a, yh, yl, z, c = place
    if (stage == 0) == (c == 0):
        return (p ^ (r & 1), a, yh ^ (r >> 1), yl, z, c)
    return (p, (a + r) % 4, yh, yl, z, c)


def stage_pairs(stage, r, back=False):
    pairs = [(device_index(*moved(q, stage, r)), device_index(*q)) for q in all_places()]
    return [(t, s) for s, t in pairs] if back else pairs


def core_pairs():
    return [(d, d ^ 1) for d in range(128)]


def octets():
    return [[8 * g + k for k in range(8)] for g in range(16)]


def send(value, pairs):
    return lax.ppermute(value, AXES, pairs)


def exchange_octet(value):
    return lax.all_to_all(value, AXES, 0, 0, axis_index_groups=octets(), tiled=True)


def my_place():
    me = lax.axis_index("pair") * 64 + lax.axis_index("dp")
    c, yh, a, p = me & 1, (me >> 3) & 1, (me >> 4) & 3, me >> 6
    i = jnp.arange(16, dtype=jnp.int32)
    late, early = i >> 2, i & 3
    zero = (p ^ (early & 1)) * 8 + ((a + late) & 3) * 2 + (yh ^ (early >> 1))
    one = (p ^ (late & 1)) * 8 + ((a + early) & 3) * 2 + (yh ^ (late >> 1))
    across = (p ^ (i >> 3)) + 2 * (yh ^ (i & 1))
    along = ((i >> 1) - a) & 3
    parts = [c[None], zero, one, 4 * along + across, 4 * across + along]
    return jnp.concatenate(parts).astype(jnp.int32)


WIDE = (1152, 128, 384)
FIRST = sum(WIDE)
SECOND = 3072


def gather_early(block):
    return [block] + [send(block, stage_pairs(0, r)) for r in (1, 2, 3)]


def gather_late(early):
    return [early] + [send(early, stage_pairs(1, r)) for r in (1, 2, 3)]


def to_core(value):
    return send(value, core_pairs())


def scatter_sends(blocks, stage):
    return [blocks[0]] + [send(blocks[r], stage_pairs(stage, r, True)) for r in (1, 2, 3)]


def add_low(parts):
    total = parts[0].astype(jnp.float32)
    for part in parts[1:]:
        total = total + part.astype(jnp.float32)
    return total.astype(jnp.bfloat16)


F32 = jnp.float32
BF16 = jnp.bfloat16
NN = (((1,), (0,)), ((), ()))
NT = (((1,), (1,)), ((), ()))
TN = (((0,), (0,)), ((), ()))
ROWS = 1024
BLOCK = 256
STEPS = ROWS // BLOCK
TALL = 512
WIDTH = 768
INNER = 3072
MIB = 2**20
WEIGHTS = {
    "attention_kernel": 5e+08,
    "first_rows_kernel": 1.25e+08,
    "contrast_kernel": 6.25e+06,
    "feed_forward_kernel": 3.125e+08,
    "feed_forward_back_kernel": 3.125e+08,
    "hidden_back_kernel": 3.75e+08,
    "attention_back_kernel": 3.125e+08,
    "tokens_back_kernel": 2.5e+08,
    "layer_grads_kernel": 6.25e+08,
    "attention_grads_kernel": 3.125e+08,
    "add_kernel": 1.25e+08,
    "collect_kernel": 1.25e+08,
    "stack_kernel": 3.125e+07,
    "pack_kernel": 3.125e+07,
    "finish_kernel": 3.125e+07,
    "sum_kernel": 3.125e+07,
}


def dot(left, right, dims=NN):
    return lax.dot_general(left, right, dims, preferred_element_type=F32)


def full_spec():
    return pl.BlockSpec(memory_space=pltpu.VMEM)


def any_spec():
    return pl.BlockSpec(memory_space=pl.ANY)


def smem_spec():
    return pl.BlockSpec(memory_space=pltpu.SMEM)


def row_spec(width, block=BLOCK):
    return pl.BlockSpec((block, width), lambda i: (i, 0))


def tall_spec(width):
    return row_spec(width, TALL)


def one_spec(rows, width):
    return pl.BlockSpec((rows, width), lambda i: (0, 0))


def shape(dims, dtype=BF16):
    return pltpu.HBM(dims, dtype)


def near(dims, dtype=BF16):
    return pltpu.VMEM(dims, dtype)


def loose(dims, dtype=BF16):
    return jax.ShapeDtypeStruct(dims, dtype)


class Near:
    def __init__(self, value):
        self.value = value


class Loose(Near):
    pass


def pinned(value):
    if isinstance(value, Loose):
        return value.value
    if isinstance(value, Near):
        return pltpu.with_memory_space_constraint(value.value, pltpu.VMEM)
    return pltpu.with_memory_space_constraint(value, pltpu.HBM)


def block_rows(step, block=TALL):
    return pl.ds(pl.multiple_of(step * block, block), block)


def limit(mib):
    return pltpu.CompilerParams(vmem_limit_bytes=mib * MIB)


def call(kernel, args, in_specs, out_shape, out_specs, mib, weight=0, grid=None, scratch=(), deps=(), **more):
    n_args, n_deps = len(args), len(deps)

    def body(*refs):
        kernel(*refs[:n_args], *refs[n_args + n_deps :])

    kwargs = dict(more)
    args = [a if spec.memory_space == pltpu.SMEM else pinned(a) for a, spec in zip(args, in_specs)]
    deps = [pinned(a) for a in deps]
    if grid is not None:
        kwargs["grid"] = grid
    return pl.pallas_call(
        body,
        out_shape=out_shape,
        in_specs=list(in_specs) + [any_spec()] * n_deps,
        out_specs=out_specs,
        scratch_shapes=list(scratch),
        cost_estimate=pl.CostEstimate(flops=int(weight or WEIGHTS.get(getattr(kernel, "func", kernel).__name__, 0)), bytes_accessed=0, transcendentals=0),
        name=getattr(kernel, "func", kernel).__name__,
        compiler_params=limit(mib),
        **kwargs,
    )(*args, *deps)


def normalize(resid):
    centered = resid - jnp.mean(resid, axis=-1, keepdims=True)
    variance = jnp.mean(centered * centered, axis=-1, keepdims=True)
    scale = lax.rsqrt(variance + epsilon)
    return centered * scale, scale


def normalize_back(grad, norm, scale):
    mean_grad = jnp.mean(grad, axis=-1, keepdims=True)
    mean_both = jnp.mean(grad * norm, axis=-1, keepdims=True)
    return scale * (grad - mean_grad - norm * mean_both)


def column_sum(value):
    return jnp.sum(value.reshape(-1, 8, value.shape[1]), axis=0)


def add_rows(ref, step, *rows):
    total = jnp.concatenate(list(rows), axis=0)

    @pl.when(step == 0)
    def _():
        ref[...] = total

    @pl.when(step > 0)
    def _():
        ref[...] += total


def unit_rows(place, half, k, times, j):
    return pl.ds(pl.multiple_of((place[1 + half * 16 + k] * times + j) * UNIT, 16), UNIT)


def piece_copies(place, pieces, targets, sems):
    core = place[0]
    for side in range(2):
        half = core if side == 0 else 1 - core
        for k in range(16):
            block = pieces[4 * side + k // 4].at[k % 4]
            for n, (ref, first, width, times, both) in enumerate(targets):
                if side == 1 and not both:
                    continue
                to = pl.ds(pl.multiple_of(half * width, 128), width) if both else pl.ds(0, width)
                for j in range(times):
                    pltpu.make_async_copy(
                        block.at[:, pl.ds(first + j * width, width)],
                        ref.at[unit_rows(place, half, k, times, j), to],
                        sems.at[n],
                    ).start()


def wait_whole(ref, sem):
    pltpu.make_async_copy(ref, ref, sem).wait()


def pair_masks():
    lane = lax.broadcasted_iota(jnp.int32, (128, 128), 1)
    return lane < HEAD_DIM


def both_heads(block, low):
    zero = jnp.zeros_like(block)
    return jnp.concatenate([jnp.where(low, block, zero), jnp.where(low, zero, block)], axis=0)


def upright(block):
    return jnp.concatenate([block[:, :128], block[:, 128:]], axis=0)


def attention_kernel(place, x_ref, *refs):
    pieces = refs[:8]
    qkv_ref, probs_ref, heads_ref, norm_ref, scale_ref, vec_ref, wqkv_hbm, wout_hbm = refs[8:16]
    wqkv, wout, wvec, sems, out_sems = refs[16:]
    step = pl.program_id(0)

    @pl.when(step == 0)
    def _():
        piece_copies(
            place,
            pieces,
            ((wqkv, 0, 1152, 1, True), (wvec, 1152, 128, 1, False), (wout, 1280, 384, 1, True)),
            sems,
        )
        wait_whole(wqkv, sems.at[0])
        wait_whole(wvec, sems.at[1])
        pltpu.make_async_copy(wqkv, wqkv_hbm, out_sems.at[0]).start()
        vec_ref[...] = wvec[...].astype(F32).T[:16]

    x = x_ref[...]
    for n in range(3):
        part = dot(x, wqkv[:, n * WIDTH : (n + 1) * WIDTH])
        if n != 1:
            part = part + vec_ref[n // 2 : n // 2 + 1, :]
        qkv_ref[:, n * WIDTH : (n + 1) * WIDTH] = part.astype(BF16)
    low = pair_masks()
    for s in range(BLOCK // 128):
        rows = slice(128 * s, 128 * s + 128)
        for h in range(HEADS // 2):
            cols = slice(128 * h, 128 * h + 128)
            query = both_heads(qkv_ref[rows, 128 * h : 128 * h + 128] * BF16(0.125), low)
            keyed = qkv_ref[rows, WIDTH + 128 * h : WIDTH + 128 * h + 128]
            valued = qkv_ref[rows, 2 * WIDTH + 128 * h : 2 * WIDTH + 128 * h + 128]
            scores = dot(keyed, query, NT)
            weight = jnp.exp(scores - jnp.max(scores, axis=0, keepdims=True))
            probs = (weight * (1.0 / jnp.sum(weight, axis=0, keepdims=True))).astype(BF16)
            probs_ref[s, h] = probs
            heads_ref[rows, cols] = dot(upright(probs), both_heads(valued, low), TN).astype(BF16)

    @pl.when(step == 0)
    def _():
        wait_whole(wout, sems.at[2])
        pltpu.make_async_copy(wout, wout_hbm, out_sems.at[1]).start()

    attn = dot(heads_ref[...], wout[...]) + vec_ref[2:3, :]
    norm, scale = normalize(x.astype(F32) + attn)
    norm_ref[...] = norm
    scale_ref[...] = jnp.broadcast_to(scale, scale_ref.shape)

    @pl.when(step == STEPS - 1)
    def _():
        wait_whole(wqkv, out_sems.at[0])
        wait_whole(wout, out_sems.at[1])


def attention_forward(place, rows, pieces):
    return call(
        attention_kernel,
        [place, rows, *pieces],
        [smem_spec(), row_spec(WIDTH)] + [any_spec()] * 8,
        [
            shape((ROWS, 3 * WIDTH)),
            shape((ROWS // 128, HEADS // 2, 128, 256)),
            shape((ROWS, WIDTH)),
            shape((ROWS, WIDTH), F32),
            shape((ROWS, 128), F32),
            shape((16, WIDTH), F32),
            shape((WIDTH, 3 * WIDTH)),
            shape((WIDTH, WIDTH)),
        ],
        [
            row_spec(3 * WIDTH),
            pl.BlockSpec((BLOCK // 128, HEADS // 2, 128, 256), lambda i: (i, 0, 0, 0)),
            row_spec(WIDTH),
            row_spec(WIDTH),
            row_spec(128),
            one_spec(16, WIDTH),
            any_spec(),
            any_spec(),
        ],
        20,
        grid=(STEPS,),
        scratch=[
            pltpu.VMEM((WIDTH, 3 * WIDTH), BF16),
            pltpu.VMEM((WIDTH, WIDTH), BF16),
            pltpu.VMEM((WIDTH, 128), BF16),
            pltpu.SemaphoreType.DMA((3,)),
            pltpu.SemaphoreType.DMA((2,)),
        ],
    )


def wide_scale(ref):
    return jnp.concatenate([ref[...]] * 6, axis=1)


def hidden_of(norm, vec_ref):
    return norm * vec_ref[3:4, :] + vec_ref[4:5, :]


def gelu_parts(upper):
    phi = 0.5 * (1.0 + lax.erf(upper * 0.7071067811865476))
    bell = jnp.exp(-0.5 * upper * upper) * 0.3989422804014327
    return upper * phi, phi + upper * bell


def first_rows_kernel(place, norm_hbm, vec_ref, b_in_ref, keep_ref, *refs):
    halves = refs[:4]
    first_ref, sent_ref, win, wdown = refs[4:8]
    rows, sems, rows_sem = refs[8:]
    for n in range(4):
        half = place[0] if n % 2 == 0 else 1 - place[0]
        target, width = (win, 1536) if n < 2 else (wdown, 384)
        pltpu.make_async_copy(halves[n], target.at[:, lanes(half, width)], sems.at[n // 2]).start()
    for s in range(8):
        pltpu.make_async_copy(norm_hbm.at[pl.ds(128 * s, 8)], rows.at[pl.ds(8 * s, 8)], rows_sem).start()
    wait_whole(rows, rows_sem)
    norm = jnp.concatenate([rows[8 * s : 8 * s + 1, :] for s in range(8)], axis=0)
    hidden = hidden_of(norm, vec_ref)
    wide = jnp.concatenate([hidden, jnp.zeros_like(hidden)], axis=0).astype(BF16)
    wait_whole(win, sems.at[0])
    wait_whole(wdown, sems.at[1])
    down = jnp.zeros((16, WIDTH), F32)
    for n in range(4):
        cols = slice(n * WIDTH, (n + 1) * WIDTH)
        upper = dot(wide, win[:, cols]) + b_in_ref[:, cols]
        down = down + dot(gelu_parts(upper)[0].astype(BF16), wdown[cols, :])
    final = normalize(hidden + down[:8] + vec_ref[5:6, :])[0] * vec_ref[6:7, :] + vec_ref[7:8, :]
    first_ref[...] = final
    sent_ref[...] = (final.astype(BF16).astype(F32) * keep_ref[...]).astype(BF16)


def first_rows(place, norm, vec, b_in, keep, halves):
    return call(
        first_rows_kernel,
        [place, norm, vec, b_in, keep, *halves],
        [smem_spec(), any_spec(), full_spec(), full_spec(), full_spec()] + [any_spec()] * 4,
        [shape((8, WIDTH), F32), loose((8, WIDTH)), near((WIDTH, INNER)), near((INNER, WIDTH))],
        [full_spec()] * 4,
        8,
        scratch=[
            pltpu.VMEM((64, WIDTH), F32),
            pltpu.SemaphoreType.DMA((2,)),
            pltpu.SemaphoreType.DMA,
        ],
    )


def contrast_kernel(first_ref, received_ref, keep_ref, partner_ref, dfirst_ref, dreceived_ref):
    first = first_ref[...]
    received = received_ref[...].astype(F32)
    logits = lax.dot_general(first, received, NT, precision=lax.Precision.HIGHEST, preferred_element_type=F32)
    logits = logits * logit_scale
    weight = jnp.exp(logits - jnp.max(logits, axis=-1, keepdims=True))
    soft = weight / jnp.sum(weight, axis=-1, keepdims=True)
    column = lax.broadcasted_iota(jnp.int32, (8, 8), 1)
    chosen = jnp.where(column == partner_ref[...], 1.0, 0.0)
    dlogits = (contrast_weight * logit_scale) * keep_ref[...] * (soft - chosen)
    high = lax.Precision.HIGHEST
    dfirst_ref[...] = lax.dot_general(dlogits, received, NN, precision=high, preferred_element_type=F32)
    dreceived_ref[...] = lax.dot_general(
        dlogits, first, TN, precision=high, preferred_element_type=F32
    ).astype(BF16)


def contrast_back(first, received, keep, partner, deps):
    return call(
        contrast_kernel,
        [Loose(first), Loose(received), Loose(keep), Loose(partner)],
        [full_spec()] * 4,
        [loose((8, WIDTH), F32), loose((8, WIDTH))],
        [full_spec()] * 2,
        4,
        deps=deps,
    )


CHUNK = 512
CHUNKS = INNER // CHUNK


def chunk(n):
    return slice(n * CHUNK, (n + 1) * CHUNK)


def feed_forward_kernel(step, count, norm_ref, vec_ref, b_in_ref, win, wdown, *refs):
    hidden_ref, active_ref, slope_ref, norm_two_ref, scale_ref, mixed_ref = refs[-6:]
    hidden = hidden_of(norm_ref[...], vec_ref)
    hidden_low = hidden.astype(BF16)
    here = block_rows(step)
    hidden_ref[here, :] = hidden_low
    down, active = hidden + vec_ref[5:6, :], None
    after = dot(hidden_low, win[:, chunk(0)])
    for n in range(CHUNKS):
        upper = after + b_in_ref[:, chunk(n)]
        if n + 1 < CHUNKS:
            after = dot(hidden_low, win[:, chunk(n + 1)])
        if n > 0:
            down = down + dot(active, wdown[chunk(n - 1), :])
        active, slope = gelu_parts(upper)
        active = active.astype(BF16)
        active_ref[here, chunk(n)] = active
        slope_ref[here, chunk(n)] = slope.astype(BF16)
    down = down + dot(active, wdown[chunk(CHUNKS - 1), :])
    norm, scale = normalize(down)
    norm_two_ref[...] = norm.astype(BF16)
    scale_ref[...] = jnp.broadcast_to(scale, scale_ref.shape)
    final = norm * vec_ref[6:7, :] + vec_ref[7:8, :]
    for s in range(TALL // 128):
        rows = slice(128 * s, 128 * s + 128)
        live = jnp.where(step * (TALL // 128) + s < count[0], 1.0, 0.0)
        mixed_ref[rows, :] = (final[rows] * live).astype(BF16)


def feed_forward(step, count, norm, vec, b_in, win, wdown, so_far=(), deps=()):
    in_half = pl.BlockSpec((TALL, WIDTH), lambda i: (step, 0))
    wide_half = pl.BlockSpec((TALL, 128), lambda i: (step, 0))
    aliases = {6 + n: n for n in range(len(so_far))}
    return call(
        functools.partial(feed_forward_kernel, step),
        [count, norm, vec, b_in, Near(win), Near(wdown)] + [Near(v) if n < 3 else v for n, v in enumerate(so_far)],
        [smem_spec(), in_half] + [full_spec()] * 4 + ([full_spec()] * 3 + [any_spec()] * 3)[: len(so_far)],
        [
            near((ROWS, WIDTH)),
            near((ROWS, INNER)),
            near((ROWS, INNER)),
            shape((ROWS, WIDTH)),
            shape((ROWS, 128), F32),
            shape((ROWS, WIDTH)),
        ],
        [full_spec()] * 3 + [in_half, wide_half, in_half],
        20,
        grid=(1,),
        input_output_aliases=aliases,
        deps=deps,
    )


def feed_forward_back_kernel(
    count, cot_ref, dfirst_ref, back_ref, keep_ref, norm_ref, scale_ref, vec_ref, slope_ref, wdown, dres_ref, ddown_ref, dupper_ref, sums_ref, db_in_ref
):
    step = pl.program_id(0)
    dfirst = dfirst_ref[...] + back_ref[...].astype(F32) * keep_ref[...]
    slot = lax.broadcasted_iota(jnp.int32, (8, 1), 0)
    parts = []
    for s in range(TALL // 128):
        span = step * (TALL // 128) + s
        live = jnp.where(span < count[0], 1.0, 0.0)
        mine = jnp.sum(jnp.where(slot == span, dfirst, 0.0), axis=0, keepdims=True)
        cot = cot_ref[128 * s : 128 * s + 128, :].astype(F32) * live
        top = cot[:8] + jnp.where(slot == 0, mine, 0.0)
        parts += [top, cot[8:]]
    dfinal = jnp.concatenate(parts, axis=0)
    norm = norm_ref[...].astype(F32)
    dres = normalize_back(dfinal * vec_ref[6:7, :], norm, wide_scale(scale_ref))
    dres_ref[...] = dres
    ddown = dres.astype(BF16)
    here = block_rows(step)
    ddown_ref[here, :] = ddown
    after, parts = dot(ddown, wdown[chunk(0), :], NT), []
    for n in range(CHUNKS):
        dactive = after
        if n + 1 < CHUNKS:
            after = dot(ddown, wdown[chunk(n + 1), :], NT)
        dupper = dactive * slope_ref[here, chunk(n)].astype(F32)
        dupper_ref[here, chunk(n)] = dupper.astype(BF16)
        parts.append(column_sum(dupper))
    add_rows(sums_ref, step, column_sum(dfinal * norm), column_sum(dfinal), column_sum(dres))
    add_rows(db_in_ref, step, jnp.concatenate(parts, axis=1))


def feed_forward_back(count, cotangent, dfirst, back, keep, norm, scale, vec, slope, wdown):
    return call(
        feed_forward_back_kernel,
        [count, cotangent, Loose(dfirst), Loose(back), Loose(keep), norm, scale, vec, Near(slope), Near(wdown)],
        [smem_spec(), tall_spec(WIDTH), full_spec(), full_spec(), full_spec(), tall_spec(WIDTH), tall_spec(128)]
        + [full_spec()] * 3,
        [
            shape((ROWS, WIDTH), F32),
            near((ROWS, WIDTH)),
            near((ROWS, INNER)),
            shape((24, WIDTH), F32),
            shape((8, INNER), F32),
        ],
        [tall_spec(WIDTH), full_spec(), full_spec(), one_spec(24, WIDTH), one_spec(8, INNER)],
        20,
        grid=(ROWS // TALL,),
        input_output_aliases={8: 2},
    )


def hidden_back_kernel(dres_ref, dupper_ref, norm_ref, scale_ref, vec_ref, win, wout, dres_one_ref, dattn_ref, dheads_ref, sums_ref):
    step = pl.program_id(0)
    count = TALL // BLOCK

    def product(n):
        here = pl.ds(pl.multiple_of(step * TALL + n * BLOCK, BLOCK), BLOCK)
        return dot(dupper_ref[here, :], win[...], NT)

    after, sums = product(0), []
    for n in range(count):
        rows = slice(n * BLOCK, (n + 1) * BLOCK)
        dhidden = dres_ref[rows, :] + after
        if n + 1 < count:
            after = product(n + 1)
        norm = norm_ref[rows, :]
        scale = jnp.concatenate([scale_ref[rows, :]] * 6, axis=1)
        dres = normalize_back(dhidden * vec_ref[3:4, :], norm, scale)
        dres_one_ref[rows, :] = dres
        dattn = dres.astype(BF16)
        dattn_ref[rows, :] = dattn
        dheads_ref[rows, :] = dot(dattn, wout[...], NT).astype(BF16)
        sums.append([column_sum(dhidden * norm), column_sum(dhidden), column_sum(dres)])
    add_rows(sums_ref, step, *[sum(group) for group in zip(*sums)])


def hidden_back(dres, dupper, norm, scale, vec, win, wout, deps):
    return call(
        hidden_back_kernel,
        [dres, Near(dupper), norm, scale, vec, Near(win), wout],
        [tall_spec(WIDTH), full_spec(), tall_spec(WIDTH), tall_spec(128)] + [full_spec()] * 3,
        [shape((ROWS, WIDTH), F32), shape((ROWS, WIDTH)), shape((ROWS, WIDTH)), shape((24, WIDTH), F32)],
        [tall_spec(WIDTH), tall_spec(WIDTH), tall_spec(WIDTH), one_spec(24, WIDTH)],
        22,
        grid=(ROWS // TALL,),
        deps=deps,
    )


def attention_back_kernel(qkv_ref, probs_ref, dheads_ref, dqkv_ref, sums_ref):
    step = pl.program_id(0)
    low = pair_masks()
    for s in range(BLOCK // 128):
        rows = slice(128 * s, 128 * s + 128)
        for h in range(HEADS // 2):
            query = both_heads(qkv_ref[rows, 128 * h : 128 * h + 128] * BF16(0.125), low)
            keyed = qkv_ref[rows, WIDTH + 128 * h : WIDTH + 128 * h + 128]
            valued = qkv_ref[rows, 2 * WIDTH + 128 * h : 2 * WIDTH + 128 * h + 128]
            dheads = both_heads(dheads_ref[rows, 128 * h : 128 * h + 128], low)
            probs_low = probs_ref[s, h]
            probs = probs_low.astype(F32)
            dprobs = dot(valued, dheads, NT)
            inner = jnp.sum(probs * dprobs, axis=0, keepdims=True)
            dscores = (probs * (dprobs - inner)).astype(BF16)
            dquery = dot(upright(dscores), both_heads(keyed * BF16(0.125), low), TN)
            dqkv_ref[rows, 128 * h : 128 * h + 128] = dquery.astype(BF16)
            dqkv_ref[rows, WIDTH + 128 * h : WIDTH + 128 * h + 128] = dot(dscores, query).astype(BF16)
            dqkv_ref[rows, 2 * WIDTH + 128 * h : 2 * WIDTH + 128 * h + 128] = dot(probs_low, dheads).astype(BF16)
    add_rows(
        sums_ref,
        step,
        column_sum(dqkv_ref[:, :WIDTH].astype(F32)),
        column_sum(dqkv_ref[:, 2 * WIDTH :].astype(F32)),
    )


def attention_back(qkv, probs, dheads, deps):
    return call(
        attention_back_kernel,
        [qkv, probs, dheads],
        [
            row_spec(3 * WIDTH),
            pl.BlockSpec((BLOCK // 128, HEADS // 2, 128, 256), lambda i: (i, 0, 0, 0)),
            row_spec(WIDTH),
        ],
        [shape((ROWS, 3 * WIDTH)), shape((16, WIDTH), F32)],
        [row_spec(3 * WIDTH), one_spec(16, WIDTH)],
        16,
        grid=(STEPS,),
        deps=deps,
    )


def tokens_back_kernel(dres_ref, dqkv_ref, wqkv, out_ref):
    out_ref[...] = (dres_ref[...] + dot(dqkv_ref[...], wqkv[...], NT)).astype(BF16)


def tokens_back(dres, dqkv, wqkv, deps):
    return call(
        tokens_back_kernel,
        [dres, dqkv, wqkv],
        [row_spec(WIDTH), row_spec(3 * WIDTH), full_spec()],
        shape((ROWS, WIDTH)),
        row_spec(WIDTH),
        14,
        grid=(STEPS,),
        deps=deps,
    )


def lanes(half, width, first=0, count=None):
    return pl.ds(pl.multiple_of(half * width + first, 128), width if count is None else count)


def put_units(place, both, half, units, cols, value):
    side = place[0] if half == 0 else 1 - place[0]
    for n, unit in enumerate(units):
        k = place[33 + 16 * half + unit]
        both[side, k, :, cols] = value[UNIT * n : UNIT * n + UNIT].astype(BF16)


def run_ahead(jobs):
    after = jobs[0][0]()
    for n, (_, use) in enumerate(jobs):
        value = after
        if n + 1 < len(jobs):
            after = jobs[n + 1][0]()
        use(value)


def layer_grads_kernel(place, active_ref, ddown_ref, hidden_ref, dupper_ref, own, theirs, both, sems):
    units = list(range(16))

    def in_product(h, n):
        first = 1536 * h + 768 * n
        return lambda: dot(hidden_ref[...], dupper_ref[:, first : first + 768], TN)

    def in_use(h, n):
        return lambda value: put_units(place, both, h, units, slice(768 * n, 768 * n + 768), value)

    run_ahead([(in_product(h, n), in_use(h, n)) for h in range(2) for n in range(2)])
    copies = [
        pltpu.make_async_copy(both.at[n, :, :, :1536], out.at[:, :, :1536], sems.at[n]) for n, out in ((1, theirs), (0, own))
    ]
    for copy in copies:
        copy.start()

    def down_product(n):
        return lambda: dot(active_ref[:, WIDTH * n : WIDTH * n + WIDTH], ddown_ref[...], TN)

    def down_use(n):
        def use(value):
            for h in range(2):
                for i in range(4):
                    for j in range(4):
                        rows = value[192 * i + UNIT * j : 192 * i + UNIT * j + UNIT, 384 * h : 384 * h + 384]
                        cols = slice(1536 + 384 * j, 1536 + 384 * j + 384)
                        put_units(place, both, h, [4 * n + i], cols, rows)

        return use

    run_ahead([(down_product(n), down_use(n)) for n in range(4)])
    for n, out in ((1, theirs), (0, own)):
        copies.append(pltpu.make_async_copy(both.at[n, :, :, 1536:], out.at[:, :, 1536:], sems.at[2 + n]))
        copies[-1].start()
    for copy in copies:
        copy.wait()


def layer_grads(place, active, ddown, hidden_low, dupper):
    return call(
        layer_grads_kernel,
        [place, Near(active), Near(ddown), Near(hidden_low), Near(dupper)],
        [smem_spec()] + [full_spec()] * 4,
        [shape((16, UNIT, 3072)), loose((16, UNIT, 3072))],
        [any_spec(), any_spec()],
        20,
        scratch=[pltpu.VMEM((2, 16, UNIT, 3072), BF16), pltpu.SemaphoreType.DMA((4,))],
    )


def attention_grads_kernel(
    place, x_hbm, dqkv_hbm, heads_hbm, dattn_hbm, sums_ref, own, theirs, both, x, heads, dattn, dqkv, sems
):
    pairs = [(heads_hbm, heads), (dattn_hbm, dattn), (x_hbm, x)]
    pairs += [(dqkv_hbm.at[:, pl.ds(768 * n, 768)], dqkv.at[n]) for n in range(3)]
    loads = [pltpu.make_async_copy(far, here, sems.at[n]) for n, (far, here) in enumerate(pairs)]
    for load in loads:
        load.start()
    units = list(range(16))
    wide = jnp.concatenate([sums_ref[...], jnp.zeros((112, WIDTH), F32)], axis=0).T
    put_units(place, both, 0, units, slice(1152, 1280), wide)
    put_units(place, both, 1, units, slice(1152, 1280), jnp.zeros_like(wide))
    loads[0].wait()
    loads[1].wait()

    def out_product():
        return dot(heads[...], dattn[...], TN)

    def out_use(value):
        for h in range(2):
            put_units(place, both, h, units, slice(1280, FIRST), value[:, 384 * h : 384 * h + 384])

    loads[2].wait()

    def product(n):
        def run():
            loads[3 + n].wait()
            return dot(x[...], dqkv[n], TN)

        return run

    def use(n):
        def keep(value):
            for m in range(2):
                first = 768 * n + 384 * m
                h, at = first // 1152, first % 1152
                put_units(place, both, h, units, slice(at, at + 384), value[:, 384 * m : 384 * m + 384])

        return keep

    run_ahead([(out_product, out_use)] + [(product(n), use(n)) for n in range(3)])
    copies = [pltpu.make_async_copy(both.at[n], out, sems.at[n]) for n, out in ((1, theirs), (0, own))]
    for copy in copies:
        copy.start()
    for copy in copies:
        copy.wait()


def attention_grads(place, rows, dqkv, heads, dattn, sums, deps):
    return call(
        attention_grads_kernel,
        [place, rows, dqkv, heads, dattn, Loose(sums)],
        [smem_spec()] + [any_spec()] * 4 + [full_spec()],
        [shape((16, UNIT, FIRST)), loose((16, UNIT, FIRST))],
        [any_spec(), any_spec()],
        24,
        scratch=[pltpu.VMEM((2, 16, UNIT, FIRST), BF16)]
        + [pltpu.VMEM((ROWS, WIDTH), BF16)] * 3
        + [pltpu.VMEM((3, ROWS, WIDTH), BF16), pltpu.SemaphoreType.DMA((6,))],
        deps=deps,
    )


def add_kernel(own_hbm, recv_hbm, *refs):
    outs, (own, recv, sems) = refs[:4], refs[4:]
    loads = []
    for r in range(4):
        part = pl.ds(4 * r, 4)
        pair = [
            pltpu.make_async_copy(own_hbm.at[part], own.at[part], sems.at[2 * r]),
            pltpu.make_async_copy(recv_hbm.at[part], recv.at[part], sems.at[2 * r + 1]),
        ]
        for load in pair:
            load.start()
        loads.append(pair)
    for r in range(4):
        for load in loads[r]:
            load.wait()
        for k in range(4):
            outs[r][k] = (own[4 * r + k].astype(F32) + recv[4 * r + k].astype(F32)).astype(BF16)


def add_theirs(own, recv, deps):
    width = recv.shape[2]
    buffer = pltpu.VMEM((16, UNIT, width), BF16)
    return call(
        add_kernel,
        [own, Loose(recv)],
        [any_spec()] * 2,
        [loose((4, UNIT, width))] * 4,
        [full_spec()] * 4,
        18,
        scratch=[buffer, buffer, pltpu.SemaphoreType.DMA((8,))],
        deps=deps,
    )


def pack_kernel(wqkv_hbm, wout_hbm, win_hbm, wdown_hbm, vec, mask, pick, out_ref, wqkv, wout, win, wdown, sems):
    loads = [
        pltpu.make_async_copy(far, here, sems.at[n])
        for n, (far, here) in enumerate(((wqkv_hbm, wqkv), (wout_hbm, wout), (win_hbm, win), (wdown_hbm, wdown)))
    ]
    for load in loads:
        load.start()
    column = dot((vec[...] * mask[...]).astype(BF16), pick[...])[:6].astype(BF16)
    for load in loads:
        load.wait()
    for k in range(8):
        h = k % 2
        out_ref[k, :, :1152] = wqkv[:, 1152 * h : 1152 * h + 1152]
        out_ref[k, :, 1152:1280] = column
        out_ref[k, :, 1280:FIRST] = wout[:, 384 * h : 384 * h + 384]
        out_ref[k, :, FIRST : FIRST + 1536] = win[:, 1536 * h : 1536 * h + 1536]
        for j in range(4):
            first = FIRST + 1536 + 384 * j
            out_ref[k, :, first : first + 384] = wdown[6 * j : 6 * j + 6, 384 * h : 384 * h + 384]


def pack(wqkv, wout, win, wdown, vectors, b_in):
    vec = jnp.zeros((128,), F32)
    for n, v in enumerate(list(vectors) + [b_in]):
        vec = vec + lax.pad(v.astype(F32), jnp.zeros((), F32), [(6 * n, 128 - 6 * n - v.shape[0], 0)])
    j = np.arange(128)
    r = np.where(j < 48, j % 6, np.where(j < 72, (j - 48) // 4, -1))
    i = np.where(j < 48, j // 6, np.where(j < 72, 8 + (j - 48) % 4, -1))
    mask = (r[None, :] == np.arange(8)[:, None]).astype(np.float32)
    pick = (i[:, None] == np.arange(128)[None, :]).astype(ml_dtypes.bfloat16)
    return call(
        pack_kernel,
        [wqkv, wout, win, wdown, vec.reshape(1, 128), mask, pick],
        [any_spec()] * 4 + [full_spec()] * 3,
        loose((8, 6, FIRST + 3072)),
        full_spec(),
        6,
        scratch=[
            pltpu.VMEM((6, 2304), BF16),
            pltpu.VMEM((6, 768), BF16),
            pltpu.VMEM((6, 3072), BF16),
            pltpu.VMEM((24, 768), BF16),
            pltpu.SemaphoreType.DMA((4,)),
        ],
    )


def stack_kernel(cuts, *refs):
    parts, outs = refs[:4], refs[4:]
    for r in range(4):
        for n, (first, width) in enumerate(cuts):
            outs[n][r] = parts[r][:, first : first + width]


def stack(parts, cuts, deps=()):
    return call(
        functools.partial(stack_kernel, cuts),
        [Loose(p) for p in parts],
        [full_spec()] * 4,
        [loose((4, UNIT, w)) for _, w in cuts],
        [full_spec()] * len(cuts),
        8,
        deps=deps,
    )


def pass_kernel(in_ref, out_ref):
    out_ref[...] = in_ref[...]


def pass_on(value, deps):
    return call(
        pass_kernel, [Loose(value)], [full_spec()], loose(value.shape, value.dtype), full_spec(), 4, deps=deps
    )


def collect_kernel(place, *refs):
    pieces, outs, here, sems = refs[:4], refs[4:6], refs[6:8], refs[8]
    half = place[0]
    for n, (first, width, times) in enumerate(((0, 1536, 1), (1536, 384, 4))):
        for k in range(16):
            for j in range(times):
                pltpu.make_async_copy(
                    pieces[k // 4].at[k % 4, :, pl.ds(first + j * width, width)],
                    here[n].at[unit_rows(place, half, k, times, j), :],
                    sems.at[n],
                ).start()
    for n in range(2):
        wait_whole(here[n], sems.at[n])
        pltpu.make_async_copy(here[n], outs[n], sems.at[n]).start()
    for n in range(2):
        pltpu.make_async_copy(here[n], outs[n], sems.at[n]).wait()


def collect(place, pieces, deps):
    dims = [(WIDTH, 1536), (INNER, 384)]
    return call(
        collect_kernel,
        [place, *pieces],
        [smem_spec()] + [any_spec()] * 4,
        [loose(d) for d in dims],
        [any_spec()] * 2,
        8,
        scratch=[pltpu.VMEM(d, BF16) for d in dims] + [pltpu.SemaphoreType.DMA((2,))],
        deps=deps,
    )


def sum_kernel(groups, *refs):
    ins, outs = refs[: 4 * groups], refs[4 * groups :]
    for r in range(4):
        first = 0
        for g in range(groups):
            part = ins[4 * g : 4 * g + 4]
            width = part[0].shape[2]
            total = part[0][r].astype(F32)
            for p in part[1:]:
                total = total + p[r].astype(F32)
            outs[r][:, first : first + width] = total.astype(BF16)
            first += width


def sum_blocks(*parts, deps=(), weight=0):
    groups = len(parts) // 4
    width = sum(parts[4 * g].shape[2] for g in range(groups))
    return call(
        functools.partial(sum_kernel, groups),
        [Loose(p) for p in parts],
        [full_spec()] * len(parts),
        [loose((UNIT, width))] * 4,
        [full_spec()] * 4,
        14,
        deps=deps,
        weight=weight,
    )


def finish_kernel(in_ref, dqkv, dout, din, ddown, dvec):
    for h in range(2):
        total = in_ref[h].astype(F32)
        for k in range(h + 2, 8, 2):
            total = total + in_ref[k].astype(F32)
        dqkv[:, 1152 * h : 1152 * h + 1152] = total[:, :1152]
        dout[:, 384 * h : 384 * h + 384] = total[:, 1280:FIRST]
        din[:, 1536 * h : 1536 * h + 1536] = total[:, FIRST : FIRST + 1536]
        for j in range(4):
            first = FIRST + 1536 + 384 * j
            ddown[6 * j : 6 * j + 6, 384 * h : 384 * h + 384] = total[:, first : first + 384]
        if h == 0:
            dvec[...] = total[:, 1152:1280]


def finish(blocks):
    return call(
        finish_kernel,
        [Loose(blocks)],
        [full_spec()],
        [shape(d, F32) for d in ((6, 2304), (6, 768), (6, 3072), (24, 768), (6, 128))],
        [full_spec()] * 5,
        6,
    )


def per_device(
    tokens,
    cotangent,
    span_counts,
    single_flags,
    partner_slots,
    w_qkv,
    b_query,
    b_value,
    w_out,
    b_out,
    gain_attn,
    shift_attn,
    w_in,
    b_in,
    w_down,
    b_down,
    gain_ffn,
    shift_ffn,
):
    place = my_place()
    packed = pack(
        w_qkv, w_out, w_in, w_down, [b_query, b_value, b_out, gain_attn, shift_attn, b_down, gain_ffn, shift_ffn], b_in
    )
    rows48 = exchange_octet(packed)
    one = rows48[:, :, : FIRST + 1536].reshape(UNIT, FIRST + 1536)
    two_down = rows48[:, :, FIRST + 1536 :].reshape(4, 2, 6, 4, 384).transpose(1, 3, 2, 0, 4).reshape(UNIT, 1536)
    unit = jnp.concatenate([one, two_down], axis=1)
    one_early, two_early = stack(gather_early(unit), ((0, FIRST), (FIRST, 3072)))
    one_late = gather_late(one_early)
    two_late = gather_late(two_early)

    count = span_counts[0]
    live = (jnp.arange(8, dtype=jnp.int32) < count).astype(F32)
    keep = (live * (1.0 - single_flags[0].astype(F32)))[:, None]
    partner = partner_slots[0][:, None]
    rows = tokens.reshape(ROWS, WIDTH)

    qkv, probs, heads, norm_one, scale_one, vec, wqkv, wout = attention_forward(
        place, rows, one_late + [to_core(piece) for piece in one_late]
    )
    full_b_in = vec[8:12].T.reshape(1, INNER)
    in_half, down_half = collect(place, two_late, [vec])
    first, sent, win, wdown = first_rows(
        place, norm_one, vec, full_b_in, keep, [in_half, to_core(in_half), down_half, to_core(down_half)]
    )
    partners = [(d, d ^ 64) for d in range(128)]
    received = send(sent, partners)
    half_way = feed_forward(0, count, norm_one, vec, full_b_in, win, wdown)
    dfirst, dreceived = contrast_back(first, received, keep, partner, [half_way[4]])
    returned = send(dreceived, partners)
    hidden_low, active, slope, norm_two, scale_two, mixed = feed_forward(
        1, count, norm_one, vec, full_b_in, win, wdown, half_way, [Loose(dreceived)]
    )
    dres_two, ddown, dupper, sums_two, db_in = feed_forward_back(
        count, cotangent.reshape(ROWS, WIDTH), dfirst, returned, keep, norm_two, scale_two, vec, slope, wdown
    )
    two_mine, two_out = layer_grads(place, active, ddown, hidden_low, dupper)
    two_recv = to_core(two_out)
    dres_one, dattn, dheads, sums_one = hidden_back(dres_two, dupper, norm_one, scale_one, vec, win, wout, [Loose(two_out)])
    two_own = add_theirs(two_mine, two_recv, [sums_one])
    two_parts = scatter_sends(two_own, 1)
    dqkv, sums_qkv = attention_back(qkv, probs, dheads, [Loose(two_own[0])])
    sums_qkv, sums_one, sums_two = [jnp.sum(v.reshape(-1, 8, WIDTH), axis=1) for v in (sums_qkv, sums_one, sums_two)]
    sums = jnp.concatenate(
        [
            sums_qkv,
            sums_one[2:3],
            sums_one[:2],
            sums_two[2:3],
            sums_two[:2],
            jnp.sum(db_in, axis=0).reshape(WIDTH, 4).T,
            jnp.zeros((4, WIDTH), F32),
        ],
        axis=0,
    )
    one_mine, one_out = attention_grads(place, rows, dqkv, heads, dattn, sums, [])
    one_recv = to_core(one_out)
    late = sum_blocks(*two_parts, deps=[one_mine], weight=3e10)
    one_own = add_theirs(one_mine, one_recv, [Loose(late[0])])
    one_parts = scatter_sends(one_own, 1)
    grad_tokens = tokens_back(dres_one, dqkv, wqkv, [Loose(one_own[0])])
    two_late = add_low(scatter_sends(late, 0))
    one_late = add_low(scatter_sends(sum_blocks(*one_parts, deps=[grad_tokens]), 0))
    two_down = two_late[:, 1536:].reshape(2, 4, 6, 4, 384).transpose(3, 0, 2, 1, 4).reshape(8, 6, 1536)
    back = jnp.concatenate([one_late.reshape(8, 6, FIRST), two_late[:, :1536].reshape(8, 6, 1536), two_down], axis=2)
    dqkv_own, dout_own, din_own, ddown_own, dvec = finish(exchange_octet(back))
    return (
        mixed.reshape(tokens.shape),
        grad_tokens.reshape(tokens.shape),
        dqkv_own,
        dvec[:, 0],
        dvec[:, 1],
        dout_own,
        dvec[:, 2],
        dvec[:, 3],
        dvec[:, 4],
        din_own,
        dvec[:, 8:12].reshape(24),
        ddown_own,
        dvec[:, 5],
        dvec[:, 6],
        dvec[:, 7],
    )


def solution(mesh):
    return jax.shard_map(
        per_device,
        mesh=mesh,
        in_specs=(
            P("pair", "dp", None, None),
            P("pair", "dp", None, None),
            P("pair", "dp"),
            P("pair", "dp"),
            P("pair", "dp"),
            P(("pair", "dp"), None),
            P(("pair", "dp")),
            P(("pair", "dp")),
            P(("pair", "dp"), None),
            P(("pair", "dp")),
            P(("pair", "dp")),
            P(("pair", "dp")),
            P(("pair", "dp"), None),
            P(("pair", "dp")),
            P(("pair", "dp"), None),
            P(("pair", "dp")),
            P(("pair", "dp")),
            P(("pair", "dp")),
        ),
        out_specs=(
            P("pair", "dp", None, None),
            P("pair", "dp", None, None),
            P(("pair", "dp"), None),
            P(("pair", "dp")),
            P(("pair", "dp")),
            P(("pair", "dp"), None),
            P(("pair", "dp")),
            P(("pair", "dp")),
            P(("pair", "dp")),
            P(("pair", "dp"), None),
            P(("pair", "dp")),
            P(("pair", "dp"), None),
            P(("pair", "dp")),
            P(("pair", "dp")),
            P(("pair", "dp")),
        ),
        check_vma=False,
    )
```

```python
import functools

import jax
import jax.numpy as jnp
import ml_dtypes
import numpy as np
from jax import lax
from jax.experimental import pallas as pl
from jax.experimental.pallas import tpu as pltpu
from jax.sharding import PartitionSpec as P

HEADS = 12
HEAD_DIM = 64


epsilon = 1e-12
contrast_weight = 8.0
logit_scale = 0.0625


AXES = ("pair", "dp")
HALF_UNIT = 24


def device_index(p, x, y, z, c):
    return (((p * 4 + x) * 4 + y) * 2 + z) * 2 + c


def all_places():
    return [(p, x, y, z, c) for p in range(2) for x in range(4) for y in range(4) for z in range(2) for c in range(2)]


def moved(place, stage, r):
    p, x, y, z, c = place
    if (stage == 0) == (c == 0):
        return (p, x, (y + r) % 4, z, c)
    return (p, (x + r) % 4, y, z, c)


def stage_pairs(stage, r, back=False):
    pairs = [(device_index(*moved(q, stage, r)), device_index(*q)) for q in all_places()]
    return [(t, s) for s, t in pairs] if back else pairs


def core_pairs():
    return [(d, d ^ 1) for d in range(128)]


def octets():
    return [
        [device_index(p, x, y, z, c) for p in range(2) for z in range(2) for c in range(2)]
        for x in range(4)
        for y in range(4)
    ]


def send(value, pairs):
    return lax.ppermute(value, AXES, pairs)


def exchange_octet(value):
    return lax.all_to_all(value, AXES, 0, 0, axis_index_groups=octets(), tiled=True)


def my_place():
    dp = lax.axis_index("dp")
    c, y, x = dp & 1, (dp >> 2) & 3, (dp >> 4) & 3
    i = jnp.arange(16, dtype=jnp.int32)
    far_x, far_y = ((i >> 2) - x) & 3, ((i & 3) - y) & 3
    r = jnp.arange(4, dtype=jnp.int32)
    slots = jnp.where(c == 0, y + r, x + r) & 3
    parts = [c[None], 4 * far_x + far_y, 4 * far_y + far_x, slots, x[None], y[None]]
    return jnp.concatenate(parts).astype(jnp.int32)


WIDE = (1152, 128, 384)
FIRST = sum(WIDE)
SECOND = 3072


def gather_early(block):
    return [block] + [send(block, stage_pairs(0, r)) for r in (1, 2, 3)]


def gather_late(early):
    return [early] + [send(early, stage_pairs(1, r)) for r in (1, 2, 3)]


def to_core(value):
    return send(value, core_pairs())


def scatter_sends(blocks, stage):
    return [blocks[0]] + [send(blocks[r], stage_pairs(stage, r, True)) for r in (1, 2, 3)]


F32 = jnp.float32
BF16 = jnp.bfloat16
NN = (((1,), (0,)), ((), ()))
NT = (((1,), (1,)), ((), ()))
TN = (((0,), (0,)), ((), ()))
ROWS = 1024
BLOCK = 256
STEPS = ROWS // BLOCK
TALL = 512
WIDTH = 768
INNER = 3072
MIB = 2**20
WEIGHTS = {
    "attention_kernel": 0,
    "first_rows_kernel": 1.25e+08,
    "contrast_kernel": 6.25e+06,
    "feed_forward_kernel": 3.125e+08,
    "feed_forward_back_kernel": 3.125e+08,
    "hidden_back_kernel": 3.75e+08,
    "upper_back_kernel": 3.75e+08,
    "lower_back_kernel": 3.75e+08,
    "attention_back_kernel": 3.125e+08,
    "tokens_back_kernel": 2.5e+08,
    "layer_grads_kernel": 6.25e+08,
    "attention_grads_kernel": 3.125e+08,
    "add_kernel": 1.25e+08,
    "gate_kernel": 0,
    "total_kernel": 3.125e+07,
    "collect_kernel": 1.25e+08,
    "stack_kernel": 3.125e+07,
    "pack_kernel": 3.125e+07,
    "finish_kernel": 3.125e+07,
    "sum_kernel": 3.125e+07,
}


def dot(left, right, dims=NN):
    return lax.dot_general(left, right, dims, preferred_element_type=F32)


def full_spec():
    return pl.BlockSpec(memory_space=pltpu.VMEM)


def any_spec():
    return pl.BlockSpec(memory_space=pl.ANY)


def smem_spec():
    return pl.BlockSpec(memory_space=pltpu.SMEM)


def row_spec(width, block=BLOCK):
    return pl.BlockSpec((block, width), lambda i: (i, 0))


def tall_spec(width):
    return row_spec(width, TALL)


def one_spec(rows, width):
    return pl.BlockSpec((rows, width), lambda i: (0, 0))


def shape(dims, dtype=BF16):
    return pltpu.HBM(dims, dtype)


def near(dims, dtype=BF16):
    return pltpu.VMEM(dims, dtype)


def loose(dims, dtype=BF16):
    return jax.ShapeDtypeStruct(dims, dtype)


class Near:
    def __init__(self, value):
        self.value = value


class Loose(Near):
    pass


def pinned(value):
    if isinstance(value, Loose):
        return value.value
    if isinstance(value, Near):
        return pltpu.with_memory_space_constraint(value.value, pltpu.VMEM)
    return pltpu.with_memory_space_constraint(value, pltpu.HBM)


def block_rows(step, block=TALL):
    return pl.ds(pl.multiple_of(step * block, block), block)


def limit(mib):
    return pltpu.CompilerParams(vmem_limit_bytes=mib * MIB)


def call(kernel, args, in_specs, out_shape, out_specs, mib, weight=0, grid=None, scratch=(), deps=(), **more):
    n_args, n_deps = len(args), len(deps)

    def body(*refs):
        kernel(*refs[:n_args], *refs[n_args + n_deps :])

    kwargs = dict(more)
    args = [a if spec.memory_space == pltpu.SMEM else pinned(a) for a, spec in zip(args, in_specs)]
    deps = [pinned(a) for a in deps]
    if grid is not None:
        kwargs["grid"] = grid
    return pl.pallas_call(
        body,
        out_shape=out_shape,
        in_specs=list(in_specs) + [any_spec()] * n_deps,
        out_specs=out_specs,
        scratch_shapes=list(scratch),
        cost_estimate=pl.CostEstimate(flops=int(weight or WEIGHTS.get(getattr(kernel, "func", kernel).__name__, 0)), bytes_accessed=0, transcendentals=0),
        name=getattr(kernel, "func", kernel).__name__,
        compiler_params=limit(24),
        **kwargs,
    )(*args, *deps)


def normalize(resid):
    centered = resid - jnp.mean(resid, axis=-1, keepdims=True)
    variance = jnp.mean(centered * centered, axis=-1, keepdims=True)
    scale = lax.rsqrt(variance + epsilon)
    return centered * scale, scale


def normalize_back(grad, norm, scale):
    mean_grad = jnp.mean(grad, axis=-1, keepdims=True)
    mean_both = jnp.mean(grad * norm, axis=-1, keepdims=True)
    return scale * (grad - mean_grad - norm * mean_both)


def column_sum(value):
    return jnp.sum(value.reshape(-1, 8, value.shape[1]), axis=0)


def add_rows(ref, step, *rows):
    total = jnp.concatenate(list(rows), axis=0)

    @pl.when(step == 0)
    def _():
        ref[...] = total

    @pl.when(step > 0)
    def _():
        ref[...] += total


def piece_copies(place, core, half, pieces, targets, sems):
    x, y = place[37], place[38]
    for r in range(4):
        for n, (ref, at, first, width, blocks) in enumerate(targets):
            for j in range(blocks):
                inner = (j, slice(None), pl.ds(at, width)) if blocks > 1 else (slice(None), pl.ds(at, width))
                for p in range(2):
                    row = (p, (x + r) & 3, slice(None)) if half == 0 else (p, slice(None), (y + r) & 3)
                    pltpu.make_async_copy(
                        pieces[r].at[:, p, :, pl.ds(first + j * width, width)], ref.at[row + inner], sems.at[n]
                    ).start()


def all_piece_copies(place, pieces, targets, sems):
    for core in range(2):

        @pl.when(place[0] == core)
        def _(core=core):
            for half in range(2):
                mine = pieces[:4] if half == core else pieces[4:]
                into = [(ref, half * width, first, width, blocks) for ref, first, width, blocks in targets]
                piece_copies(place, core, half, mine, into, sems)


def flat(value):
    return value.reshape(-1, value.shape[-1])


ORDER = (2, 4, 4, HALF_UNIT)


def wait_whole(ref, sem):
    pltpu.make_async_copy(ref, ref, sem).wait()


def pair_masks():
    lane = lax.broadcasted_iota(jnp.int32, (128, 128), 1)
    return lane < HEAD_DIM


def both_heads(block, low):
    zero = jnp.zeros_like(block)
    return jnp.concatenate([jnp.where(low, block, zero), jnp.where(low, zero, block)], axis=0)


def upright(block):
    return jnp.concatenate([block[:, :128], block[:, 128:]], axis=0)


def attention_kernel(place, x_ref, *refs):
    pieces = refs[:8]
    qkv_ref, probs_ref, heads_ref, norm_ref, scale_ref, vec_ref = refs[8:14]
    wqkv, wout, wvec, sems = refs[14:]
    step = pl.program_id(0)

    @pl.when(step == 0)
    def _():
        for core in range(2):

            @pl.when(place[0] == core)
            def _(core=core):
                for part in range(3):
                    for half in range(2):
                        first = max(768 * part, 1152 * half)
                        width = min(768 * part + 768, 1152 * half + 1152) - first
                        if width > 0:
                            mine = pieces[:4] if half == core else pieces[4:]
                            target = (wqkv, first, first - 1152 * half, width, 1)
                            piece_copies(place, core, half, mine, [target], sems.at[pl.ds(part, 1)])
                    if part == 0:
                        piece_copies(place, core, core, pieces[:4], [(wvec, 0, 1152, 128, 1)], sems.at[pl.ds(3, 1)])

        all_piece_copies(place, pieces, ((wout, 1280, 384, 1),), sems.at[pl.ds(4, 1)])
        wait_whole(wvec, sems.at[3])
        vec_ref[...] = flat(wvec[...]).astype(F32).T[:16]

    x = x_ref[...]
    for n in range(3):

        @pl.when(step == 0)
        def _():
            wait_whole(wqkv.at[:, :, :, :, pl.ds(n * WIDTH, WIDTH)], sems.at[n])

        part = dot(x, flat(wqkv[:, :, :, :, n * WIDTH : (n + 1) * WIDTH]))
        if n != 1:
            part = part + vec_ref[n // 2 : n // 2 + 1, :]
        qkv_ref[:, n * WIDTH : (n + 1) * WIDTH] = part.astype(BF16)
    low = pair_masks()
    for s in range(BLOCK // 128):
        rows = slice(128 * s, 128 * s + 128)
        for h in range(HEADS // 2):
            cols = slice(128 * h, 128 * h + 128)
            query = both_heads(qkv_ref[rows, 128 * h : 128 * h + 128] * BF16(0.125), low)
            keyed = qkv_ref[rows, WIDTH + 128 * h : WIDTH + 128 * h + 128]
            valued = qkv_ref[rows, 2 * WIDTH + 128 * h : 2 * WIDTH + 128 * h + 128]
            scores = dot(keyed, query, NT)
            weight = jnp.exp(scores - jnp.max(scores, axis=0, keepdims=True))
            probs = (weight * (1.0 / jnp.sum(weight, axis=0, keepdims=True))).astype(BF16)
            probs_ref[s, h] = probs
            heads_ref[rows, cols] = dot(upright(probs), both_heads(valued, low), TN).astype(BF16)

    @pl.when(step == 0)
    def _():
        wait_whole(wout, sems.at[4])

    attn = dot(heads_ref[...], flat(wout[...])) + vec_ref[2:3, :]
    norm, scale = normalize(x.astype(F32) + attn)
    norm_ref[...] = norm
    scale_ref[...] = jnp.broadcast_to(scale, scale_ref.shape)


def attention_forward(place, rows, pieces):
    return call(
        attention_kernel,
        [place, rows, *pieces],
        [smem_spec(), row_spec(WIDTH)] + [any_spec()] * 8,
        [
            shape((ROWS, 3 * WIDTH)),
            shape((ROWS // 128, HEADS // 2, 128, 256)),
            shape((ROWS, WIDTH)),
            shape((ROWS, WIDTH), F32),
            shape((ROWS, 128), F32),
            shape((16, WIDTH), F32),
        ],
        [
            row_spec(3 * WIDTH),
            pl.BlockSpec((BLOCK // 128, HEADS // 2, 128, 256), lambda i: (i, 0, 0, 0)),
            row_spec(WIDTH),
            row_spec(WIDTH),
            row_spec(128),
            one_spec(16, WIDTH),
        ],
        20,
        grid=(STEPS,),
        scratch=[
            pltpu.VMEM(ORDER + (3 * WIDTH,), BF16),
            pltpu.VMEM(ORDER + (WIDTH,), BF16),
            pltpu.VMEM(ORDER + (128,), BF16),
            pltpu.SemaphoreType.DMA((5,)),
        ],
    )


def wide_scale(ref):
    return jnp.concatenate([ref[...]] * 6, axis=1)


def hidden_of(norm, vec_ref):
    return norm * vec_ref[3:4, :] + vec_ref[4:5, :]


def gelu_parts(upper):
    phi = 0.5 * (1.0 + lax.erf(upper * 0.7071067811865476))
    bell = jnp.exp(-0.5 * upper * upper) * 0.3989422804014327
    return upper * phi, phi + upper * bell


def first_rows_kernel(place, norm_hbm, vec_ref, b_in_ref, keep_ref, *refs):
    pieces = refs[:8]
    first_ref, sent_ref, win, wdown = refs[8:12]
    rows, sems, rows_sem = refs[12:]
    all_piece_copies(place, pieces, ((win, 0, 1536, 1), (wdown, 1536, 384, 4)), sems)
    for s in range(8):
        pltpu.make_async_copy(norm_hbm.at[pl.ds(128 * s, 8)], rows.at[pl.ds(8 * s, 8)], rows_sem).start()
    wait_whole(rows, rows_sem)
    norm = jnp.concatenate([rows[8 * s : 8 * s + 1, :] for s in range(8)], axis=0)
    hidden = hidden_of(norm, vec_ref)
    wide = jnp.concatenate([hidden, jnp.zeros_like(hidden)], axis=0).astype(BF16)
    wait_whole(win, sems.at[0])
    wait_whole(wdown, sems.at[1])
    down = jnp.zeros((16, WIDTH), F32)
    for n in range(4):
        cols = slice(n * WIDTH, (n + 1) * WIDTH)
        upper = dot(wide, flat(win[:, :, :, :, cols])) + b_in_ref[:, cols]
        part = flat(wdown[n // 2, 2 * (n % 2) : 2 * (n % 2) + 2])
        down = down + dot(gelu_parts(upper)[0].astype(BF16), part)
    final = normalize(hidden + down[:8] + vec_ref[5:6, :])[0] * vec_ref[6:7, :] + vec_ref[7:8, :]
    first_ref[...] = final
    sent_ref[...] = (final.astype(BF16).astype(F32) * keep_ref[...]).astype(BF16)


def first_rows(place, norm, vec, b_in, keep, pieces):
    return call(
        first_rows_kernel,
        [place, norm, vec, b_in, keep, *pieces],
        [smem_spec(), any_spec(), full_spec(), full_spec(), full_spec()] + [any_spec()] * 8,
        [
            shape((8, WIDTH), F32),
            loose((8, WIDTH)),
            near(ORDER + (INNER,)),
            near((2, 4, 4, 4, HALF_UNIT, WIDTH)),
        ],
        [full_spec()] * 4,
        8,
        scratch=[
            pltpu.VMEM((64, WIDTH), F32),
            pltpu.SemaphoreType.DMA((2,)),
            pltpu.SemaphoreType.DMA,
        ],
    )


def contrast_kernel(first_ref, received_ref, keep_ref, partner_ref, dfirst_ref, dreceived_ref):
    first = first_ref[...]
    received = received_ref[...].astype(F32)
    logits = lax.dot_general(first, received, NT, precision=lax.Precision.HIGHEST, preferred_element_type=F32)
    logits = logits * logit_scale
    weight = jnp.exp(logits - jnp.max(logits, axis=-1, keepdims=True))
    soft = weight / jnp.sum(weight, axis=-1, keepdims=True)
    column = lax.broadcasted_iota(jnp.int32, (8, 8), 1)
    chosen = jnp.where(column == partner_ref[...], 1.0, 0.0)
    dlogits = (contrast_weight * logit_scale) * keep_ref[...] * (soft - chosen)
    high = lax.Precision.HIGHEST
    dfirst_ref[...] = lax.dot_general(dlogits, received, NN, precision=high, preferred_element_type=F32)
    dreceived_ref[...] = lax.dot_general(
        dlogits, first, TN, precision=high, preferred_element_type=F32
    ).astype(BF16)


def contrast_back(first, received, keep, partner, deps):
    return call(
        contrast_kernel,
        [Loose(first), Loose(received), Loose(keep), Loose(partner)],
        [full_spec()] * 4,
        [loose((8, WIDTH), F32), loose((8, WIDTH))],
        [full_spec()] * 2,
        4,
        deps=deps,
    )


CHUNK = 512
CHUNKS = INNER // CHUNK


def chunk(n):
    return slice(n * CHUNK, (n + 1) * CHUNK)


def feed_forward_kernel(step, count, norm_ref, vec_ref, b_in_ref, win, wdown, *refs):
    hidden_ref, active_ref, slope_ref, norm_two_ref, scale_ref, mixed_ref = refs[-6:]
    hidden = hidden_of(norm_ref[...], vec_ref)
    hidden_low = hidden.astype(BF16)
    here = block_rows(step)
    hidden_ref[here, :] = hidden_low
    down, active = hidden + vec_ref[5:6, :], None
    after = dot(hidden_low, win[:, chunk(0)])
    for n in range(CHUNKS):
        upper = after + b_in_ref[:, chunk(n)]
        if n + 1 < CHUNKS:
            after = dot(hidden_low, win[:, chunk(n + 1)])
        if n > 0:
            down = down + dot(active, wdown[chunk(n - 1), :])
        active, slope = gelu_parts(upper)
        active = active.astype(BF16)
        active_ref[here, chunk(n)] = active
        slope_ref[here, chunk(n)] = slope.astype(BF16)
    down = down + dot(active, wdown[chunk(CHUNKS - 1), :])
    norm, scale = normalize(down)
    norm_two_ref[...] = norm.astype(BF16)
    scale_ref[...] = jnp.broadcast_to(scale, scale_ref.shape)
    final = norm * vec_ref[6:7, :] + vec_ref[7:8, :]
    for s in range(TALL // 128):
        rows = slice(128 * s, 128 * s + 128)
        live = jnp.where(step * (TALL // 128) + s < count[0], 1.0, 0.0)
        mixed_ref[rows, :] = (final[rows] * live).astype(BF16)


def feed_forward(step, count, norm, vec, b_in, win, wdown, so_far=(), deps=()):
    in_half = pl.BlockSpec((TALL, WIDTH), lambda i: (step, 0))
    wide_half = pl.BlockSpec((TALL, 128), lambda i: (step, 0))
    aliases = {6 + n: n for n in range(len(so_far))}
    return call(
        functools.partial(feed_forward_kernel, step),
        [count, norm, vec, b_in, Near(win), Near(wdown)] + [Near(v) if n < 3 else v for n, v in enumerate(so_far)],
        [smem_spec(), in_half] + [full_spec()] * 4 + ([full_spec()] * 3 + [any_spec()] * 3)[: len(so_far)],
        [
            near((ROWS, WIDTH)),
            near((ROWS, INNER)),
            near((ROWS, INNER)),
            shape((ROWS, WIDTH)),
            shape((ROWS, 128), F32),
            shape((ROWS, WIDTH)),
        ],
        [full_spec()] * 3 + [in_half, wide_half, in_half],
        20,
        grid=(1,),
        input_output_aliases=aliases,
        deps=deps,
    )


def feed_forward_back_kernel(
    count, cot_ref, dfirst_ref, back_ref, keep_ref, norm_ref, scale_ref, vec_ref, slope_ref, wdown, dres_ref, ddown_ref, dupper_ref, sums_ref, db_in_ref
):
    step = pl.program_id(0)
    dfirst = dfirst_ref[...] + back_ref[...].astype(F32) * keep_ref[...]
    slot = lax.broadcasted_iota(jnp.int32, (8, 1), 0)
    parts = []
    for s in range(TALL // 128):
        span = step * (TALL // 128) + s
        live = jnp.where(span < count[0], 1.0, 0.0)
        mine = jnp.sum(jnp.where(slot == span, dfirst, 0.0), axis=0, keepdims=True)
        cot = cot_ref[128 * s : 128 * s + 128, :].astype(F32) * live
        top = cot[:8] + jnp.where(slot == 0, mine, 0.0)
        parts += [top, cot[8:]]
    dfinal = jnp.concatenate(parts, axis=0)
    norm = norm_ref[...].astype(F32)
    dres = normalize_back(dfinal * vec_ref[6:7, :], norm, wide_scale(scale_ref))
    here = block_rows(step)
    dres_ref[here, :] = dres
    ddown = dres.astype(BF16)
    ddown_ref[here, :] = ddown
    after, parts = dot(ddown, wdown[chunk(0), :], NT), []
    for n in range(CHUNKS):
        dactive = after
        if n + 1 < CHUNKS:
            after = dot(ddown, wdown[chunk(n + 1), :], NT)
        dupper = dactive * slope_ref[here, chunk(n)].astype(F32)
        dupper_ref[here, chunk(n)] = dupper.astype(BF16)
        parts.append(column_sum(dupper))
    add_rows(sums_ref, step, column_sum(dfinal * norm), column_sum(dfinal), column_sum(dres))
    add_rows(db_in_ref, step, jnp.concatenate(parts, axis=1))


def feed_forward_back(count, cotangent, dfirst, back, keep, norm, scale, vec, slope, wdown):
    return call(
        feed_forward_back_kernel,
        [count, cotangent, Loose(dfirst), Loose(back), Loose(keep), norm, scale, vec, Near(slope), Near(wdown)],
        [smem_spec(), tall_spec(WIDTH), full_spec(), full_spec(), full_spec(), tall_spec(WIDTH), tall_spec(128)]
        + [full_spec()] * 3,
        [
            near((ROWS, WIDTH), F32),
            near((ROWS, WIDTH)),
            near((ROWS, INNER)),
            shape((24, WIDTH), F32),
            shape((8, INNER), F32),
        ],
        [full_spec(), full_spec(), full_spec(), one_spec(24, WIDTH), one_spec(8, INNER)],
        20,
        grid=(ROWS // TALL,),
        input_output_aliases={8: 2},
    )


def hidden_back_kernel(place, dres_ref, dupper_ref, norm_ref, scale_ref, vec_ref, win, *refs):
    pieces = refs[:8]
    dres_one_ref, dattn_ref, dheads_ref, sums_ref, wout, sems = refs[8:]
    step = pl.program_id(0)
    count = TALL // BLOCK

    @pl.when(step == 0)
    def _():
        all_piece_copies(place, pieces, ((wout, 1280, 384, 1),), sems)

    def here(n):
        return pl.ds(pl.multiple_of(step * TALL + n * BLOCK, BLOCK), BLOCK)

    def product(n):
        return dot(dupper_ref[here(n), :], win[...], NT)

    after, sums = product(0), []

    @pl.when(step == 0)
    def _():
        wait_whole(wout, sems.at[0])

    for n in range(count):
        rows = slice(n * BLOCK, (n + 1) * BLOCK)
        dhidden = dres_ref[here(n), :] + after
        if n + 1 < count:
            after = product(n + 1)
        norm = norm_ref[rows, :]
        scale = jnp.concatenate([scale_ref[rows, :]] * 6, axis=1)
        dres = normalize_back(dhidden * vec_ref[3:4, :], norm, scale)
        dres_one_ref[rows, :] = dres
        dattn = dres.astype(BF16)
        dattn_ref[rows, :] = dattn
        dheads_ref[rows, :] = dot(dattn, flat(wout[...]), NT).astype(BF16)
        sums.append([column_sum(dhidden * norm), column_sum(dhidden), column_sum(dres)])
    add_rows(sums_ref, step, *[sum(group) for group in zip(*sums)])


def hidden_back(place, dres, dupper, norm, scale, vec, win, pieces, deps):
    return call(
        hidden_back_kernel,
        [place, Near(dres), Near(dupper), norm, scale, vec, Near(win), *pieces],
        [smem_spec(), full_spec(), full_spec(), tall_spec(WIDTH), tall_spec(128)] + [full_spec()] * 2 + [any_spec()] * 8,
        [shape((ROWS, WIDTH), F32), shape((ROWS, WIDTH)), shape((ROWS, WIDTH)), shape((24, WIDTH), F32)],
        [tall_spec(WIDTH), tall_spec(WIDTH), tall_spec(WIDTH), one_spec(24, WIDTH)],
        22,
        grid=(ROWS // TALL,),
        scratch=[pltpu.VMEM(ORDER + (WIDTH,), BF16), pltpu.SemaphoreType.DMA((1,))],
        deps=deps,
    )


def attention_back_kernel(qkv_ref, probs_ref, dheads_ref, dqkv_ref, near_ref, sums_ref):
    step = pl.program_id(0)
    low = pair_masks()
    for s in range(BLOCK // 128):
        rows = slice(128 * s, 128 * s + 128)
        for h in range(HEADS // 2):
            query = both_heads(qkv_ref[rows, 128 * h : 128 * h + 128] * BF16(0.125), low)
            keyed = qkv_ref[rows, WIDTH + 128 * h : WIDTH + 128 * h + 128]
            valued = qkv_ref[rows, 2 * WIDTH + 128 * h : 2 * WIDTH + 128 * h + 128]
            dheads = both_heads(dheads_ref[rows, 128 * h : 128 * h + 128], low)
            probs_low = probs_ref[s, h]
            probs = probs_low.astype(F32)
            dprobs = dot(valued, dheads, NT)
            inner = jnp.sum(probs * dprobs, axis=0, keepdims=True)
            dscores = (probs * (dprobs - inner)).astype(BF16)
            dquery = dot(upright(dscores), both_heads(keyed * BF16(0.125), low), TN)
            dqkv_ref[rows, 128 * h : 128 * h + 128] = dquery.astype(BF16)
            dqkv_ref[rows, WIDTH + 128 * h : WIDTH + 128 * h + 128] = dot(dscores, query).astype(BF16)
            dqkv_ref[rows, 2 * WIDTH + 128 * h : 2 * WIDTH + 128 * h + 128] = dot(probs_low, dheads).astype(BF16)
    near_ref[block_rows(step, BLOCK), :] = dqkv_ref[...]
    add_rows(
        sums_ref,
        step,
        column_sum(dqkv_ref[:, :WIDTH].astype(F32)),
        column_sum(dqkv_ref[:, 2 * WIDTH :].astype(F32)),
    )


def attention_back(qkv, probs, dheads, deps):
    return call(
        attention_back_kernel,
        [qkv, probs, dheads],
        [
            row_spec(3 * WIDTH),
            pl.BlockSpec((BLOCK // 128, HEADS // 2, 128, 256), lambda i: (i, 0, 0, 0)),
            row_spec(WIDTH),
        ],
        [shape((ROWS, 3 * WIDTH)), near((ROWS, 3 * WIDTH)), shape((16, WIDTH), F32)],
        [row_spec(3 * WIDTH), full_spec(), one_spec(16, WIDTH)],
        16,
        grid=(STEPS,),
        deps=deps,
    )


def tokens_back_kernel(place, dres_ref, dqkv_ref, *refs):
    pieces, (out_ref, wqkv, sems) = refs[:8], refs[8:]

    @pl.when(pl.program_id(0) == 0)
    def _():
        all_piece_copies(place, pieces, ((wqkv, 0, 1152, 1),), sems)
        wait_whole(wqkv, sems.at[0])

    out_ref[...] = (dres_ref[...] + dot(dqkv_ref[...], flat(wqkv[...]), NT)).astype(BF16)


def tokens_back(place, dres, dqkv, pieces, deps):
    return call(
        tokens_back_kernel,
        [place, dres, dqkv, *pieces],
        [smem_spec(), row_spec(WIDTH), row_spec(3 * WIDTH)] + [any_spec()] * 8,
        shape((ROWS, WIDTH)),
        row_spec(WIDTH),
        14,
        grid=(STEPS,),
        scratch=[pltpu.VMEM(ORDER + (3 * WIDTH,), BF16), pltpu.SemaphoreType.DMA((1,))],
        deps=deps,
    )


def put_unit(place, both, half, unit, p, cols, value):
    side = place[0] if half == 0 else 1 - place[0]
    both[side, place[1 + 16 * half + unit], p, :, cols] = value.astype(BF16)


def put_units(place, both, half, cols, value):
    for p in range(2):
        for unit in range(16):
            row = 384 * p + HALF_UNIT * unit
            put_unit(place, both, half, unit, p, cols, value[row : row + HALF_UNIT])


def write_half(place, both, half, outs, sem, cols):
    for core in range(2):

        @pl.when(place[0] == core)
        def _(side=half ^ core):
            pltpu.make_async_copy(both.at[side, :, :, :, cols], outs[side].at[:, :, :, cols], sem).start()


def run_ahead(jobs):
    after = jobs[0][0]()
    for n, (_, use) in enumerate(jobs):
        value = after
        if n + 1 < len(jobs):
            after = jobs[n + 1][0]()
        use(value)


def layer_grads_kernel(place, active_ref, ddown_ref, hidden_ref, dupper_ref, own, theirs, both, sem):
    outs = (own, theirs)

    def in_job(h, n):
        cols = slice(768 * n, 768 * n + 768)

        def product():
            first = 1536 * h + 768 * n
            return dot(hidden_ref[...], dupper_ref[:, first : first + 768], TN)

        return product, lambda value: put_units(place, both, h, cols, value)

    def down_job(n):
        def product():
            return dot(active_ref[:, WIDTH * n : WIDTH * n + WIDTH], ddown_ref[...], TN)

        def use(value):
            for h in range(2):
                for i in range(2):
                    for y in range(4):
                        for j in range(4):
                            row = 384 * i + 96 * y + HALF_UNIT * j
                            part = value[row : row + HALF_UNIT, 384 * h : 384 * h + 384]
                            cols = slice(1536 + 384 * j, 1536 + 384 * j + 384)
                            put_unit(place, both, h, 4 * (2 * (n % 2) + i) + y, n // 2, cols, part)

        return product, use

    def write(cols):
        for side in (1, 0):
            pltpu.make_async_copy(both.at[side, :, :, :, cols], outs[side].at[:, :, :, cols], sem).start()

    run_ahead([in_job(h, n) for h in range(2) for n in range(2)])
    write(slice(0, 1536))
    run_ahead([down_job(n) for n in range(4)])
    write(slice(1536, 3072))
    wait_whole(both, sem)


def layer_grads(place, active, ddown, hidden_low, dupper):
    return call(
        layer_grads_kernel,
        [place, Near(active), Near(ddown), Near(hidden_low), Near(dupper)],
        [smem_spec()] + [full_spec()] * 4,
        [shape((16, 2, HALF_UNIT, 3072)), loose((16, 2, HALF_UNIT, 3072))],
        [any_spec(), any_spec()],
        20,
        scratch=[pltpu.VMEM((2, 16, 2, HALF_UNIT, 3072), BF16), pltpu.SemaphoreType.DMA],
    )


def attention_grads_kernel(
    place, x_hbm, dqkv_ref, heads_hbm, dattn_hbm, sums_qkv, sums_one, sums_two, db_in, own, theirs, both, x, heads, dattn, sems
):
    pairs = ((x_hbm, x), (heads_hbm, heads), (dattn_hbm, dattn))
    loads = [pltpu.make_async_copy(far, here, sems.at[n]) for n, (far, here) in enumerate(pairs)]
    for load in loads:
        load.start()
    outs, done = (own, theirs), sems.at[3]

    def total(ref, n):
        return jnp.sum(ref[8 * n : 8 * n + 8, :], axis=0, keepdims=True)

    rows = [total(sums_qkv, 0), total(sums_qkv, 1), total(sums_one, 2), total(sums_one, 0), total(sums_one, 1)]
    rows += [total(sums_two, 2), total(sums_two, 0), total(sums_two, 1), db_in[...], jnp.zeros((116, WIDTH), F32)]
    wide = jnp.concatenate(rows, axis=0).T
    put_units(place, both, 0, slice(1152, 1280), wide)
    put_units(place, both, 1, slice(1152, 1280), jnp.zeros_like(wide))
    for load in loads:
        load.wait()

    def job(n):
        def product():
            return dot(x[...], dqkv_ref[:, 768 * n : 768 * n + 768], TN)

        def use(value):
            for m in range(2):
                first = 768 * n + 384 * m
                h, at = first // 1152, first % 1152
                put_units(place, both, h, slice(at, at + 384), value[:, 384 * m : 384 * m + 384])
                write_half(place, both, h, outs, done, slice(at, at + 384))

        return product, use

    def out_product():
        return dot(heads[...], dattn[...], TN)

    def out_use(value):
        for h in range(2):
            put_units(place, both, h, slice(1280, FIRST), value[:, 384 * h : 384 * h + 384])
            write_half(place, both, h, outs, done, slice(1152, FIRST))

    run_ahead([job(n) for n in range(3)] + [(out_product, out_use)])
    wait_whole(both, done)


def attention_grads(place, rows, dqkv, heads, dattn, sums, deps):
    sums_qkv, sums_one, sums_two, db_in = sums
    return call(
        attention_grads_kernel,
        [place, rows, Near(dqkv), heads, dattn, sums_qkv, sums_one, sums_two, db_in],
        [smem_spec(), any_spec(), full_spec(), any_spec(), any_spec()] + [full_spec()] * 4,
        [shape((16, 2, HALF_UNIT, FIRST)), loose((16, 2, HALF_UNIT, FIRST))],
        [any_spec(), any_spec()],
        20,
        scratch=[pltpu.VMEM((2, 16, 2, HALF_UNIT, FIRST), BF16)]
        + [pltpu.VMEM((ROWS, WIDTH), BF16)] * 3
        + [pltpu.SemaphoreType.DMA((4,))],
        deps=deps,
    )


def add_kernel(own_hbm, recv_hbm, *refs):
    outs, (own, recv, sems) = refs[:4], refs[4:]
    loads = []
    for r in range(4):
        part = pl.ds(4 * r, 4)
        pair = [
            pltpu.make_async_copy(own_hbm.at[part], own.at[part], sems.at[2 * r]),
            pltpu.make_async_copy(recv_hbm.at[part], recv.at[part], sems.at[2 * r + 1]),
        ]
        for load in pair:
            load.start()
        loads.append(pair)
    for r in range(4):
        for load in loads[r]:
            load.wait()
        for k in range(4):
            outs[r][k] = (own[4 * r + k].astype(F32) + recv[4 * r + k].astype(F32)).astype(BF16)


def add_theirs(own, recv, deps):
    width = recv.shape[3]
    buffer = pltpu.VMEM((16, 2, HALF_UNIT, width), BF16)
    return call(
        add_kernel,
        [own, Loose(recv)],
        [any_spec()] * 2,
        [loose((4, 2, HALF_UNIT, width))] * 4,
        [full_spec()] * 4,
        18,
        scratch=[buffer, buffer, pltpu.SemaphoreType.DMA((8,))],
        deps=deps,
    )


def pack_kernel(wqkv_hbm, wout_hbm, win_hbm, wdown_hbm, vec, mask, pick, out_ref, wqkv, wout, win, wdown, sems):
    loads = [
        pltpu.make_async_copy(far, here, sems.at[n])
        for n, (far, here) in enumerate(((wqkv_hbm, wqkv), (wout_hbm, wout), (win_hbm, win), (wdown_hbm, wdown)))
    ]
    for load in loads:
        load.start()
    column = dot((vec[...] * mask[...]).astype(BF16), pick[...])[:6].astype(BF16)
    for load in loads:
        load.wait()
    for k in range(8):
        h = k % 2
        out_ref[k, :, :1152] = wqkv[:, 1152 * h : 1152 * h + 1152]
        out_ref[k, :, 1152:1280] = column
        out_ref[k, :, 1280:FIRST] = wout[:, 384 * h : 384 * h + 384]
        out_ref[k, :, FIRST : FIRST + 1536] = win[:, 1536 * h : 1536 * h + 1536]
        for j in range(4):
            first = FIRST + 1536 + 384 * j
            out_ref[k, :, first : first + 384] = wdown[6 * j : 6 * j + 6, 384 * h : 384 * h + 384]


def pack(wqkv, wout, win, wdown, vectors, b_in):
    vec = jnp.zeros((128,), F32)
    for n, v in enumerate(list(vectors) + [b_in]):
        vec = vec + lax.pad(v.astype(F32), jnp.zeros((), F32), [(6 * n, 128 - 6 * n - v.shape[0], 0)])
    j = np.arange(128)
    r = np.where(j < 48, j % 6, np.where(j < 72, (j - 48) // 4, -1))
    i = np.where(j < 48, j // 6, np.where(j < 72, 8 + (j - 48) % 4, -1))
    mask = (r[None, :] == np.arange(8)[:, None]).astype(np.float32)
    pick = (i[:, None] == np.arange(128)[None, :]).astype(ml_dtypes.bfloat16)
    return call(
        pack_kernel,
        [wqkv, wout, win, wdown, vec.reshape(1, 128), mask, pick],
        [any_spec()] * 4 + [full_spec()] * 3,
        loose((8, 6, FIRST + 3072)),
        full_spec(),
        6,
        scratch=[
            pltpu.VMEM((6, 2304), BF16),
            pltpu.VMEM((6, 768), BF16),
            pltpu.VMEM((6, 3072), BF16),
            pltpu.VMEM((24, 768), BF16),
            pltpu.SemaphoreType.DMA((4,)),
        ],
    )


def stack_kernel(cuts, place, *refs):
    parts, outs = refs[:4], refs[4:]
    for r in range(4):
        slot = place[33 + r]
        for n, (first, width) in enumerate(cuts):
            outs[n][slot] = parts[r][:, :, first : first + width]


def stack(place, parts, cuts):
    return call(
        functools.partial(stack_kernel, cuts),
        [place, *[Loose(p) for p in parts]],
        [smem_spec()] + [full_spec()] * 4,
        [loose((4, 2, HALF_UNIT, w)) for _, w in cuts],
        [full_spec()] * len(cuts),
        8,
    )


def gate_kernel(*refs):
    pass


def gate(values, deps):
    return call(
        gate_kernel,
        [Loose(v) for v in values],
        [any_spec()] * len(values),
        [loose(v.shape, v.dtype) for v in values],
        [any_spec()] * len(values),
        2,
        deps=deps,
        input_output_aliases={n: n for n in range(len(values))},
    )


def sum_kernel(sets, more, *refs):
    ins, rest, outs = refs[: 4 * sets], refs[4 * sets : 4 * sets + more], refs[4 * sets + more :]
    for r in range(4):
        first = 0
        for g in range(sets):
            part = ins[4 * g : 4 * g + 4]
            width = part[0].shape[3]
            total = part[0][r].astype(F32)
            for p in part[1:]:
                total = total + p[r].astype(F32)
            outs[r][:, :, first : first + width] = total.astype(BF16)
            first += width
        if more:
            outs[r][:, :, first:] = rest[r][...]


def sum_blocks(parts, more=(), deps=(), weight=0):
    width = parts[0].shape[3] + (more[0].shape[2] if more else 0)
    args = [Loose(p) for p in list(parts) + list(more)]
    return call(
        functools.partial(sum_kernel, 1, len(more)),
        args,
        [full_spec()] * len(args),
        [loose((2, HALF_UNIT, width))] * 4,
        [full_spec()] * 4,
        14,
        deps=deps,
        weight=weight,
    )


def finish_kernel(in_ref, dqkv, dout, din, ddown, *vectors):
    for h in range(2):
        total = in_ref[h].astype(F32)
        for k in range(h + 2, 8, 2):
            total = total + in_ref[k].astype(F32)
        dqkv[:, 1152 * h : 1152 * h + 1152] = total[:, :1152]
        dout[:, 384 * h : 384 * h + 384] = total[:, 1280:FIRST]
        din[:, 1536 * h : 1536 * h + 1536] = total[:, FIRST : FIRST + 1536]
        for j in range(4):
            first = FIRST + 1536 + 384 * j
            ddown[6 * j : 6 * j + 6, 384 * h : 384 * h + 384] = total[:, first : first + 384]
        if h == 0:
            wide = jnp.concatenate([total[:, 1152:1280], jnp.zeros((122, 128), F32)], axis=0).T
    for n in range(8):
        vectors[n][...] = wide[n, :6]
    row = lax.broadcasted_iota(jnp.int32, (128, 128), 0)
    lane = lax.broadcasted_iota(jnp.int32, (128, 128), 1)
    b_in = jnp.zeros((8, 128), F32)
    for j in range(4):
        spread = jnp.where(lane == 4 * row + j, 1.0, 0.0)
        line = jnp.concatenate([wide[8 + j : 9 + j]] * 8, axis=0)
        b_in = b_in + lax.dot_general(line, spread, NN, precision=lax.Precision.HIGHEST, preferred_element_type=F32)
    vectors[8][...] = b_in[0, :24]


def finish(blocks):
    return call(
        finish_kernel,
        [Loose(blocks)],
        [full_spec()],
        [shape(d, F32) for d in ((6, 2304), (6, 768), (6, 3072), (24, 768)) + ((6,),) * 8 + ((24,),)],
        [full_spec()] * 13,
        6,
    )


def total_kernel(*refs):
    total = refs[0][...].astype(F32)
    for part in refs[1:4]:
        total = total + part[...].astype(F32)
    refs[4][...] = total.astype(BF16)


def total_of(parts, deps=()):
    return call(
        total_kernel,
        [Loose(p) for p in parts],
        [full_spec()] * 4,
        loose(parts[0].shape),
        full_spec(),
        6,
        deps=deps,
    )


def per_device(
    tokens,
    cotangent,
    span_counts,
    single_flags,
    partner_slots,
    w_qkv,
    b_query,
    b_value,
    w_out,
    b_out,
    gain_attn,
    shift_attn,
    w_in,
    b_in,
    w_down,
    b_down,
    gain_ffn,
    shift_ffn,
):
    place = my_place()
    packed = pack(
        w_qkv, w_out, w_in, w_down, [b_query, b_value, b_out, gain_attn, shift_attn, b_down, gain_ffn, shift_ffn], b_in
    )
    rows48 = exchange_octet(packed)
    straight = rows48[:, :, : FIRST + 1536].reshape(2, HALF_UNIT, FIRST + 1536)
    turned = rows48[:, :, FIRST + 1536 :].reshape(2, 4, 6, 4, 384).transpose(0, 3, 2, 1, 4).reshape(2, HALF_UNIT, 1536)
    unit = jnp.concatenate([straight, turned], axis=2)
    one_early, two_early = stack(place, gather_early(unit), ((0, FIRST), (FIRST, 3072)))
    one_late = gather_late(one_early)
    one_pieces = one_late + [to_core(piece) for piece in one_late]
    two_late = gather_late(two_early)

    count = span_counts[0]
    live = (jnp.arange(8, dtype=jnp.int32) < count).astype(F32)
    keep = (live * (1.0 - single_flags[0].astype(F32)))[:, None]
    partner = partner_slots[0][:, None]
    rows = tokens.reshape(ROWS, WIDTH)

    qkv, probs, heads, norm_one, scale_one, vec = attention_forward(place, rows, one_pieces)
    full_b_in = vec[8:12].T.reshape(1, INNER)
    two_late = [two_late[0], *gate(two_late[1:], [vec])]
    first, sent, win, wdown = first_rows(
        place, norm_one, vec, full_b_in, keep, two_late + [to_core(piece) for piece in two_late]
    )
    win, wdown = win.reshape(WIDTH, INNER), wdown.reshape(INNER, WIDTH)
    partners = [(d, d ^ 64) for d in range(128)]
    received = send(sent, partners)
    half_way = feed_forward(0, count, norm_one, vec, full_b_in, win, wdown)
    dfirst, dreceived = contrast_back(first, received, keep, partner, [half_way[4]])
    returned = send(dreceived, partners)
    hidden_low, active, slope, norm_two, scale_two, mixed = feed_forward(
        1, count, norm_one, vec, full_b_in, win, wdown, half_way, [Loose(dreceived)]
    )
    dres_two, ddown, dupper, sums_two, db_in = feed_forward_back(
        count, cotangent.reshape(ROWS, WIDTH), dfirst, returned, keep, norm_two, scale_two, vec, slope, wdown
    )
    two_mine, two_out = layer_grads(place, active, ddown, hidden_low, dupper)
    two_recv = to_core(two_out)
    dres_one, dattn, dheads, sums_one = hidden_back(
        place, dres_two, dupper, norm_one, scale_one, vec, win, one_pieces, [Loose(two_out)]
    )
    two_own = add_theirs(two_mine, two_recv, [sums_one])
    two_parts = scatter_sends(two_own, 1)
    dqkv, dqkv_near, sums_qkv = attention_back(qkv, probs, dheads, [Loose(two_own[0])])
    sums = (sums_qkv, sums_one, sums_two, jnp.sum(db_in, axis=0).reshape(WIDTH, 4).T)
    one_mine, one_out = attention_grads(place, rows, dqkv_near, heads, dattn, sums, [])
    one_recv = to_core(one_out)
    late = sum_blocks(two_parts, deps=[one_mine], weight=3e10)
    one_own = add_theirs(one_mine, one_recv, [Loose(late[0])])
    one_parts = scatter_sends(one_own, 1)
    grad_tokens = tokens_back(place, dres_one, dqkv, one_pieces, [Loose(one_own[0])])
    total = total_of(scatter_sends(sum_blocks(one_parts, late, deps=[grad_tokens]), 0))
    straight = total[:, :, : FIRST + 1536].reshape(8, 6, FIRST + 1536)
    turned = total[:, :, FIRST + 1536 :].reshape(2, 4, 6, 4, 384).transpose(0, 3, 2, 1, 4).reshape(8, 6, 1536)
    back = jnp.concatenate([straight, turned], axis=2)
    dqkv_own, dout_own, din_own, ddown_own, *vectors = finish(exchange_octet(back))
    return (
        mixed.reshape(tokens.shape),
        grad_tokens.reshape(tokens.shape),
        dqkv_own,
        vectors[0],
        vectors[1],
        dout_own,
        vectors[2],
        vectors[3],
        vectors[4],
        din_own,
        vectors[8],
        ddown_own,
        vectors[5],
        vectors[6],
        vectors[7],
    )


def solution(mesh):
    return jax.shard_map(
        per_device,
        mesh=mesh,
        in_specs=(
            P("pair", "dp", None, None),
            P("pair", "dp", None, None),
            P("pair", "dp"),
            P("pair", "dp"),
            P("pair", "dp"),
            P(("pair", "dp"), None),
            P(("pair", "dp")),
            P(("pair", "dp")),
            P(("pair", "dp"), None),
            P(("pair", "dp")),
            P(("pair", "dp")),
            P(("pair", "dp")),
            P(("pair", "dp"), None),
            P(("pair", "dp")),
            P(("pair", "dp"), None),
            P(("pair", "dp")),
            P(("pair", "dp")),
            P(("pair", "dp")),
        ),
        out_specs=(
            P("pair", "dp", None, None),
            P("pair", "dp", None, None),
            P(("pair", "dp"), None),
            P(("pair", "dp")),
            P(("pair", "dp")),
            P(("pair", "dp"), None),
            P(("pair", "dp")),
            P(("pair", "dp")),
            P(("pair", "dp")),
            P(("pair", "dp"), None),
            P(("pair", "dp")),
            P(("pair", "dp"), None),
            P(("pair", "dp")),
            P(("pair", "dp")),
            P(("pair", "dp")),
        ),
        check_vma=False,
    )
```

```python
import functools

import jax
import jax.numpy as jnp
import ml_dtypes
import numpy as np
from jax import lax
from jax.experimental import pallas as pl
from jax.experimental.pallas import tpu as pltpu
from jax.sharding import PartitionSpec as P

HEADS = 12
HEAD_DIM = 64


epsilon = 1e-12
contrast_weight = 8.0
logit_scale = 0.0625


AXES = ("pair", "dp")
HALF_UNIT = 24


def device_index(p, x, y, z, c):
    return (((p * 4 + x) * 4 + y) * 2 + z) * 2 + c


def all_places():
    return [(p, x, y, z, c) for p in range(2) for x in range(4) for y in range(4) for z in range(2) for c in range(2)]


def moved(place, stage, r):
    p, x, y, z, c = place
    if (stage == 0) == (c == 0):
        return (p, x, (y + r) % 4, z, c)
    return (p, (x + r) % 4, y, z, c)


def stage_pairs(stage, r, back=False):
    pairs = [(device_index(*moved(q, stage, r)), device_index(*q)) for q in all_places()]
    return [(t, s) for s, t in pairs] if back else pairs


def core_pairs():
    return [(d, d ^ 1) for d in range(128)]


def octets():
    return [
        [device_index(p, x, y, z, c) for p in range(2) for z in range(2) for c in range(2)]
        for x in range(4)
        for y in range(4)
    ]


def send(value, pairs):
    return lax.ppermute(value, AXES, pairs)


def exchange_octet(value):
    return lax.all_to_all(value, AXES, 0, 0, axis_index_groups=octets(), tiled=True)


def my_place():
    dp = lax.axis_index("dp")
    c, y, x = dp & 1, (dp >> 2) & 3, (dp >> 4) & 3
    i = jnp.arange(16, dtype=jnp.int32)
    far_x, far_y = ((i >> 2) - x) & 3, ((i & 3) - y) & 3
    r = jnp.arange(4, dtype=jnp.int32)
    slots = jnp.where(c == 0, y + r, x + r) & 3
    parts = [c[None], 4 * far_x + far_y, 4 * far_y + far_x, slots, x[None], y[None]]
    return jnp.concatenate(parts).astype(jnp.int32)


WIDE = (1152, 128, 384)
FIRST = sum(WIDE)
SECOND = 3072


def gather(block, stage):
    return [block] + [send(block, stage_pairs(stage, r)) for r in (3, 2, 1)]


def to_core(value):
    return send(value, core_pairs())


def scatter_sends(blocks, stage):
    return [blocks[0]] + [send(blocks[r], stage_pairs(stage, r, True)) for r in (1, 2, 3)]


F32 = jnp.float32
BF16 = jnp.bfloat16
NN = (((1,), (0,)), ((), ()))
NT = (((1,), (1,)), ((), ()))
TN = (((0,), (0,)), ((), ()))
ROWS = 1024
BLOCK = 256
STEPS = ROWS // BLOCK
TALL = 512
WIDTH = 768
INNER = 3072
MIB = 2**20
WEIGHTS = {
    "attention_kernel": 0,
    "feed_forward_first_kernel": 3.75e+08,
    "contrast_kernel": 6.25e+06,
    "feed_forward_kernel": 1.875e+08,
    "feed_forward_back_kernel": 3.125e+08,
    "hidden_back_kernel": 3.75e+08,
    "upper_back_kernel": 3.75e+08,
    "lower_back_kernel": 3.75e+08,
    "attention_back_kernel": 3.125e+08,
    "tokens_back_kernel": 2.5e+08,
    "layer_grads_kernel": 6.25e+08,
    "attention_grads_kernel": 3.125e+08,
    "add_kernel": 1.25e+08,
    "gate_kernel": 0,
    "total_kernel": 3.125e+07,
    "collect_kernel": 1.25e+08,
    "stack_kernel": 3.125e+07,
    "pack_kernel": 3.125e+07,
    "finish_kernel": 3.125e+07,
    "sum_kernel": 3.125e+07,
}


def dot(left, right, dims=NN):
    return lax.dot_general(left, right, dims, preferred_element_type=F32)


def full_spec():
    return pl.BlockSpec(memory_space=pltpu.VMEM)


def any_spec():
    return pl.BlockSpec(memory_space=pl.ANY)


def smem_spec():
    return pl.BlockSpec(memory_space=pltpu.SMEM)


def row_spec(width, block=BLOCK):
    return pl.BlockSpec((block, width), lambda i: (i, 0))


def tall_spec(width):
    return row_spec(width, TALL)


def one_spec(rows, width):
    return pl.BlockSpec((rows, width), lambda i: (0, 0))


def shape(dims, dtype=BF16):
    return pltpu.HBM(dims, dtype)


def near(dims, dtype=BF16):
    return pltpu.VMEM(dims, dtype)


def loose(dims, dtype=BF16):
    return jax.ShapeDtypeStruct(dims, dtype)


class Near:
    def __init__(self, value):
        self.value = value


class Loose(Near):
    pass


def pinned(value):
    if isinstance(value, Loose):
        return value.value
    if isinstance(value, Near):
        return pltpu.with_memory_space_constraint(value.value, pltpu.VMEM)
    return pltpu.with_memory_space_constraint(value, pltpu.HBM)


def block_rows(step, block=TALL):
    return pl.ds(pl.multiple_of(step * block, block), block)


def limit(mib):
    return pltpu.CompilerParams(vmem_limit_bytes=mib * MIB)


def call(kernel, args, in_specs, out_shape, out_specs, mib, weight=0, grid=None, scratch=(), deps=(), **more):
    n_args, n_deps = len(args), len(deps)

    def body(*refs):
        kernel(*refs[:n_args], *refs[n_args + n_deps :])

    kwargs = dict(more)
    args = [a if spec.memory_space == pltpu.SMEM else pinned(a) for a, spec in zip(args, in_specs)]
    deps = [pinned(a) for a in deps]
    if grid is not None:
        kwargs["grid"] = grid
    return pl.pallas_call(
        body,
        out_shape=out_shape,
        in_specs=list(in_specs) + [any_spec()] * n_deps,
        out_specs=out_specs,
        scratch_shapes=list(scratch),
        cost_estimate=pl.CostEstimate(flops=int(weight or WEIGHTS.get(getattr(kernel, "func", kernel).__name__, 0)), bytes_accessed=0, transcendentals=0),
        name=getattr(kernel, "func", kernel).__name__,
        compiler_params=limit(24),
        **kwargs,
    )(*args, *deps)


def normalize(resid):
    centered = resid - jnp.mean(resid, axis=-1, keepdims=True)
    variance = jnp.mean(centered * centered, axis=-1, keepdims=True)
    scale = lax.rsqrt(variance + epsilon)
    return centered * scale, scale


def normalize_back(grad, norm, scale):
    mean_grad = jnp.mean(grad, axis=-1, keepdims=True)
    mean_both = jnp.mean(grad * norm, axis=-1, keepdims=True)
    return scale * (grad - mean_grad - norm * mean_both)


def column_sum(value):
    return jnp.sum(value.reshape(-1, 8, value.shape[1]), axis=0)


def add_rows(ref, step, *rows):
    total = jnp.concatenate(list(rows), axis=0)

    @pl.when(step == 0)
    def _():
        ref[...] = total

    @pl.when(step > 0)
    def _():
        ref[...] += total


def piece_copies(place, core, half, pieces, targets, sems):
    x, y = place[37], place[38]
    for q in range(4):
        r = (4 - q) % 4
        for n, (ref, at, first, width, blocks) in enumerate(targets):
            for j in range(blocks):
                inner = (j, slice(None), pl.ds(at, width)) if blocks > 1 else (slice(None), pl.ds(at, width))
                for p in range(2):
                    row = (p, (x + r) & 3, slice(None)) if half == 0 else (p, slice(None), (y + r) & 3)
                    pltpu.make_async_copy(
                        pieces[q].at[:, p, :, pl.ds(first + j * width, width)], ref.at[row + inner], sems.at[n]
                    ).start()


def all_piece_copies(place, pieces, targets, sems):
    for core in range(2):

        @pl.when(place[0] == core)
        def _(core=core):
            for half in range(2):
                mine = pieces[:4] if half == core else pieces[4:]
                into = [(ref, half * width, first, width, blocks) for ref, first, width, blocks in targets]
                piece_copies(place, core, half, mine, into, sems)


def flat(value):
    return value.reshape(-1, value.shape[-1])


ORDER = (2, 4, 4, HALF_UNIT)


def wait_whole(ref, sem):
    pltpu.make_async_copy(ref, ref, sem).wait()


def pair_masks():
    lane = lax.broadcasted_iota(jnp.int32, (128, 128), 1)
    return lane < HEAD_DIM


def both_heads(block, low):
    zero = jnp.zeros_like(block)
    return jnp.concatenate([jnp.where(low, block, zero), jnp.where(low, zero, block)], axis=0)


def upright(block):
    return jnp.concatenate([block[:, :128], block[:, 128:]], axis=0)


def attention_kernel(place, x_ref, *refs):
    pieces = refs[:8]
    qkv_ref, probs_ref, heads_ref, norm_ref, scale_ref, vec_ref = refs[8:14]
    wqkv, wout, wvec, sems = refs[14:]
    step = pl.program_id(0)

    @pl.when(step == 0)
    def _():
        for core in range(2):

            @pl.when(place[0] == core)
            def _(core=core):
                for part in range(3):
                    for half in range(2):
                        first = max(768 * part, 1152 * half)
                        width = min(768 * part + 768, 1152 * half + 1152) - first
                        if width > 0:
                            mine = pieces[:4] if half == core else pieces[4:]
                            target = (wqkv, first, first - 1152 * half, width, 1)
                            piece_copies(place, core, half, mine, [target], sems.at[pl.ds(part, 1)])
                    if part == 0:
                        piece_copies(place, core, core, pieces[:4], [(wvec, 0, 1152, 128, 1)], sems.at[pl.ds(3, 1)])

        all_piece_copies(place, pieces, ((wout, 1280, 384, 1),), sems.at[pl.ds(4, 1)])
        wait_whole(wvec, sems.at[3])
        vec_ref[...] = flat(wvec[...]).astype(F32).T[:16]

    x = x_ref[...]
    for n in range(3):

        @pl.when(step == 0)
        def _():
            wait_whole(wqkv.at[:, :, :, :, pl.ds(n * WIDTH, WIDTH)], sems.at[n])

        part = dot(x, flat(wqkv[:, :, :, :, n * WIDTH : (n + 1) * WIDTH]))
        if n != 1:
            part = part + vec_ref[n // 2 : n // 2 + 1, :]
        qkv_ref[:, n * WIDTH : (n + 1) * WIDTH] = part.astype(BF16)
    low = pair_masks()
    for s in range(BLOCK // 128):
        rows = slice(128 * s, 128 * s + 128)
        for h in range(HEADS // 2):
            cols = slice(128 * h, 128 * h + 128)
            query = both_heads(qkv_ref[rows, 128 * h : 128 * h + 128] * BF16(0.125), low)
            keyed = qkv_ref[rows, WIDTH + 128 * h : WIDTH + 128 * h + 128]
            valued = qkv_ref[rows, 2 * WIDTH + 128 * h : 2 * WIDTH + 128 * h + 128]
            scores = dot(keyed, query, NT)
            weight = jnp.exp(scores - jnp.max(scores, axis=0, keepdims=True))
            probs = (weight * (1.0 / jnp.sum(weight, axis=0, keepdims=True))).astype(BF16)
            probs_ref[s, h] = probs
            heads_ref[rows, cols] = dot(upright(probs), both_heads(valued, low), TN).astype(BF16)

    @pl.when(step == 0)
    def _():
        wait_whole(wout, sems.at[4])

    attn = dot(heads_ref[...], flat(wout[...])) + vec_ref[2:3, :]
    norm, scale = normalize(x.astype(F32) + attn)
    norm_ref[...] = norm
    scale_ref[...] = jnp.broadcast_to(scale, scale_ref.shape)


def attention_forward(place, rows, pieces):
    return call(
        attention_kernel,
        [place, rows, *pieces],
        [smem_spec(), row_spec(WIDTH)] + [any_spec()] * 8,
        [
            shape((ROWS, 3 * WIDTH)),
            shape((ROWS // 128, HEADS // 2, 128, 256)),
            shape((ROWS, WIDTH)),
            shape((ROWS, WIDTH), F32),
            shape((ROWS, 128), F32),
            shape((16, WIDTH), F32),
        ],
        [
            row_spec(3 * WIDTH),
            pl.BlockSpec((BLOCK // 128, HEADS // 2, 128, 256), lambda i: (i, 0, 0, 0)),
            row_spec(WIDTH),
            row_spec(WIDTH),
            row_spec(128),
            one_spec(16, WIDTH),
        ],
        20,
        grid=(STEPS,),
        scratch=[
            pltpu.VMEM(ORDER + (3 * WIDTH,), BF16),
            pltpu.VMEM(ORDER + (WIDTH,), BF16),
            pltpu.VMEM(ORDER + (128,), BF16),
            pltpu.SemaphoreType.DMA((5,)),
        ],
    )


def wide_scale(ref):
    return jnp.concatenate([ref[...]] * 6, axis=1)


def hidden_of(norm, vec_ref):
    return norm * vec_ref[3:4, :] + vec_ref[4:5, :]


def gelu_parts(upper):
    phi = 0.5 * (1.0 + lax.erf(upper * 0.7071067811865476))
    bell = jnp.exp(-0.5 * upper * upper) * 0.3989422804014327
    return upper * phi, phi + upper * bell


def contrast_kernel(first_ref, received_ref, keep_ref, partner_ref, dfirst_ref, dreceived_ref):
    first = first_ref[...]
    received = received_ref[...].astype(F32)
    logits = lax.dot_general(first, received, NT, precision=lax.Precision.HIGHEST, preferred_element_type=F32)
    logits = logits * logit_scale
    weight = jnp.exp(logits - jnp.max(logits, axis=-1, keepdims=True))
    soft = weight / jnp.sum(weight, axis=-1, keepdims=True)
    column = lax.broadcasted_iota(jnp.int32, (8, 8), 1)
    chosen = jnp.where(column == partner_ref[...], 1.0, 0.0)
    dlogits = (contrast_weight * logit_scale) * keep_ref[...] * (soft - chosen)
    high = lax.Precision.HIGHEST
    dfirst_ref[...] = lax.dot_general(dlogits, received, NN, precision=high, preferred_element_type=F32)
    dreceived_ref[...] = lax.dot_general(
        dlogits, first, TN, precision=high, preferred_element_type=F32
    ).astype(BF16)


def contrast_back(first, received, keep, partner, deps):
    return call(
        contrast_kernel,
        [Loose(first), Loose(received), Loose(keep), Loose(partner)],
        [full_spec()] * 4,
        [loose((8, WIDTH), F32), loose((8, WIDTH))],
        [full_spec()] * 2,
        4,
        deps=deps,
    )


CHUNK = 512
CHUNKS = INNER // CHUNK


def chunk(n):
    return slice(n * CHUNK, (n + 1) * CHUNK)


def feed_forward_rows(hidden, vec_ref, b_in_ref, size, win_part, wdown_part, put):
    hidden_low = hidden.astype(BF16)
    down, active = hidden + vec_ref[5:6, :], None
    after = dot(hidden_low, win_part(0))
    for n in range(INNER // size):
        upper = after + b_in_ref[:, n * size : (n + 1) * size]
        if (n + 1) * size < INNER:
            after = dot(hidden_low, win_part(n + 1))
        if n > 0:
            down = down + dot(active, wdown_part(n - 1))
        active, slope = gelu_parts(upper)
        active = active.astype(BF16)
        put(slice(n * size, (n + 1) * size), active, slope.astype(BF16))
    down = down + dot(active, wdown_part(INNER // size - 1))
    return normalize(down)


def put_norm(first_span, count, norm, scale, vec_ref, norm_two_ref, scale_ref, mixed_ref):
    norm_two_ref[...] = norm.astype(BF16)
    scale_ref[...] = jnp.broadcast_to(scale, scale_ref.shape)
    final = norm * vec_ref[6:7, :] + vec_ref[7:8, :]
    for s in range(norm.shape[0] // 128):
        rows = slice(128 * s, 128 * s + 128)
        live = jnp.where(first_span + s < count[0], 1.0, 0.0)
        mixed_ref[rows, :] = (final[rows] * live).astype(BF16)


def feed_forward_first_kernel(place, count, norm_ref, norm_hbm, vec_ref, b_in_ref, keep_ref, *refs):
    pieces = refs[:8]
    first_ref, sent_ref, win, wdown, hidden_ref, active_ref, slope_ref, norm_two_ref, scale_ref, mixed_ref = refs[8:18]
    tops, sems, tops_sem = refs[18:]
    for s in range(8):
        pltpu.make_async_copy(norm_hbm.at[pl.ds(128 * s, 8)], tops.at[pl.ds(8 * s, 8)], tops_sem).start()
    all_piece_copies(place, pieces, ((win, 0, 1536, 1),), sems)
    all_piece_copies(place, pieces, ((wdown, 1536, 384, 4),), sems.at[pl.ds(1, 1)])
    wait_whole(tops, tops_sem)
    top = hidden_of(jnp.concatenate([tops[8 * s : 8 * s + 1, :] for s in range(8)], axis=0), vec_ref)
    hidden = hidden_of(norm_ref[...], vec_ref)
    hidden_ref[:TALL, :] = hidden.astype(BF16)
    hidden = jnp.concatenate([hidden, top, jnp.zeros_like(top)], axis=0)
    wait_whole(win, sems.at[0])

    def win_part(n):
        return flat(win[:, :, :, :, n * WIDTH : (n + 1) * WIDTH])

    def wdown_part(n):
        if n == 0:
            wait_whole(wdown, sems.at[1])
        return flat(wdown[n // 2, 2 * (n % 2) : 2 * (n % 2) + 2])

    def put(cols, active, slope):
        active_ref[:TALL, cols] = active[:TALL]
        slope_ref[:TALL, cols] = slope[:TALL]

    norm, scale = feed_forward_rows(hidden, vec_ref, b_in_ref, WIDTH, win_part, wdown_part, put)
    put_norm(0, count, norm[:TALL], scale[:TALL], vec_ref, norm_two_ref, scale_ref, mixed_ref)
    final = norm[TALL : TALL + 8] * vec_ref[6:7, :] + vec_ref[7:8, :]
    first_ref[...] = final
    sent_ref[...] = (final.astype(BF16).astype(F32) * keep_ref[...]).astype(BF16)


def feed_forward_shapes():
    return [
        near((ROWS, WIDTH)),
        near((ROWS, INNER)),
        near((ROWS, INNER)),
        shape((ROWS, WIDTH)),
        shape((ROWS, 128), F32),
        shape((ROWS, WIDTH)),
    ]


def feed_forward_first(place, count, norm, vec, b_in, keep, pieces):
    def rows(width):
        return pl.BlockSpec((TALL, width), lambda i: (0, 0))

    return call(
        feed_forward_first_kernel,
        [place, count, norm, norm, vec, b_in, keep, *pieces],
        [smem_spec(), smem_spec(), rows(WIDTH), any_spec()] + [full_spec()] * 3 + [any_spec()] * 8,
        [
            shape((8, WIDTH), F32),
            loose((8, WIDTH)),
            near(ORDER + (INNER,)),
            near((2, 4, 4, 4, HALF_UNIT, WIDTH)),
        ]
        + feed_forward_shapes(),
        [full_spec()] * 7 + [rows(WIDTH), rows(128), rows(WIDTH)],
        24,
        grid=(1,),
        scratch=[
            pltpu.VMEM((64, WIDTH), F32),
            pltpu.SemaphoreType.DMA((2,)),
            pltpu.SemaphoreType.DMA,
        ],
    )


def feed_forward_kernel(index, count, norm_ref, vec_ref, b_in_ref, win, wdown, *refs):
    hidden_ref, active_ref, slope_ref, norm_two_ref, scale_ref, mixed_ref = refs[-6:]
    here = slice(index * BLOCK, (index + 1) * BLOCK)
    hidden = hidden_of(norm_ref[...], vec_ref)
    hidden_ref[here, :] = hidden.astype(BF16)

    def put(cols, active, slope):
        active_ref[here, cols] = active
        slope_ref[here, cols] = slope

    norm, scale = feed_forward_rows(
        hidden, vec_ref, b_in_ref, CHUNK, lambda n: win[:, chunk(n)], lambda n: wdown[chunk(n), :], put
    )
    put_norm(index * (BLOCK // 128), count, norm, scale, vec_ref, norm_two_ref, scale_ref, mixed_ref)


def feed_forward(index, count, norm, vec, b_in, win, wdown, so_far, deps=()):
    def rows(width):
        return pl.BlockSpec((BLOCK, width), lambda i: (index, 0))

    return call(
        functools.partial(feed_forward_kernel, index),
        [count, norm, vec, b_in, Near(win), Near(wdown)] + [Near(v) if n < 3 else v for n, v in enumerate(so_far)],
        [smem_spec(), rows(WIDTH)] + [full_spec()] * 7 + [any_spec()] * 3,
        feed_forward_shapes(),
        [full_spec()] * 3 + [rows(WIDTH), rows(128), rows(WIDTH)],
        20,
        grid=(1,),
        input_output_aliases={6 + n: n for n in range(6)},
        deps=deps,
    )


def feed_forward_back_kernel(
    count, cot_ref, dfirst_ref, back_ref, keep_ref, norm_ref, scale_ref, vec_ref, slope_ref, wdown, dres_ref, ddown_ref, dupper_ref, sums_ref, db_in_ref
):
    step = pl.program_id(0)
    dfirst = dfirst_ref[...] + back_ref[...].astype(F32) * keep_ref[...]
    slot = lax.broadcasted_iota(jnp.int32, (8, 1), 0)
    blocks = TALL // BLOCK

    def here(b):
        return pl.ds(pl.multiple_of(step * TALL + b * BLOCK, BLOCK), BLOCK)

    def norm_back(b):
        parts = []
        for s in range(BLOCK // 128):
            row = b * BLOCK + 128 * s
            span = step * (TALL // 128) + b * (BLOCK // 128) + s
            live = jnp.where(span < count[0], 1.0, 0.0)
            mine = jnp.sum(jnp.where(slot == span, dfirst, 0.0), axis=0, keepdims=True)
            cot = cot_ref[row : row + 128, :].astype(F32) * live
            top = cot[:8] + jnp.where(slot == 0, mine, 0.0)
            parts += [top, cot[8:]]
        dfinal = jnp.concatenate(parts, axis=0)
        rows = slice(b * BLOCK, (b + 1) * BLOCK)
        norm = norm_ref[rows, :].astype(F32)
        scale = jnp.concatenate([scale_ref[rows, :]] * 6, axis=1)
        dres = normalize_back(dfinal * vec_ref[6:7, :], norm, scale)
        dres_ref[here(b), :] = dres
        ddown = dres.astype(BF16)
        ddown_ref[here(b), :] = ddown
        return ddown, [column_sum(dfinal * norm), column_sum(dfinal), column_sum(dres)]

    jobs = [(b, n) for b in range(blocks) for n in range(CHUNKS)]
    ready, sums, sums_in = norm_back(0), [], [[] for _ in range(blocks)]
    sums.append(ready[1])
    ddown = ready[0]
    after = dot(ddown, wdown[chunk(0), :], NT)
    for k, (b, n) in enumerate(jobs):
        dactive = after
        if n == 0 and b + 1 < blocks:
            ready = norm_back(b + 1)
            sums.append(ready[1])
        if k + 1 < len(jobs):
            if n + 1 == CHUNKS:
                ddown = ready[0]
            after = dot(ddown, wdown[chunk(jobs[k + 1][1]), :], NT)
        dupper = dactive * slope_ref[here(b), chunk(n)].astype(F32)
        dupper_ref[here(b), chunk(n)] = dupper.astype(BF16)
        sums_in[b].append(column_sum(dupper))
    add_rows(sums_ref, step, *[sum(group) for group in zip(*sums)])
    add_rows(db_in_ref, step, sum(jnp.concatenate(parts, axis=1) for parts in sums_in))


def feed_forward_back(count, cotangent, dfirst, back, keep, norm, scale, vec, slope, wdown):
    return call(
        feed_forward_back_kernel,
        [count, cotangent, Loose(dfirst), Loose(back), Loose(keep), norm, scale, vec, Near(slope), Near(wdown)],
        [smem_spec(), tall_spec(WIDTH), full_spec(), full_spec(), full_spec(), tall_spec(WIDTH), tall_spec(128)]
        + [full_spec()] * 3,
        [
            near((ROWS, WIDTH), F32),
            near((ROWS, WIDTH)),
            near((ROWS, INNER)),
            shape((24, WIDTH), F32),
            shape((8, INNER), F32),
        ],
        [full_spec(), full_spec(), full_spec(), one_spec(24, WIDTH), one_spec(8, INNER)],
        20,
        grid=(ROWS // TALL,),
        input_output_aliases={8: 2},
    )


def hidden_back_kernel(place, dres_ref, dupper_ref, norm_ref, scale_ref, vec_ref, win, *refs):
    pieces = refs[:8]
    dres_one_ref, dattn_ref, dheads_ref, sums_ref, wout, sems = refs[8:]
    step = pl.program_id(0)
    count = TALL // BLOCK

    @pl.when(step == 0)
    def _():
        all_piece_copies(place, pieces, ((wout, 1280, 384, 1),), sems)

    def here(n):
        return pl.ds(pl.multiple_of(step * TALL + n * BLOCK, BLOCK), BLOCK)

    def product(n):
        return dot(dupper_ref[here(n), :], win[...], NT)

    after, sums = product(0), []

    @pl.when(step == 0)
    def _():
        wait_whole(wout, sems.at[0])

    for n in range(count):
        rows = slice(n * BLOCK, (n + 1) * BLOCK)
        dhidden = dres_ref[here(n), :] + after
        if n + 1 < count:
            after = product(n + 1)
        norm = norm_ref[rows, :]
        scale = jnp.concatenate([scale_ref[rows, :]] * 6, axis=1)
        dres = normalize_back(dhidden * vec_ref[3:4, :], norm, scale)
        dres_one_ref[rows, :] = dres
        dattn = dres.astype(BF16)
        dattn_ref[rows, :] = dattn
        dheads_ref[rows, :] = dot(dattn, flat(wout[...]), NT).astype(BF16)
        sums.append([column_sum(dhidden * norm), column_sum(dhidden), column_sum(dres)])
    add_rows(sums_ref, step, *[sum(group) for group in zip(*sums)])


def hidden_back(place, dres, dupper, norm, scale, vec, win, pieces, deps):
    return call(
        hidden_back_kernel,
        [place, Near(dres), Near(dupper), norm, scale, vec, Near(win), *pieces],
        [smem_spec(), full_spec(), full_spec(), tall_spec(WIDTH), tall_spec(128)] + [full_spec()] * 2 + [any_spec()] * 8,
        [shape((ROWS, WIDTH), F32), shape((ROWS, WIDTH)), shape((ROWS, WIDTH)), shape((24, WIDTH), F32)],
        [tall_spec(WIDTH), tall_spec(WIDTH), tall_spec(WIDTH), one_spec(24, WIDTH)],
        22,
        grid=(ROWS // TALL,),
        scratch=[pltpu.VMEM(ORDER + (WIDTH,), BF16), pltpu.SemaphoreType.DMA((1,))],
        deps=deps,
    )


def attention_back_kernel(qkv_ref, probs_ref, dheads_ref, dqkv_ref, near_ref, sums_ref):
    step = pl.program_id(0)
    low = pair_masks()
    for s in range(BLOCK // 128):
        rows = slice(128 * s, 128 * s + 128)
        for h in range(HEADS // 2):
            query = both_heads(qkv_ref[rows, 128 * h : 128 * h + 128] * BF16(0.125), low)
            keyed = qkv_ref[rows, WIDTH + 128 * h : WIDTH + 128 * h + 128]
            valued = qkv_ref[rows, 2 * WIDTH + 128 * h : 2 * WIDTH + 128 * h + 128]
            dheads = both_heads(dheads_ref[rows, 128 * h : 128 * h + 128], low)
            probs_low = probs_ref[s, h]
            probs = probs_low.astype(F32)
            dprobs = dot(valued, dheads, NT)
            inner = jnp.sum(probs * dprobs, axis=0, keepdims=True)
            dscores = (probs * (dprobs - inner)).astype(BF16)
            dquery = dot(upright(dscores), both_heads(keyed * BF16(0.125), low), TN)
            dqkv_ref[rows, 128 * h : 128 * h + 128] = dquery.astype(BF16)
            dqkv_ref[rows, WIDTH + 128 * h : WIDTH + 128 * h + 128] = dot(dscores, query).astype(BF16)
            dqkv_ref[rows, 2 * WIDTH + 128 * h : 2 * WIDTH + 128 * h + 128] = dot(probs_low, dheads).astype(BF16)
    near_ref[block_rows(step, BLOCK), :] = dqkv_ref[...]
    add_rows(
        sums_ref,
        step,
        column_sum(dqkv_ref[:, :WIDTH].astype(F32)),
        column_sum(dqkv_ref[:, 2 * WIDTH :].astype(F32)),
    )


def attention_back(qkv, probs, dheads, deps):
    return call(
        attention_back_kernel,
        [qkv, probs, dheads],
        [
            row_spec(3 * WIDTH),
            pl.BlockSpec((BLOCK // 128, HEADS // 2, 128, 256), lambda i: (i, 0, 0, 0)),
            row_spec(WIDTH),
        ],
        [shape((ROWS, 3 * WIDTH)), near((ROWS, 3 * WIDTH)), shape((16, WIDTH), F32)],
        [row_spec(3 * WIDTH), full_spec(), one_spec(16, WIDTH)],
        16,
        grid=(STEPS,),
        deps=deps,
    )


def tokens_back_kernel(place, dres_ref, dqkv_ref, *refs):
    pieces, (out_ref, wqkv, sems) = refs[:8], refs[8:]

    @pl.when(pl.program_id(0) == 0)
    def _():
        all_piece_copies(place, pieces, ((wqkv, 0, 1152, 1),), sems)
        wait_whole(wqkv, sems.at[0])

    out_ref[...] = (dres_ref[...] + dot(dqkv_ref[...], flat(wqkv[...]), NT)).astype(BF16)


def tokens_back(place, dres, dqkv, pieces, deps):
    return call(
        tokens_back_kernel,
        [place, dres, dqkv, *pieces],
        [smem_spec(), row_spec(WIDTH), row_spec(3 * WIDTH)] + [any_spec()] * 8,
        shape((ROWS, WIDTH)),
        row_spec(WIDTH),
        14,
        grid=(STEPS,),
        scratch=[pltpu.VMEM(ORDER + (3 * WIDTH,), BF16), pltpu.SemaphoreType.DMA((1,))],
        deps=deps,
    )


def put_unit(place, both, half, unit, p, cols, value):
    side = place[0] if half == 0 else 1 - place[0]
    both[side, place[1 + 16 * half + unit], p, :, cols] = value.astype(BF16)


def put_units(place, both, half, cols, value):
    for p in range(2):
        for unit in range(16):
            row = 384 * p + HALF_UNIT * unit
            put_unit(place, both, half, unit, p, cols, value[row : row + HALF_UNIT])


def write_half(place, both, half, outs, sem, cols):
    for core in range(2):

        @pl.when(place[0] == core)
        def _(side=half ^ core):
            pltpu.make_async_copy(both.at[side, :, :, :, cols], outs[side].at[:, :, :, cols], sem).start()


def run_ahead(jobs):
    after = jobs[0][0]()
    for n, (_, use) in enumerate(jobs):
        value = after
        if n + 1 < len(jobs):
            after = jobs[n + 1][0]()
        use(value)


def layer_grads_kernel(place, active_ref, ddown_ref, hidden_ref, dupper_ref, own, theirs, both, sem):
    outs = (own, theirs)

    def in_job(h, n):
        cols = slice(768 * n, 768 * n + 768)

        def product():
            first = 1536 * h + 768 * n
            return dot(hidden_ref[...], dupper_ref[:, first : first + 768], TN)

        return product, lambda value: put_units(place, both, h, cols, value)

    def down_job(n):
        def product():
            return dot(active_ref[:, WIDTH * n : WIDTH * n + WIDTH], ddown_ref[...], TN)

        def use(value):
            for h in range(2):
                for i in range(2):
                    for y in range(4):
                        for j in range(4):
                            row = 384 * i + 96 * y + HALF_UNIT * j
                            part = value[row : row + HALF_UNIT, 384 * h : 384 * h + 384]
                            cols = slice(1536 + 384 * j, 1536 + 384 * j + 384)
                            put_unit(place, both, h, 4 * (2 * (n % 2) + i) + y, n // 2, cols, part)

        return product, use

    def write(p, cols):
        for side in (1, 0):
            pltpu.make_async_copy(both.at[side, :, p, :, cols], outs[side].at[:, p, :, cols], sem).start()

    run_ahead([in_job(h, n) for h in range(2) for n in range(2)])
    write(0, slice(0, 1536))
    write(1, slice(0, 1536))
    run_ahead([down_job(n) for n in range(2)])
    write(0, slice(1536, 3072))
    run_ahead([down_job(n) for n in range(2, 4)])
    write(1, slice(1536, 3072))
    wait_whole(both, sem)


def layer_grads(place, active, ddown, hidden_low, dupper):
    return call(
        layer_grads_kernel,
        [place, Near(active), Near(ddown), Near(hidden_low), Near(dupper)],
        [smem_spec()] + [full_spec()] * 4,
        [shape((16, 2, HALF_UNIT, 3072)), loose((16, 2, HALF_UNIT, 3072))],
        [any_spec(), any_spec()],
        20,
        scratch=[pltpu.VMEM((2, 16, 2, HALF_UNIT, 3072), BF16), pltpu.SemaphoreType.DMA],
    )


def every_fourth(line, j):
    blocks = jnp.concatenate([line[:, 512 * n : 512 * n + 512] for n in range(6)] + [jnp.zeros((2, 512), F32)], axis=0)
    row = lax.broadcasted_iota(jnp.int32, (512, 128), 0)
    lane = lax.broadcasted_iota(jnp.int32, (512, 128), 1)
    pick = jnp.where(row == 4 * lane + j, 1.0, 0.0)
    picked = lax.dot_general(blocks, pick, NN, precision=lax.Precision.HIGHEST, preferred_element_type=F32)
    return jnp.concatenate([picked[n : n + 1] for n in range(6)], axis=1)


def attention_grads_kernel(
    place, x_hbm, dqkv_ref, heads_hbm, dattn_hbm, sums_qkv, sums_one, sums_two, db_in, own, theirs, both, x, heads, dattn, sems
):
    pairs = ((x_hbm, x), (heads_hbm, heads), (dattn_hbm, dattn))
    loads = [pltpu.make_async_copy(far, here, sems.at[n]) for n, (far, here) in enumerate(pairs)]
    for load in loads:
        load.start()
    outs, done = (own, theirs), sems.at[3]

    def total(ref, n):
        return jnp.sum(ref[8 * n : 8 * n + 8, :], axis=0, keepdims=True)

    rows = [total(sums_qkv, 0), total(sums_qkv, 1), total(sums_one, 2), total(sums_one, 0), total(sums_one, 1)]
    rows += [total(sums_two, 2), total(sums_two, 0), total(sums_two, 1)]
    rows += [every_fourth(total(db_in, 0), j) for j in range(4)] + [jnp.zeros((116, WIDTH), F32)]
    wide = jnp.concatenate(rows, axis=0).T
    put_units(place, both, 0, slice(1152, 1280), wide)
    put_units(place, both, 1, slice(1152, 1280), jnp.zeros_like(wide))
    loads[0].wait()

    def job(n):
        def product():
            return dot(x[...], dqkv_ref[:, 768 * n : 768 * n + 768], TN)

        def use(value):
            for m in range(2):
                first = 768 * n + 384 * m
                h, at = first // 1152, first % 1152
                put_units(place, both, h, slice(at, at + 384), value[:, 384 * m : 384 * m + 384])
                write_half(place, both, h, outs, done, slice(at, at + 384))

        return product, use

    def out_product():
        loads[1].wait()
        loads[2].wait()
        return dot(heads[...], dattn[...], TN)

    def out_use(value):
        for h in range(2):
            put_units(place, both, h, slice(1280, FIRST), value[:, 384 * h : 384 * h + 384])
            write_half(place, both, h, outs, done, slice(1152, FIRST))

    run_ahead([job(n) for n in range(3)] + [(out_product, out_use)])
    wait_whole(both, done)


def attention_grads(place, rows, dqkv, heads, dattn, sums, deps):
    sums_qkv, sums_one, sums_two, db_in = sums
    return call(
        attention_grads_kernel,
        [place, rows, Near(dqkv), heads, dattn, sums_qkv, sums_one, sums_two, db_in],
        [smem_spec(), any_spec(), full_spec(), any_spec(), any_spec()] + [full_spec()] * 4,
        [shape((16, 2, HALF_UNIT, FIRST)), loose((16, 2, HALF_UNIT, FIRST))],
        [any_spec(), any_spec()],
        20,
        scratch=[pltpu.VMEM((2, 16, 2, HALF_UNIT, FIRST), BF16)]
        + [pltpu.VMEM((ROWS, WIDTH), BF16)] * 3
        + [pltpu.SemaphoreType.DMA((4,))],
        deps=deps,
    )


def add_kernel(own_hbm, recv_hbm, *refs):
    outs, (own, recv, sems) = refs[:-3], refs[-3:]
    loads = []
    for r in range(4):
        part = pl.ds(4 * r, 4)
        pair = [
            pltpu.make_async_copy(own_hbm.at[part], own.at[part], sems.at[2 * r]),
            pltpu.make_async_copy(recv_hbm.at[part], recv.at[part], sems.at[2 * r + 1]),
        ]
        for load in pair:
            load.start()
        loads.append(pair)
    for r in range(4):
        for load in loads[r]:
            load.wait()
        for k in range(4):
            outs[r][k] = (own[4 * r + k].astype(F32) + recv[4 * r + k].astype(F32)).astype(BF16)


def add_theirs(own, recv, deps):
    width = recv.shape[3]
    buffer = pltpu.VMEM((16, 2, HALF_UNIT, width), BF16)
    return call(
        add_kernel,
        [own, Loose(recv)],
        [any_spec()] * 2,
        [loose((4, 2, HALF_UNIT, width))] * 4,
        [full_spec()] * 4,
        18,
        scratch=[buffer, buffer, pltpu.SemaphoreType.DMA((8,))],
        deps=deps,
    )


def pack_kernel(wqkv_hbm, wout_hbm, win_hbm, wdown_hbm, vec, mask, pick, out_ref, wqkv, wout, win, wdown, sems):
    loads = [
        pltpu.make_async_copy(far, here, sems.at[n])
        for n, (far, here) in enumerate(((wqkv_hbm, wqkv), (wout_hbm, wout), (win_hbm, win), (wdown_hbm, wdown)))
    ]
    for load in loads:
        load.start()
    column = dot((vec[...] * mask[...]).astype(BF16), pick[...])[:6].astype(BF16)
    for load in loads:
        load.wait()
    for k in range(8):
        h = k % 2
        out_ref[k, :, :1152] = wqkv[:, 1152 * h : 1152 * h + 1152]
        out_ref[k, :, 1152:1280] = column
        out_ref[k, :, 1280:FIRST] = wout[:, 384 * h : 384 * h + 384]
        out_ref[k, :, FIRST : FIRST + 1536] = win[:, 1536 * h : 1536 * h + 1536]
        for j in range(4):
            first = FIRST + 1536 + 384 * j
            out_ref[k, :, first : first + 384] = wdown[6 * j : 6 * j + 6, 384 * h : 384 * h + 384]


def pack(wqkv, wout, win, wdown, vectors, b_in):
    vec = jnp.zeros((128,), F32)
    for n, v in enumerate(list(vectors) + [b_in]):
        vec = vec + lax.pad(v.astype(F32), jnp.zeros((), F32), [(6 * n, 128 - 6 * n - v.shape[0], 0)])
    j = np.arange(128)
    r = np.where(j < 48, j % 6, np.where(j < 72, (j - 48) // 4, -1))
    i = np.where(j < 48, j // 6, np.where(j < 72, 8 + (j - 48) % 4, -1))
    mask = (r[None, :] == np.arange(8)[:, None]).astype(np.float32)
    pick = (i[:, None] == np.arange(128)[None, :]).astype(ml_dtypes.bfloat16)
    return call(
        pack_kernel,
        [wqkv, wout, win, wdown, vec.reshape(1, 128), mask, pick],
        [any_spec()] * 4 + [full_spec()] * 3,
        loose((8, 6, FIRST + 3072)),
        full_spec(),
        6,
        scratch=[
            pltpu.VMEM((6, 2304), BF16),
            pltpu.VMEM((6, 768), BF16),
            pltpu.VMEM((6, 3072), BF16),
            pltpu.VMEM((24, 768), BF16),
            pltpu.SemaphoreType.DMA((4,)),
        ],
    )


def stack_kernel(cuts, place, *refs):
    parts, outs = refs[:4], refs[4:]
    for q in range(4):
        slot = place[33 + (4 - q) % 4]
        for n, (first, width) in enumerate(cuts):
            outs[n][slot] = parts[q][:, :, first : first + width]


def stack(place, parts, cuts):
    return call(
        functools.partial(stack_kernel, cuts),
        [place, *[Loose(p) for p in parts]],
        [smem_spec()] + [full_spec()] * 4,
        [loose((4, 2, HALF_UNIT, w)) for _, w in cuts],
        [full_spec()] * len(cuts),
        8,
    )


def gate_kernel(*refs):
    pass


def gate(values, deps):
    return call(
        gate_kernel,
        [Loose(v) for v in values],
        [any_spec()] * len(values),
        [loose(v.shape, v.dtype) for v in values],
        [any_spec()] * len(values),
        2,
        deps=deps,
        input_output_aliases={n: n for n in range(len(values))},
    )


def sum_kernel(sets, more, *refs):
    ins, rest, outs = refs[: 4 * sets], refs[4 * sets : 4 * sets + more], refs[4 * sets + more :]
    for r in range(4):
        first = 0
        for g in range(sets):
            part = ins[4 * g : 4 * g + 4]
            width = part[0].shape[3]
            total = part[0][r].astype(F32)
            for p in part[1:]:
                total = total + p[r].astype(F32)
            outs[r][:, :, first : first + width] = total.astype(BF16)
            first += width
        if more:
            outs[r][:, :, first:] = rest[r][...]


def sum_blocks(parts, more=(), deps=(), weight=0):
    width = parts[0].shape[3] + (more[0].shape[2] if more else 0)
    args = [Loose(p) for p in list(parts) + list(more)]
    return call(
        functools.partial(sum_kernel, 1, len(more)),
        args,
        [full_spec()] * len(args),
        [loose((2, HALF_UNIT, width))] * 4,
        [full_spec()] * 4,
        14,
        deps=deps,
        weight=weight,
    )


def finish_kernel(in_ref, dqkv, dout, din, ddown, *vectors):
    for h in range(2):
        total = in_ref[h].astype(F32)
        for k in range(h + 2, 8, 2):
            total = total + in_ref[k].astype(F32)
        dqkv[:, 1152 * h : 1152 * h + 1152] = total[:, :1152]
        dout[:, 384 * h : 384 * h + 384] = total[:, 1280:FIRST]
        din[:, 1536 * h : 1536 * h + 1536] = total[:, FIRST : FIRST + 1536]
        for j in range(4):
            first = FIRST + 1536 + 384 * j
            ddown[6 * j : 6 * j + 6, 384 * h : 384 * h + 384] = total[:, first : first + 384]
        if h == 0:
            wide = jnp.concatenate([total[:, 1152:1280], jnp.zeros((122, 128), F32)], axis=0).T
    for n in range(8):
        vectors[n][...] = wide[n, :6]
    row = lax.broadcasted_iota(jnp.int32, (128, 128), 0)
    lane = lax.broadcasted_iota(jnp.int32, (128, 128), 1)
    b_in = jnp.zeros((8, 128), F32)
    for j in range(4):
        spread = jnp.where(lane == 4 * row + j, 1.0, 0.0)
        line = jnp.concatenate([wide[8 + j : 9 + j]] * 8, axis=0)
        b_in = b_in + lax.dot_general(line, spread, NN, precision=lax.Precision.HIGHEST, preferred_element_type=F32)
    vectors[8][...] = b_in[0, :24]


def finish(blocks):
    return call(
        finish_kernel,
        [Loose(blocks)],
        [full_spec()],
        [shape(d, F32) for d in ((6, 2304), (6, 768), (6, 3072), (24, 768)) + ((6,),) * 8 + ((24,),)],
        [full_spec()] * 13,
        6,
    )


def total_kernel(*refs):
    total = refs[0][...].astype(F32)
    for part in refs[1:4]:
        total = total + part[...].astype(F32)
    refs[4][...] = total.astype(BF16)


def total_of(parts, deps=()):
    return call(
        total_kernel,
        [Loose(p) for p in parts],
        [full_spec()] * 4,
        loose(parts[0].shape),
        full_spec(),
        6,
        deps=deps,
    )


def per_device(
    tokens,
    cotangent,
    span_counts,
    single_flags,
    partner_slots,
    w_qkv,
    b_query,
    b_value,
    w_out,
    b_out,
    gain_attn,
    shift_attn,
    w_in,
    b_in,
    w_down,
    b_down,
    gain_ffn,
    shift_ffn,
):
    place = my_place()
    packed = pack(
        w_qkv, w_out, w_in, w_down, [b_query, b_value, b_out, gain_attn, shift_attn, b_down, gain_ffn, shift_ffn], b_in
    )
    rows48 = exchange_octet(packed)
    straight = rows48[:, :, : FIRST + 1536].reshape(2, HALF_UNIT, FIRST + 1536)
    turned = rows48[:, :, FIRST + 1536 :].reshape(2, 4, 6, 4, 384).transpose(0, 3, 2, 1, 4).reshape(2, HALF_UNIT, 1536)
    unit = jnp.concatenate([straight, turned], axis=2)
    one_early, two_early = stack(place, gather(unit, 0), ((0, FIRST), (FIRST, 3072)))
    one_late = gather(one_early, 1)
    one_pieces = one_late + [to_core(piece) for piece in one_late]
    two_late = gather(two_early, 1)

    count = span_counts[0]
    live = (jnp.arange(8, dtype=jnp.int32) < count).astype(F32)
    keep = (live * (1.0 - single_flags[0].astype(F32)))[:, None]
    partner = partner_slots[0][:, None]
    rows = tokens.reshape(ROWS, WIDTH)

    qkv, probs, heads, norm_one, scale_one, vec = attention_forward(place, rows, one_pieces)
    full_b_in = vec[8:12].T.reshape(1, INNER)
    two_late = [two_late[0], *gate(two_late[1:], [vec])]
    first, sent, win, wdown, *so_far = feed_forward_first(
        place, count, norm_one, vec, full_b_in, keep, two_late + [to_core(piece) for piece in two_late]
    )
    win, wdown = win.reshape(WIDTH, INNER), wdown.reshape(INNER, WIDTH)
    partners = [(d, d ^ 64) for d in range(128)]
    received = send(sent, partners)
    so_far = feed_forward(2, count, norm_one, vec, full_b_in, win, wdown, so_far)
    dfirst, dreceived = contrast_back(first, received, keep, partner, [so_far[4]])
    returned = send(dreceived, partners)
    hidden_low, active, slope, norm_two, scale_two, mixed = feed_forward(
        3, count, norm_one, vec, full_b_in, win, wdown, so_far, [Loose(dreceived)]
    )
    dres_two, ddown, dupper, sums_two, db_in = feed_forward_back(
        count, cotangent.reshape(ROWS, WIDTH), dfirst, returned, keep, norm_two, scale_two, vec, slope, wdown
    )
    two_mine, two_out = layer_grads(place, active, ddown, hidden_low, dupper)
    two_recv = to_core(two_out)
    dres_one, dattn, dheads, sums_one = hidden_back(
        place, dres_two, dupper, norm_one, scale_one, vec, win, one_pieces, [Loose(two_out)]
    )
    two_own = add_theirs(two_mine, two_recv, [sums_one])
    two_parts = scatter_sends(two_own, 1)
    dqkv, dqkv_near, sums_qkv = attention_back(qkv, probs, dheads, [Loose(two_own[0])])
    sums = (sums_qkv, sums_one, sums_two, db_in)
    one_mine, one_out = attention_grads(place, rows, dqkv_near, heads, dattn, sums, [])
    one_recv = to_core(one_out)
    late = sum_blocks(two_parts, deps=[one_mine], weight=3e10)
    one_own = add_theirs(one_mine, one_recv, [Loose(late[0])])
    one_parts = scatter_sends(one_own, 1)
    grad_tokens = tokens_back(place, dres_one, dqkv, one_pieces, [Loose(one_own[0])])
    total = total_of(scatter_sends(sum_blocks(one_parts, late, deps=[grad_tokens]), 0))
    straight = total[:, :, : FIRST + 1536].reshape(8, 6, FIRST + 1536)
    turned = total[:, :, FIRST + 1536 :].reshape(2, 4, 6, 4, 384).transpose(0, 3, 2, 1, 4).reshape(8, 6, 1536)
    back = jnp.concatenate([straight, turned], axis=2)
    dqkv_own, dout_own, din_own, ddown_own, *vectors = finish(exchange_octet(back))
    return (
        mixed.reshape(tokens.shape),
        grad_tokens.reshape(tokens.shape),
        dqkv_own,
        vectors[0],
        vectors[1],
        dout_own,
        vectors[2],
        vectors[3],
        vectors[4],
        din_own,
        vectors[8],
        ddown_own,
        vectors[5],
        vectors[6],
        vectors[7],
    )


def solution(mesh):
    return jax.shard_map(
        per_device,
        mesh=mesh,
        in_specs=(
            P("pair", "dp", None, None),
            P("pair", "dp", None, None),
            P("pair", "dp"),
            P("pair", "dp"),
            P("pair", "dp"),
            P(("pair", "dp"), None),
            P(("pair", "dp")),
            P(("pair", "dp")),
            P(("pair", "dp"), None),
            P(("pair", "dp")),
            P(("pair", "dp")),
            P(("pair", "dp")),
            P(("pair", "dp"), None),
            P(("pair", "dp")),
            P(("pair", "dp"), None),
            P(("pair", "dp")),
            P(("pair", "dp")),
            P(("pair", "dp")),
        ),
        out_specs=(
            P("pair", "dp", None, None),
            P("pair", "dp", None, None),
            P(("pair", "dp"), None),
            P(("pair", "dp")),
            P(("pair", "dp")),
            P(("pair", "dp"), None),
            P(("pair", "dp")),
            P(("pair", "dp")),
            P(("pair", "dp")),
            P(("pair", "dp"), None),
            P(("pair", "dp")),
            P(("pair", "dp"), None),
            P(("pair", "dp")),
            P(("pair", "dp")),
            P(("pair", "dp")),
        ),
        check_vma=False,
    )
```

```python
import functools

import jax
import jax.numpy as jnp
import ml_dtypes
import numpy as np
from jax import lax
from jax.experimental import pallas as pl
from jax.experimental.pallas import tpu as pltpu
from jax.sharding import PartitionSpec as P

HEADS = 12
HEAD_DIM = 64


epsilon = 1e-12
contrast_weight = 8.0
logit_scale = 0.0625


AXES = ("pair", "dp")
HALF_UNIT = 24


def device_index(p, x, y, z, c):
    return (((p * 4 + x) * 4 + y) * 2 + z) * 2 + c


def all_places():
    return [(p, x, y, z, c) for p in range(2) for x in range(4) for y in range(4) for z in range(2) for c in range(2)]


def moved(place, stage, r):
    p, x, y, z, c = place
    if (stage == 0) == (c == 0):
        return (p, x, (y + r) % 4, z, c)
    return (p, (x + r) % 4, y, z, c)


def stage_pairs(stage, r, back=False):
    pairs = [(device_index(*moved(q, stage, r)), device_index(*q)) for q in all_places()]
    return [(t, s) for s, t in pairs] if back else pairs


def core_pairs():
    return [(d, d ^ 1) for d in range(128)]


def octets():
    return [
        [device_index(p, x, y, z, c) for p in range(2) for z in range(2) for c in range(2)]
        for x in range(4)
        for y in range(4)
    ]


def send(value, pairs):
    return lax.ppermute(value, AXES, pairs)


def exchange_octet(value):
    return lax.all_to_all(value, AXES, 0, 0, axis_index_groups=octets(), tiled=True)


def my_place():
    dp = lax.axis_index("dp")
    c, y, x = dp & 1, (dp >> 2) & 3, (dp >> 4) & 3
    i = jnp.arange(16, dtype=jnp.int32)
    far_x, far_y = ((i >> 2) - x) & 3, ((i & 3) - y) & 3
    r = jnp.arange(4, dtype=jnp.int32)
    slots = jnp.where(c == 0, y + r, x + r) & 3
    parts = [c[None], 4 * far_x + far_y, 4 * far_y + far_x, slots, x[None], y[None]]
    return jnp.concatenate(parts).astype(jnp.int32)


WIDE = (1152, 128, 384)
FIRST = sum(WIDE)
SECOND = 3072


def gather(block, stage):
    return [block] + [send(block, stage_pairs(stage, r)) for r in (3, 2, 1)]


def to_core(value):
    return send(value, core_pairs())


def scatter_sends(blocks, stage):
    return [blocks[0]] + [send(blocks[r], stage_pairs(stage, r, True)) for r in (1, 2, 3)]


F32 = jnp.float32
BF16 = jnp.bfloat16
NN = (((1,), (0,)), ((), ()))
NT = (((1,), (1,)), ((), ()))
TN = (((0,), (0,)), ((), ()))
ROWS = 1024
BLOCK = 256
STEPS = ROWS // BLOCK
TALL = 512
WIDTH = 768
INNER = 3072
MIB = 2**20
WEIGHTS = {
    "attention_kernel": 0,
    "feed_forward_first_kernel": 3.75e+08,
    "contrast_kernel": 6.25e+06,
    "feed_forward_kernel": 1.875e+08,
    "feed_forward_back_kernel": 3.125e+08,
    "hidden_back_kernel": 3.75e+08,
    "upper_back_kernel": 3.75e+08,
    "lower_back_kernel": 3.75e+08,
    "attention_back_kernel": 3.125e+08,
    "tokens_back_kernel": 2.5e+08,
    "layer_grads_kernel": 6.25e+08,
    "attention_grads_kernel": 3.125e+08,
    "add_kernel": 1.25e+08,
    "gate_kernel": 0,
    "total_kernel": 3.125e+07,
    "collect_kernel": 1.25e+08,
    "stack_kernel": 3.125e+07,
    "pack_kernel": 3.125e+07,
    "finish_kernel": 3.125e+07,
    "sum_kernel": 3.125e+07,
}


def dot(left, right, dims=NN):
    return lax.dot_general(left, right, dims, preferred_element_type=F32)


def full_spec():
    return pl.BlockSpec(memory_space=pltpu.VMEM)


def any_spec():
    return pl.BlockSpec(memory_space=pl.ANY)


def smem_spec():
    return pl.BlockSpec(memory_space=pltpu.SMEM)


def row_spec(width, block=BLOCK):
    return pl.BlockSpec((block, width), lambda i: (i, 0))


def tall_spec(width):
    return row_spec(width, TALL)


def one_spec(rows, width):
    return pl.BlockSpec((rows, width), lambda i: (0, 0))


def shape(dims, dtype=BF16):
    return pltpu.HBM(dims, dtype)


def near(dims, dtype=BF16):
    return pltpu.VMEM(dims, dtype)


def loose(dims, dtype=BF16):
    return jax.ShapeDtypeStruct(dims, dtype)


class Near:
    def __init__(self, value):
        self.value = value


class Loose(Near):
    pass


def pinned(value):
    if isinstance(value, Loose):
        return value.value
    if isinstance(value, Near):
        return pltpu.with_memory_space_constraint(value.value, pltpu.VMEM)
    return pltpu.with_memory_space_constraint(value, pltpu.HBM)


def block_rows(step, block=TALL):
    return pl.ds(pl.multiple_of(step * block, block), block)


def limit(mib):
    return pltpu.CompilerParams(vmem_limit_bytes=mib * MIB)


def call(kernel, args, in_specs, out_shape, out_specs, mib, weight=0, grid=None, scratch=(), deps=(), **more):
    n_args, n_deps = len(args), len(deps)

    def body(*refs):
        kernel(*refs[:n_args], *refs[n_args + n_deps :])

    kwargs = dict(more)
    args = [a if spec.memory_space == pltpu.SMEM else pinned(a) for a, spec in zip(args, in_specs)]
    deps = [pinned(a) for a in deps]
    if grid is not None:
        kwargs["grid"] = grid
    return pl.pallas_call(
        body,
        out_shape=out_shape,
        in_specs=list(in_specs) + [any_spec()] * n_deps,
        out_specs=out_specs,
        scratch_shapes=list(scratch),
        cost_estimate=pl.CostEstimate(flops=int(weight or WEIGHTS.get(getattr(kernel, "func", kernel).__name__, 0)), bytes_accessed=0, transcendentals=0),
        name=getattr(kernel, "func", kernel).__name__,
        compiler_params=limit(24),
        **kwargs,
    )(*args, *deps)


def normalize(resid):
    centered = resid - jnp.mean(resid, axis=-1, keepdims=True)
    variance = jnp.mean(centered * centered, axis=-1, keepdims=True)
    scale = lax.rsqrt(variance + epsilon)
    return centered * scale, scale


def normalize_back(grad, norm, scale):
    mean_grad = jnp.mean(grad, axis=-1, keepdims=True)
    mean_both = jnp.mean(grad * norm, axis=-1, keepdims=True)
    return scale * (grad - mean_grad - norm * mean_both)


def column_sum(value):
    return jnp.sum(value.reshape(-1, 8, value.shape[1]), axis=0)


def add_rows(ref, step, *rows):
    total = jnp.concatenate(list(rows), axis=0)

    @pl.when(step == 0)
    def _():
        ref[...] = total

    @pl.when(step > 0)
    def _():
        ref[...] += total


def piece_copies(place, core, half, pieces, targets, sems):
    x, y = place[37], place[38]
    for q in range(4):
        r = (4 - q) % 4
        for n, (ref, at, first, width, blocks) in enumerate(targets):
            for j in range(blocks):
                inner = (j, slice(None), pl.ds(at, width)) if blocks > 1 else (slice(None), pl.ds(at, width))
                for p in range(2):
                    row = (p, (x + r) & 3, slice(None)) if half == 0 else (p, slice(None), (y + r) & 3)
                    pltpu.make_async_copy(
                        pieces[q].at[:, p, :, pl.ds(first + j * width, width)], ref.at[row + inner], sems.at[n]
                    ).start()


def all_piece_copies(place, pieces, targets, sems):
    for core in range(2):

        @pl.when(place[0] == core)
        def _(core=core):
            for half in range(2):
                mine = pieces[:4] if half == core else pieces[4:]
                into = [(ref, half * width, first, width, blocks) for ref, first, width, blocks in targets]
                piece_copies(place, core, half, mine, into, sems)


def flat(value):
    return value.reshape(-1, value.shape[-1])


ORDER = (2, 4, 4, HALF_UNIT)


def wait_whole(ref, sem):
    pltpu.make_async_copy(ref, ref, sem).wait()


def pair_masks():
    lane = lax.broadcasted_iota(jnp.int32, (128, 128), 1)
    return lane < HEAD_DIM


def both_heads(block, low):
    zero = jnp.zeros_like(block)
    return jnp.concatenate([jnp.where(low, block, zero), jnp.where(low, zero, block)], axis=0)


def upright(block):
    return jnp.concatenate([block[:, :128], block[:, 128:]], axis=0)


def attention_kernel(place, x_ref, *refs):
    pieces = refs[:8]
    qkv_ref, probs_ref, heads_ref, norm_ref, scale_ref, vec_ref, wout_hbm = refs[8:15]
    wqkv, wout, wvec, sems = refs[15:]
    step = pl.program_id(0)

    @pl.when(step == 0)
    def _():
        for core in range(2):

            @pl.when(place[0] == core)
            def _(core=core):
                for part in range(3):
                    for half in range(2):
                        first = max(768 * part, 1152 * half)
                        width = min(768 * part + 768, 1152 * half + 1152) - first
                        if width > 0:
                            mine = pieces[:4] if half == core else pieces[4:]
                            target = (wqkv, first, first - 1152 * half, width, 1)
                            piece_copies(place, core, half, mine, [target], sems.at[pl.ds(part, 1)])
                    if part == 0:
                        piece_copies(place, core, core, pieces[:4], [(wvec, 0, 1152, 128, 1)], sems.at[pl.ds(3, 1)])

        all_piece_copies(place, pieces, ((wout, 1280, 384, 1),), sems.at[pl.ds(4, 1)])
        wait_whole(wvec, sems.at[3])
        vec_ref[...] = flat(wvec[...]).astype(F32).T[:16]

    x = x_ref[...]
    for n in range(3):

        @pl.when(step == 0)
        def _():
            wait_whole(wqkv.at[:, :, :, :, pl.ds(n * WIDTH, WIDTH)], sems.at[n])

        part = dot(x, flat(wqkv[:, :, :, :, n * WIDTH : (n + 1) * WIDTH]))
        if n != 1:
            part = part + vec_ref[n // 2 : n // 2 + 1, :]
        qkv_ref[:, n * WIDTH : (n + 1) * WIDTH] = part.astype(BF16)
    low = pair_masks()
    for s in range(BLOCK // 128):
        rows = slice(128 * s, 128 * s + 128)
        for h in range(HEADS // 2):
            cols = slice(128 * h, 128 * h + 128)
            query = both_heads(qkv_ref[rows, 128 * h : 128 * h + 128] * BF16(0.125), low)
            keyed = qkv_ref[rows, WIDTH + 128 * h : WIDTH + 128 * h + 128]
            valued = qkv_ref[rows, 2 * WIDTH + 128 * h : 2 * WIDTH + 128 * h + 128]
            scores = dot(keyed, query, NT)
            weight = jnp.exp(scores - jnp.max(scores, axis=0, keepdims=True))
            probs = (weight * (1.0 / jnp.sum(weight, axis=0, keepdims=True))).astype(BF16)
            probs_ref[s, h] = probs
            heads_ref[rows, cols] = dot(upright(probs), both_heads(valued, low), TN).astype(BF16)

    @pl.when(step == 0)
    def _():
        wait_whole(wout, sems.at[4])
        pltpu.make_async_copy(wout, wout_hbm, sems.at[5]).start()

    attn = dot(heads_ref[...], flat(wout[...])) + vec_ref[2:3, :]
    norm, scale = normalize(x.astype(F32) + attn)
    norm_ref[...] = norm
    scale_ref[...] = jnp.broadcast_to(scale, scale_ref.shape)

    @pl.when(step == STEPS - 1)
    def _():
        pltpu.make_async_copy(wout, wout_hbm, sems.at[5]).wait()


def attention_forward(place, rows, pieces):
    return call(
        attention_kernel,
        [place, rows, *pieces],
        [smem_spec(), row_spec(WIDTH)] + [any_spec()] * 8,
        [
            shape((ROWS, 3 * WIDTH)),
            shape((ROWS // 128, HEADS // 2, 128, 256)),
            shape((ROWS, WIDTH)),
            shape((ROWS, WIDTH), F32),
            shape((ROWS, 128), F32),
            shape((16, WIDTH), F32),
            shape(ORDER + (WIDTH,)),
        ],
        [
            row_spec(3 * WIDTH),
            pl.BlockSpec((BLOCK // 128, HEADS // 2, 128, 256), lambda i: (i, 0, 0, 0)),
            row_spec(WIDTH),
            row_spec(WIDTH),
            row_spec(128),
            one_spec(16, WIDTH),
            any_spec(),
        ],
        20,
        grid=(STEPS,),
        scratch=[
            pltpu.VMEM(ORDER + (3 * WIDTH,), BF16),
            pltpu.VMEM(ORDER + (WIDTH,), BF16),
            pltpu.VMEM(ORDER + (128,), BF16),
            pltpu.SemaphoreType.DMA((6,)),
        ],
    )


def wide_scale(ref):
    return jnp.concatenate([ref[...]] * 6, axis=1)


def hidden_of(norm, vec_ref):
    return norm * vec_ref[3:4, :] + vec_ref[4:5, :]


def gelu_parts(upper):
    phi = 0.5 * (1.0 + lax.erf(upper * 0.7071067811865476))
    bell = jnp.exp(-0.5 * upper * upper) * 0.3989422804014327
    return upper * phi, phi + upper * bell


def contrast_kernel(first_ref, received_ref, keep_ref, partner_ref, dfirst_ref, dreceived_ref):
    first = first_ref[...]
    received = received_ref[...].astype(F32)
    logits = lax.dot_general(first, received, NT, precision=lax.Precision.HIGHEST, preferred_element_type=F32)
    logits = logits * logit_scale
    weight = jnp.exp(logits - jnp.max(logits, axis=-1, keepdims=True))
    soft = weight / jnp.sum(weight, axis=-1, keepdims=True)
    column = lax.broadcasted_iota(jnp.int32, (8, 8), 1)
    chosen = jnp.where(column == partner_ref[...], 1.0, 0.0)
    dlogits = (contrast_weight * logit_scale) * keep_ref[...] * (soft - chosen)
    high = lax.Precision.HIGHEST
    dfirst_ref[...] = lax.dot_general(dlogits, received, NN, precision=high, preferred_element_type=F32)
    dreceived_ref[...] = lax.dot_general(
        dlogits, first, TN, precision=high, preferred_element_type=F32
    ).astype(BF16)


def contrast_back(first, received, keep, partner, deps):
    return call(
        contrast_kernel,
        [Loose(first), Loose(received), Loose(keep), Loose(partner)],
        [full_spec()] * 4,
        [loose((8, WIDTH), F32), loose((8, WIDTH))],
        [full_spec()] * 2,
        4,
        deps=deps,
    )


CHUNK = 512
CHUNKS = INNER // CHUNK


def chunk(n):
    return slice(n * CHUNK, (n + 1) * CHUNK)


def feed_forward_rows(hidden, vec_ref, b_in_ref, size, win_part, wdown_part, put):
    hidden_low = hidden.astype(BF16)
    down, active = hidden + vec_ref[5:6, :], None
    after = dot(hidden_low, win_part(0))
    for n in range(INNER // size):
        upper = after + b_in_ref[:, n * size : (n + 1) * size]
        if (n + 1) * size < INNER:
            after = dot(hidden_low, win_part(n + 1))
        if n > 0:
            down = down + dot(active, wdown_part(n - 1))
        active, slope = gelu_parts(upper)
        active = active.astype(BF16)
        put(slice(n * size, (n + 1) * size), active, slope.astype(BF16))
    down = down + dot(active, wdown_part(INNER // size - 1))
    return normalize(down)


def put_norm(first_span, count, norm, scale, vec_ref, norm_two_ref, scale_ref, mixed_ref):
    norm_two_ref[...] = norm.astype(BF16)
    scale_ref[...] = jnp.broadcast_to(scale, scale_ref.shape)
    final = norm * vec_ref[6:7, :] + vec_ref[7:8, :]
    for s in range(norm.shape[0] // 128):
        rows = slice(128 * s, 128 * s + 128)
        live = jnp.where(first_span + s < count[0], 1.0, 0.0)
        mixed_ref[rows, :] = (final[rows] * live).astype(BF16)


def feed_forward_first_kernel(place, count, norm_ref, norm_hbm, vec_ref, b_in_ref, keep_ref, *refs):
    pieces = refs[:8]
    first_ref, sent_ref, win, wdown, hidden_ref, active_ref, slope_ref, norm_two_ref, scale_ref, mixed_ref = refs[8:18]
    tops, sems, tops_sem = refs[18:]
    for s in range(8):
        pltpu.make_async_copy(norm_hbm.at[pl.ds(128 * s, 8)], tops.at[pl.ds(8 * s, 8)], tops_sem).start()
    for core in range(2):

        @pl.when(place[0] == core)
        def _(core=core):
            for n in range(4):
                half, first = n // 2, 768 * (n % 2)
                mine = pieces[:4] if half == core else pieces[4:]
                piece_copies(place, core, half, mine, [(win, WIDTH * n, first, WIDTH, 1)], sems.at[pl.ds(n, 1)])

    all_piece_copies(place, pieces, ((wdown, 1536, 384, 4),), sems.at[pl.ds(4, 1)])
    wait_whole(tops, tops_sem)
    top = hidden_of(jnp.concatenate([tops[8 * s : 8 * s + 1, :] for s in range(8)], axis=0), vec_ref)
    hidden = hidden_of(norm_ref[...], vec_ref)
    hidden_ref[:TALL, :] = hidden.astype(BF16)
    hidden = jnp.concatenate([hidden, top, jnp.zeros_like(top)], axis=0)

    def win_part(n):
        wait_whole(win.at[:, :, :, :, pl.ds(n * WIDTH, WIDTH)], sems.at[n])
        return flat(win[:, :, :, :, n * WIDTH : (n + 1) * WIDTH])

    def wdown_part(n):
        if n == 0:
            wait_whole(wdown, sems.at[4])
        return flat(wdown[n // 2, 2 * (n % 2) : 2 * (n % 2) + 2])

    def put(cols, active, slope):
        active_ref[:TALL, cols] = active[:TALL]
        slope_ref[:TALL, cols] = slope[:TALL]

    norm, scale = feed_forward_rows(hidden, vec_ref, b_in_ref, WIDTH, win_part, wdown_part, put)
    put_norm(0, count, norm[:TALL], scale[:TALL], vec_ref, norm_two_ref, scale_ref, mixed_ref)
    final = norm[TALL : TALL + 8] * vec_ref[6:7, :] + vec_ref[7:8, :]
    first_ref[...] = final
    sent_ref[...] = (final.astype(BF16).astype(F32) * keep_ref[...]).astype(BF16)


def feed_forward_shapes():
    return [
        near((ROWS, WIDTH)),
        near((ROWS, INNER)),
        near((ROWS, INNER)),
        shape((ROWS, WIDTH)),
        shape((ROWS, 128), F32),
        shape((ROWS, WIDTH)),
    ]


def feed_forward_first(place, count, norm, vec, b_in, keep, pieces):
    def rows(width):
        return pl.BlockSpec((TALL, width), lambda i: (0, 0))

    return call(
        feed_forward_first_kernel,
        [place, count, norm, norm, vec, b_in, keep, *pieces],
        [smem_spec(), smem_spec(), rows(WIDTH), any_spec()] + [full_spec()] * 3 + [any_spec()] * 8,
        [
            shape((8, WIDTH), F32),
            loose((8, WIDTH)),
            near(ORDER + (INNER,)),
            near((2, 4, 4, 4, HALF_UNIT, WIDTH)),
        ]
        + feed_forward_shapes(),
        [full_spec()] * 7 + [rows(WIDTH), rows(128), rows(WIDTH)],
        24,
        grid=(1,),
        scratch=[
            pltpu.VMEM((64, WIDTH), F32),
            pltpu.SemaphoreType.DMA((5,)),
            pltpu.SemaphoreType.DMA,
        ],
    )


def feed_forward_kernel(index, count, norm_ref, vec_ref, b_in_ref, win, wdown, *refs):
    hidden_ref, active_ref, slope_ref, norm_two_ref, scale_ref, mixed_ref = refs[-6:]
    here = slice(index * BLOCK, (index + 1) * BLOCK)
    hidden = hidden_of(norm_ref[...], vec_ref)
    hidden_ref[here, :] = hidden.astype(BF16)

    def put(cols, active, slope):
        active_ref[here, cols] = active
        slope_ref[here, cols] = slope

    norm, scale = feed_forward_rows(
        hidden, vec_ref, b_in_ref, CHUNK, lambda n: win[:, chunk(n)], lambda n: wdown[chunk(n), :], put
    )
    put_norm(index * (BLOCK // 128), count, norm, scale, vec_ref, norm_two_ref, scale_ref, mixed_ref)


def feed_forward(index, count, norm, vec, b_in, win, wdown, so_far, deps=()):
    def rows(width):
        return pl.BlockSpec((BLOCK, width), lambda i: (index, 0))

    return call(
        functools.partial(feed_forward_kernel, index),
        [count, norm, vec, b_in, Near(win), Near(wdown)] + [Near(v) if n < 3 else v for n, v in enumerate(so_far)],
        [smem_spec(), rows(WIDTH)] + [full_spec()] * 7 + [any_spec()] * 3,
        feed_forward_shapes(),
        [full_spec()] * 3 + [rows(WIDTH), rows(128), rows(WIDTH)],
        20,
        grid=(1,),
        input_output_aliases={6 + n: n for n in range(6)},
        deps=deps,
    )


def feed_forward_back_kernel(
    count, cot_ref, dfirst_ref, back_ref, keep_ref, norm_ref, scale_ref, vec_ref, slope_ref, wdown, dres_ref, ddown_ref, dupper_ref, sums_ref, db_in_ref
):
    step = pl.program_id(0)
    dfirst = dfirst_ref[...] + back_ref[...].astype(F32) * keep_ref[...]
    slot = lax.broadcasted_iota(jnp.int32, (8, 1), 0)
    blocks = TALL // BLOCK

    def here(b):
        return pl.ds(pl.multiple_of(step * TALL + b * BLOCK, BLOCK), BLOCK)

    def norm_back(b):
        parts = []
        for s in range(BLOCK // 128):
            row = b * BLOCK + 128 * s
            span = step * (TALL // 128) + b * (BLOCK // 128) + s
            live = jnp.where(span < count[0], 1.0, 0.0)
            mine = jnp.sum(jnp.where(slot == span, dfirst, 0.0), axis=0, keepdims=True)
            cot = cot_ref[row : row + 128, :].astype(F32) * live
            top = cot[:8] + jnp.where(slot == 0, mine, 0.0)
            parts += [top, cot[8:]]
        dfinal = jnp.concatenate(parts, axis=0)
        rows = slice(b * BLOCK, (b + 1) * BLOCK)
        norm = norm_ref[rows, :].astype(F32)
        scale = jnp.concatenate([scale_ref[rows, :]] * 6, axis=1)
        dres = normalize_back(dfinal * vec_ref[6:7, :], norm, scale)
        dres_ref[here(b), :] = dres
        ddown = dres.astype(BF16)
        ddown_ref[here(b), :] = ddown
        return ddown, [column_sum(dfinal * norm), column_sum(dfinal), column_sum(dres)]

    jobs = [(b, n) for b in range(blocks) for n in range(CHUNKS)]
    ready, sums, sums_in = norm_back(0), [], [[] for _ in range(blocks)]
    sums.append(ready[1])
    ddown = ready[0]
    after = dot(ddown, wdown[chunk(0), :], NT)
    for k, (b, n) in enumerate(jobs):
        dactive = after
        if n == 0 and b + 1 < blocks:
            ready = norm_back(b + 1)
            sums.append(ready[1])
        if k + 1 < len(jobs):
            if n + 1 == CHUNKS:
                ddown = ready[0]
            after = dot(ddown, wdown[chunk(jobs[k + 1][1]), :], NT)
        dupper = dactive * slope_ref[here(b), chunk(n)].astype(F32)
        dupper_ref[here(b), chunk(n)] = dupper.astype(BF16)
        sums_in[b].append(column_sum(dupper))
    add_rows(sums_ref, step, *[sum(group) for group in zip(*sums)])
    add_rows(db_in_ref, step, sum(jnp.concatenate(parts, axis=1) for parts in sums_in))


def feed_forward_back(count, cotangent, dfirst, back, keep, norm, scale, vec, slope, wdown):
    return call(
        feed_forward_back_kernel,
        [count, cotangent, Loose(dfirst), Loose(back), Loose(keep), norm, scale, vec, Near(slope), Near(wdown)],
        [smem_spec(), tall_spec(WIDTH), full_spec(), full_spec(), full_spec(), tall_spec(WIDTH), tall_spec(128)]
        + [full_spec()] * 3,
        [
            near((ROWS, WIDTH), F32),
            near((ROWS, WIDTH)),
            near((ROWS, INNER)),
            shape((24, WIDTH), F32),
            shape((8, INNER), F32),
        ],
        [full_spec(), full_spec(), full_spec(), one_spec(24, WIDTH), one_spec(8, INNER)],
        20,
        grid=(ROWS // TALL,),
        input_output_aliases={8: 2},
    )


def hidden_back_kernel(
    dres_ref, dupper_ref, norm_ref, scale_ref, vec_ref, win, wout, dres_one_ref, dattn_ref, dheads_ref, sums_ref
):
    step = pl.program_id(0)
    count = TALL // BLOCK

    def here(n):
        return pl.ds(pl.multiple_of(step * TALL + n * BLOCK, BLOCK), BLOCK)

    def product(n):
        return dot(dupper_ref[here(n), :], win[...], NT)

    after, sums = product(0), []

    for n in range(count):
        rows = slice(n * BLOCK, (n + 1) * BLOCK)
        dhidden = dres_ref[here(n), :] + after
        if n + 1 < count:
            after = product(n + 1)
        norm = norm_ref[rows, :]
        scale = jnp.concatenate([scale_ref[rows, :]] * 6, axis=1)
        dres = normalize_back(dhidden * vec_ref[3:4, :], norm, scale)
        dres_one_ref[rows, :] = dres
        dattn = dres.astype(BF16)
        dattn_ref[rows, :] = dattn
        dheads_ref[rows, :] = dot(dattn, flat(wout[...]), NT).astype(BF16)
        sums.append([column_sum(dhidden * norm), column_sum(dhidden), column_sum(dres)])
    add_rows(sums_ref, step, *[sum(group) for group in zip(*sums)])


def hidden_back(dres, dupper, norm, scale, vec, win, wout, deps):
    return call(
        hidden_back_kernel,
        [Near(dres), Near(dupper), norm, scale, vec, Near(win), wout],
        [full_spec(), full_spec(), tall_spec(WIDTH), tall_spec(128)] + [full_spec()] * 3,
        [shape((ROWS, WIDTH), F32), shape((ROWS, WIDTH)), shape((ROWS, WIDTH)), shape((24, WIDTH), F32)],
        [tall_spec(WIDTH), tall_spec(WIDTH), tall_spec(WIDTH), one_spec(24, WIDTH)],
        22,
        grid=(ROWS // TALL,),
        deps=deps,
    )


def attention_back_kernel(qkv_ref, probs_ref, dheads_ref, dqkv_ref, near_ref, sums_ref):
    step = pl.program_id(0)
    low = pair_masks()
    for s in range(BLOCK // 128):
        rows = slice(128 * s, 128 * s + 128)
        for h in range(HEADS // 2):
            query = both_heads(qkv_ref[rows, 128 * h : 128 * h + 128] * BF16(0.125), low)
            keyed = qkv_ref[rows, WIDTH + 128 * h : WIDTH + 128 * h + 128]
            valued = qkv_ref[rows, 2 * WIDTH + 128 * h : 2 * WIDTH + 128 * h + 128]
            dheads = both_heads(dheads_ref[rows, 128 * h : 128 * h + 128], low)
            probs_low = probs_ref[s, h]
            probs = probs_low.astype(F32)
            dprobs = dot(valued, dheads, NT)
            inner = jnp.sum(probs * dprobs, axis=0, keepdims=True)
            dscores = (probs * (dprobs - inner)).astype(BF16)
            dquery = dot(upright(dscores), both_heads(keyed * BF16(0.125), low), TN)
            dqkv_ref[rows, 128 * h : 128 * h + 128] = dquery.astype(BF16)
            dqkv_ref[rows, WIDTH + 128 * h : WIDTH + 128 * h + 128] = dot(dscores, query).astype(BF16)
            dqkv_ref[rows, 2 * WIDTH + 128 * h : 2 * WIDTH + 128 * h + 128] = dot(probs_low, dheads).astype(BF16)
    near_ref[block_rows(step, BLOCK), :] = dqkv_ref[...]
    add_rows(
        sums_ref,
        step,
        column_sum(dqkv_ref[:, :WIDTH].astype(F32)),
        column_sum(dqkv_ref[:, 2 * WIDTH :].astype(F32)),
    )


def attention_back(qkv, probs, dheads, deps):
    return call(
        attention_back_kernel,
        [qkv, probs, dheads],
        [
            row_spec(3 * WIDTH),
            pl.BlockSpec((BLOCK // 128, HEADS // 2, 128, 256), lambda i: (i, 0, 0, 0)),
            row_spec(WIDTH),
        ],
        [shape((ROWS, 3 * WIDTH)), near((ROWS, 3 * WIDTH)), shape((16, WIDTH), F32)],
        [row_spec(3 * WIDTH), full_spec(), one_spec(16, WIDTH)],
        16,
        grid=(STEPS,),
        deps=deps,
    )


def tokens_back_kernel(place, dres_ref, dqkv_ref, *refs):
    pieces, (out_ref, wqkv, sems) = refs[:8], refs[8:]

    @pl.when(pl.program_id(0) == 0)
    def _():
        all_piece_copies(place, pieces, ((wqkv, 0, 1152, 1),), sems)
        wait_whole(wqkv, sems.at[0])

    out_ref[...] = (dres_ref[...] + dot(dqkv_ref[...], flat(wqkv[...]), NT)).astype(BF16)


def tokens_back(place, dres, dqkv, pieces, deps):
    return call(
        tokens_back_kernel,
        [place, dres, dqkv, *pieces],
        [smem_spec(), row_spec(WIDTH), row_spec(3 * WIDTH)] + [any_spec()] * 8,
        shape((ROWS, WIDTH)),
        row_spec(WIDTH),
        14,
        grid=(STEPS,),
        scratch=[pltpu.VMEM(ORDER + (3 * WIDTH,), BF16), pltpu.SemaphoreType.DMA((1,))],
        deps=deps,
    )


def put_unit(place, both, half, unit, p, cols, value):
    side = place[0] if half == 0 else 1 - place[0]
    both[side, place[1 + 16 * half + unit], p, :, cols] = value.astype(BF16)


def put_units(place, both, half, cols, value):
    for p in range(2):
        for unit in range(16):
            row = 384 * p + HALF_UNIT * unit
            put_unit(place, both, half, unit, p, cols, value[row : row + HALF_UNIT])


def write_half(place, both, half, outs, sem, cols):
    for core in range(2):

        @pl.when(place[0] == core)
        def _(side=half ^ core):
            pltpu.make_async_copy(both.at[side, :, :, :, cols], outs[side].at[:, :, :, cols], sem).start()


def run_ahead(jobs):
    after = jobs[0][0]()
    for n, (_, use) in enumerate(jobs):
        value = after
        if n + 1 < len(jobs):
            after = jobs[n + 1][0]()
        use(value)


def layer_grads_kernel(place, active_ref, ddown_ref, hidden_ref, dupper_ref, own, theirs, both, sem):
    outs = (own, theirs)

    def in_job(h, n):
        cols = slice(768 * n, 768 * n + 768)

        def product():
            first = 1536 * h + 768 * n
            return dot(hidden_ref[...], dupper_ref[:, first : first + 768], TN)

        return product, lambda value: put_units(place, both, h, cols, value)

    def down_job(n):
        def product():
            return dot(active_ref[:, WIDTH * n : WIDTH * n + WIDTH], ddown_ref[...], TN)

        def use(value):
            for h in range(2):
                for i in range(2):
                    for y in range(4):
                        for j in range(4):
                            row = 384 * i + 96 * y + HALF_UNIT * j
                            part = value[row : row + HALF_UNIT, 384 * h : 384 * h + 384]
                            cols = slice(1536 + 384 * j, 1536 + 384 * j + 384)
                            put_unit(place, both, h, 4 * (2 * (n % 2) + i) + y, n // 2, cols, part)

        return product, use

    def write(p, cols):
        for side in (1, 0):
            pltpu.make_async_copy(both.at[side, :, p, :, cols], outs[side].at[:, p, :, cols], sem).start()

    run_ahead([in_job(h, n) for h in range(2) for n in range(2)])
    write(0, slice(0, 1536))
    write(1, slice(0, 1536))
    run_ahead([down_job(n) for n in range(2)])
    write(0, slice(1536, 3072))
    run_ahead([down_job(n) for n in range(2, 4)])
    write(1, slice(1536, 3072))
    wait_whole(both, sem)


def layer_grads(place, active, ddown, hidden_low, dupper):
    return call(
        layer_grads_kernel,
        [place, Near(active), Near(ddown), Near(hidden_low), Near(dupper)],
        [smem_spec()] + [full_spec()] * 4,
        [shape((16, 2, HALF_UNIT, 3072)), loose((16, 2, HALF_UNIT, 3072))],
        [any_spec(), any_spec()],
        20,
        scratch=[pltpu.VMEM((2, 16, 2, HALF_UNIT, 3072), BF16), pltpu.SemaphoreType.DMA],
    )


def every_fourth(line, j):
    blocks = jnp.concatenate([line[:, 512 * n : 512 * n + 512] for n in range(6)] + [jnp.zeros((2, 512), F32)], axis=0)
    row = lax.broadcasted_iota(jnp.int32, (512, 128), 0)
    lane = lax.broadcasted_iota(jnp.int32, (512, 128), 1)
    pick = jnp.where(row == 4 * lane + j, 1.0, 0.0)
    picked = lax.dot_general(blocks, pick, NN, precision=lax.Precision.HIGHEST, preferred_element_type=F32)
    return jnp.concatenate([picked[n : n + 1] for n in range(6)], axis=1)


def attention_grads_kernel(
    place, x_hbm, dqkv_ref, heads_hbm, dattn_hbm, sums_qkv, sums_one, sums_two, db_in, own, theirs, both, x, heads, dattn, sems
):
    pairs = ((x_hbm, x), (heads_hbm, heads), (dattn_hbm, dattn))
    loads = [pltpu.make_async_copy(far, here, sems.at[n]) for n, (far, here) in enumerate(pairs)]
    for load in loads:
        load.start()
    outs, done = (own, theirs), sems.at[3]

    def total(ref, n):
        return jnp.sum(ref[8 * n : 8 * n + 8, :], axis=0, keepdims=True)

    rows = [total(sums_qkv, 0), total(sums_qkv, 1), total(sums_one, 2), total(sums_one, 0), total(sums_one, 1)]
    rows += [total(sums_two, 2), total(sums_two, 0), total(sums_two, 1)]
    rows += [every_fourth(total(db_in, 0), j) for j in range(4)] + [jnp.zeros((116, WIDTH), F32)]
    wide = jnp.concatenate(rows, axis=0).T
    put_units(place, both, 0, slice(1152, 1280), wide)
    put_units(place, both, 1, slice(1152, 1280), jnp.zeros_like(wide))
    loads[0].wait()

    def job(n):
        def product():
            return dot(x[...], dqkv_ref[:, 768 * n : 768 * n + 768], TN)

        def use(value):
            for m in range(2):
                first = 768 * n + 384 * m
                h, at = first // 1152, first % 1152
                put_units(place, both, h, slice(at, at + 384), value[:, 384 * m : 384 * m + 384])
                write_half(place, both, h, outs, done, slice(at, at + 384))

        return product, use

    def out_product():
        loads[1].wait()
        loads[2].wait()
        return dot(heads[...], dattn[...], TN)

    def out_use(value):
        for h in range(2):
            put_units(place, both, h, slice(1280, FIRST), value[:, 384 * h : 384 * h + 384])
            write_half(place, both, h, outs, done, slice(1152, FIRST))

    run_ahead([job(n) for n in range(3)] + [(out_product, out_use)])
    wait_whole(both, done)


def attention_grads(place, rows, dqkv, heads, dattn, sums, deps):
    sums_qkv, sums_one, sums_two, db_in = sums
    return call(
        attention_grads_kernel,
        [place, rows, Near(dqkv), heads, dattn, sums_qkv, sums_one, sums_two, db_in],
        [smem_spec(), any_spec(), full_spec(), any_spec(), any_spec()] + [full_spec()] * 4,
        [shape((16, 2, HALF_UNIT, FIRST)), loose((16, 2, HALF_UNIT, FIRST))],
        [any_spec(), any_spec()],
        20,
        scratch=[pltpu.VMEM((2, 16, 2, HALF_UNIT, FIRST), BF16)]
        + [pltpu.VMEM((ROWS, WIDTH), BF16)] * 3
        + [pltpu.SemaphoreType.DMA((4,))],
        deps=deps,
    )


def add_kernel(own_hbm, recv_hbm, *refs):
    outs, (own, recv, sems) = refs[:-3], refs[-3:]
    loads = []
    for r in range(4):
        part = pl.ds(4 * r, 4)
        pair = [
            pltpu.make_async_copy(own_hbm.at[part], own.at[part], sems.at[2 * r]),
            pltpu.make_async_copy(recv_hbm.at[part], recv.at[part], sems.at[2 * r + 1]),
        ]
        for load in pair:
            load.start()
        loads.append(pair)
    for r in range(4):
        for load in loads[r]:
            load.wait()
        for k in range(4):
            outs[r][k] = (own[4 * r + k].astype(F32) + recv[4 * r + k].astype(F32)).astype(BF16)


def add_theirs(own, recv, deps):
    width = recv.shape[3]
    buffer = pltpu.VMEM((16, 2, HALF_UNIT, width), BF16)
    return call(
        add_kernel,
        [own, Loose(recv)],
        [any_spec()] * 2,
        [loose((4, 2, HALF_UNIT, width))] * 4,
        [full_spec()] * 4,
        18,
        scratch=[buffer, buffer, pltpu.SemaphoreType.DMA((8,))],
        deps=deps,
    )


def pack_kernel(wqkv_hbm, wout_hbm, win_hbm, wdown_hbm, vec, mask, pick, out_ref, wqkv, wout, win, wdown, sems):
    loads = [
        pltpu.make_async_copy(far, here, sems.at[n])
        for n, (far, here) in enumerate(((wqkv_hbm, wqkv), (wout_hbm, wout), (win_hbm, win), (wdown_hbm, wdown)))
    ]
    for load in loads:
        load.start()
    column = dot((vec[...] * mask[...]).astype(BF16), pick[...])[:6].astype(BF16)
    for load in loads:
        load.wait()
    for k in range(8):
        h = k % 2
        out_ref[k, :, :1152] = wqkv[:, 1152 * h : 1152 * h + 1152]
        out_ref[k, :, 1152:1280] = column
        out_ref[k, :, 1280:FIRST] = wout[:, 384 * h : 384 * h + 384]
        out_ref[k, :, FIRST : FIRST + 1536] = win[:, 1536 * h : 1536 * h + 1536]
        for j in range(4):
            first = FIRST + 1536 + 384 * j
            out_ref[k, :, first : first + 384] = wdown[6 * j : 6 * j + 6, 384 * h : 384 * h + 384]


def pack(wqkv, wout, win, wdown, vectors, b_in):
    vec = jnp.zeros((128,), F32)
    for n, v in enumerate(list(vectors) + [b_in]):
        vec = vec + lax.pad(v.astype(F32), jnp.zeros((), F32), [(6 * n, 128 - 6 * n - v.shape[0], 0)])
    j = np.arange(128)
    r = np.where(j < 48, j % 6, np.where(j < 72, (j - 48) // 4, -1))
    i = np.where(j < 48, j // 6, np.where(j < 72, 8 + (j - 48) % 4, -1))
    mask = (r[None, :] == np.arange(8)[:, None]).astype(np.float32)
    pick = (i[:, None] == np.arange(128)[None, :]).astype(ml_dtypes.bfloat16)
    return call(
        pack_kernel,
        [wqkv, wout, win, wdown, vec.reshape(1, 128), mask, pick],
        [any_spec()] * 4 + [full_spec()] * 3,
        loose((8, 6, FIRST + 3072)),
        full_spec(),
        6,
        scratch=[
            pltpu.VMEM((6, 2304), BF16),
            pltpu.VMEM((6, 768), BF16),
            pltpu.VMEM((6, 3072), BF16),
            pltpu.VMEM((24, 768), BF16),
            pltpu.SemaphoreType.DMA((4,)),
        ],
    )


def stack_kernel(cuts, place, *refs):
    parts, outs = refs[:4], refs[4:]
    for q in range(4):
        slot = place[33 + (4 - q) % 4]
        for n, (first, width) in enumerate(cuts):
            outs[n][slot] = parts[q][:, :, first : first + width]


def stack(place, parts, cuts):
    return call(
        functools.partial(stack_kernel, cuts),
        [place, *[Loose(p) for p in parts]],
        [smem_spec()] + [full_spec()] * 4,
        [loose((4, 2, HALF_UNIT, w)) for _, w in cuts],
        [full_spec()] * len(cuts),
        8,
    )


def gate_kernel(*refs):
    pass


def gate(values, deps):
    return call(
        gate_kernel,
        [Loose(v) for v in values],
        [any_spec()] * len(values),
        [loose(v.shape, v.dtype) for v in values],
        [any_spec()] * len(values),
        2,
        deps=deps,
        input_output_aliases={n: n for n in range(len(values))},
    )


def sum_kernel(sets, more, *refs):
    ins, rest, outs = refs[: 4 * sets], refs[4 * sets : 4 * sets + more], refs[4 * sets + more :]
    for r in range(4):
        first = 0
        for g in range(sets):
            part = ins[4 * g : 4 * g + 4]
            width = part[0].shape[3]
            total = part[0][r].astype(F32)
            for p in part[1:]:
                total = total + p[r].astype(F32)
            outs[r][:, :, first : first + width] = total.astype(BF16)
            first += width
        if more:
            outs[r][:, :, first:] = rest[r][...]


def sum_blocks(parts, more=(), deps=(), weight=0):
    width = parts[0].shape[3] + (more[0].shape[2] if more else 0)
    args = [Loose(p) for p in list(parts) + list(more)]
    return call(
        functools.partial(sum_kernel, 1, len(more)),
        args,
        [full_spec()] * len(args),
        [loose((2, HALF_UNIT, width))] * 4,
        [full_spec()] * 4,
        14,
        deps=deps,
        weight=weight,
    )


def finish_kernel(in_ref, dqkv, dout, din, ddown, *vectors):
    for h in range(2):
        total = in_ref[h].astype(F32)
        for k in range(h + 2, 8, 2):
            total = total + in_ref[k].astype(F32)
        dqkv[:, 1152 * h : 1152 * h + 1152] = total[:, :1152]
        dout[:, 384 * h : 384 * h + 384] = total[:, 1280:FIRST]
        din[:, 1536 * h : 1536 * h + 1536] = total[:, FIRST : FIRST + 1536]
        for j in range(4):
            first = FIRST + 1536 + 384 * j
            ddown[6 * j : 6 * j + 6, 384 * h : 384 * h + 384] = total[:, first : first + 384]
        if h == 0:
            wide = jnp.concatenate([total[:, 1152:1280], jnp.zeros((122, 128), F32)], axis=0).T
    for n in range(8):
        vectors[n][...] = wide[n, :6]
    row = lax.broadcasted_iota(jnp.int32, (128, 128), 0)
    lane = lax.broadcasted_iota(jnp.int32, (128, 128), 1)
    b_in = jnp.zeros((8, 128), F32)
    for j in range(4):
        spread = jnp.where(lane == 4 * row + j, 1.0, 0.0)
        line = jnp.concatenate([wide[8 + j : 9 + j]] * 8, axis=0)
        b_in = b_in + lax.dot_general(line, spread, NN, precision=lax.Precision.HIGHEST, preferred_element_type=F32)
    vectors[8][...] = b_in[0, :24]


def finish(blocks):
    return call(
        finish_kernel,
        [Loose(blocks)],
        [full_spec()],
        [shape(d, F32) for d in ((6, 2304), (6, 768), (6, 3072), (24, 768)) + ((6,),) * 8 + ((24,),)],
        [full_spec()] * 13,
        6,
    )


def total_kernel(*refs):
    total = refs[0][...].astype(F32)
    for part in refs[1:4]:
        total = total + part[...].astype(F32)
    refs[4][...] = total.astype(BF16)


def total_of(parts, deps=()):
    return call(
        total_kernel,
        [Loose(p) for p in parts],
        [full_spec()] * 4,
        loose(parts[0].shape),
        full_spec(),
        6,
        deps=deps,
    )


def per_device(
    tokens,
    cotangent,
    span_counts,
    single_flags,
    partner_slots,
    w_qkv,
    b_query,
    b_value,
    w_out,
    b_out,
    gain_attn,
    shift_attn,
    w_in,
    b_in,
    w_down,
    b_down,
    gain_ffn,
    shift_ffn,
):
    place = my_place()
    packed = pack(
        w_qkv, w_out, w_in, w_down, [b_query, b_value, b_out, gain_attn, shift_attn, b_down, gain_ffn, shift_ffn], b_in
    )
    rows48 = exchange_octet(packed)
    straight = rows48[:, :, : FIRST + 1536].reshape(2, HALF_UNIT, FIRST + 1536)
    turned = rows48[:, :, FIRST + 1536 :].reshape(2, 4, 6, 4, 384).transpose(0, 3, 2, 1, 4).reshape(2, HALF_UNIT, 1536)
    unit = jnp.concatenate([straight, turned], axis=2)
    one_early, two_early = stack(place, gather(unit, 0), ((0, FIRST), (FIRST, 3072)))
    one_late = gather(one_early, 1)
    one_pieces = one_late + [to_core(piece) for piece in one_late]
    two_late = gather(two_early, 1)

    count = span_counts[0]
    live = (jnp.arange(8, dtype=jnp.int32) < count).astype(F32)
    keep = (live * (1.0 - single_flags[0].astype(F32)))[:, None]
    partner = partner_slots[0][:, None]
    rows = tokens.reshape(ROWS, WIDTH)

    qkv, probs, heads, norm_one, scale_one, vec, wout = attention_forward(place, rows, one_pieces)
    full_b_in = vec[8:12].T.reshape(1, INNER)
    two_late = [two_late[0], *gate(two_late[1:], [vec])]
    first, sent, win, wdown, *so_far = feed_forward_first(
        place, count, norm_one, vec, full_b_in, keep, two_late + [to_core(piece) for piece in two_late]
    )
    win, wdown = win.reshape(WIDTH, INNER), wdown.reshape(INNER, WIDTH)
    partners = [(d, d ^ 64) for d in range(128)]
    received = send(sent, partners)
    so_far = feed_forward(2, count, norm_one, vec, full_b_in, win, wdown, so_far)
    dfirst, dreceived = contrast_back(first, received, keep, partner, [so_far[4]])
    returned = send(dreceived, partners)
    hidden_low, active, slope, norm_two, scale_two, mixed = feed_forward(
        3, count, norm_one, vec, full_b_in, win, wdown, so_far, [Loose(dreceived)]
    )
    dres_two, ddown, dupper, sums_two, db_in = feed_forward_back(
        count, cotangent.reshape(ROWS, WIDTH), dfirst, returned, keep, norm_two, scale_two, vec, slope, wdown
    )
    two_mine, two_out = layer_grads(place, active, ddown, hidden_low, dupper)
    two_recv = to_core(two_out)
    dres_one, dattn, dheads, sums_one = hidden_back(
        dres_two, dupper, norm_one, scale_one, vec, win, wout, [Loose(two_out)]
    )
    two_own = add_theirs(two_mine, two_recv, [sums_one])
    two_parts = scatter_sends(two_own, 1)
    dqkv, dqkv_near, sums_qkv = attention_back(qkv, probs, dheads, [Loose(two_own[0])])
    sums = (sums_qkv, sums_one, sums_two, db_in)
    one_mine, one_out = attention_grads(place, rows, dqkv_near, heads, dattn, sums, [])
    one_recv = to_core(one_out)
    late = sum_blocks(two_parts, deps=[one_mine], weight=3e10)
    one_own = add_theirs(one_mine, one_recv, [Loose(late[0])])
    one_parts = scatter_sends(one_own, 1)
    grad_tokens = tokens_back(place, dres_one, dqkv, one_pieces, [Loose(one_own[0])])
    total = total_of(scatter_sends(sum_blocks(one_parts, late, deps=[grad_tokens]), 0))
    straight = total[:, :, : FIRST + 1536].reshape(8, 6, FIRST + 1536)
    turned = total[:, :, FIRST + 1536 :].reshape(2, 4, 6, 4, 384).transpose(0, 3, 2, 1, 4).reshape(8, 6, 1536)
    back = jnp.concatenate([straight, turned], axis=2)
    dqkv_own, dout_own, din_own, ddown_own, *vectors = finish(exchange_octet(back))
    return (
        mixed.reshape(tokens.shape),
        grad_tokens.reshape(tokens.shape),
        dqkv_own,
        vectors[0],
        vectors[1],
        dout_own,
        vectors[2],
        vectors[3],
        vectors[4],
        din_own,
        vectors[8],
        ddown_own,
        vectors[5],
        vectors[6],
        vectors[7],
    )


def solution(mesh):
    return jax.shard_map(
        per_device,
        mesh=mesh,
        in_specs=(
            P("pair", "dp", None, None),
            P("pair", "dp", None, None),
            P("pair", "dp"),
            P("pair", "dp"),
            P("pair", "dp"),
            P(("pair", "dp"), None),
            P(("pair", "dp")),
            P(("pair", "dp")),
            P(("pair", "dp"), None),
            P(("pair", "dp")),
            P(("pair", "dp")),
            P(("pair", "dp")),
            P(("pair", "dp"), None),
            P(("pair", "dp")),
            P(("pair", "dp"), None),
            P(("pair", "dp")),
            P(("pair", "dp")),
            P(("pair", "dp")),
        ),
        out_specs=(
            P("pair", "dp", None, None),
            P("pair", "dp", None, None),
            P(("pair", "dp"), None),
            P(("pair", "dp")),
            P(("pair", "dp")),
            P(("pair", "dp"), None),
            P(("pair", "dp")),
            P(("pair", "dp")),
            P(("pair", "dp")),
            P(("pair", "dp"), None),
            P(("pair", "dp")),
            P(("pair", "dp"), None),
            P(("pair", "dp")),
            P(("pair", "dp")),
            P(("pair", "dp")),
        ),
        check_vma=False,
    )
```

```python
import functools

import jax
import jax.numpy as jnp
import ml_dtypes
import numpy as np
from jax import lax
from jax.experimental import pallas as pl
from jax.experimental.pallas import tpu as pltpu
from jax.sharding import PartitionSpec as P

HEADS = 12
HEAD_DIM = 64


epsilon = 1e-12
contrast_weight = 8.0
logit_scale = 0.0625


AXES = ("pair", "dp")
HALF_UNIT = 24


def device_index(p, x, y, z, c):
    return (((p * 4 + x) * 4 + y) * 2 + z) * 2 + c


def all_places():
    return [(p, x, y, z, c) for p in range(2) for x in range(4) for y in range(4) for z in range(2) for c in range(2)]


def moved(place, stage, r):
    p, x, y, z, c = place
    if (stage == 0) == (c == 0):
        return (p, x, (y + r) % 4, z, c)
    return (p, (x + r) % 4, y, z, c)


def stage_pairs(stage, r, back=False):
    pairs = [(device_index(*moved(q, stage, r)), device_index(*q)) for q in all_places()]
    return [(t, s) for s, t in pairs] if back else pairs


def core_pairs():
    return [(d, d ^ 1) for d in range(128)]


def octets():
    return [
        [device_index(p, x, y, z, c) for p in range(2) for z in range(2) for c in range(2)]
        for x in range(4)
        for y in range(4)
    ]


def send(value, pairs):
    return lax.ppermute(value, AXES, pairs)


def exchange_octet(value):
    return lax.all_to_all(value, AXES, 0, 0, axis_index_groups=octets(), tiled=True)


def my_place():
    dp = lax.axis_index("dp")
    c, y, x = dp & 1, (dp >> 2) & 3, (dp >> 4) & 3
    i = jnp.arange(16, dtype=jnp.int32)
    far_x, far_y = ((i >> 2) - x) & 3, ((i & 3) - y) & 3
    r = jnp.arange(4, dtype=jnp.int32)
    slots = jnp.where(c == 0, y + r, x + r) & 3
    parts = [c[None], 4 * far_x + far_y, 4 * far_y + far_x, slots, x[None], y[None]]
    return jnp.concatenate(parts).astype(jnp.int32)


WIDE = (1152, 128, 384)
FIRST = sum(WIDE)
SECOND = 3072


def gather(block, stage):
    return [block] + [send(block, stage_pairs(stage, r)) for r in (3, 2, 1)]


def to_core(value):
    return send(value, core_pairs())


def scatter_sends(blocks, stage):
    return [blocks[0]] + [send(blocks[r], stage_pairs(stage, r, True)) for r in (1, 2, 3)]


F32 = jnp.float32
BF16 = jnp.bfloat16
NN = (((1,), (0,)), ((), ()))
NT = (((1,), (1,)), ((), ()))
TN = (((0,), (0,)), ((), ()))
ROWS = 1024
BLOCK = 256
STEPS = ROWS // BLOCK
TALL = 512
WIDTH = 768
INNER = 3072
MIB = 2**20
WEIGHTS = {
    "attention_kernel": 0,
    "feed_forward_first_kernel": 3.75e+08,
    "contrast_kernel": 6.25e+06,
    "feed_forward_kernel": 1.875e+08,
    "feed_forward_back_kernel": 3.125e+08,
    "hidden_back_kernel": 3.75e+08,
    "upper_back_kernel": 3.75e+08,
    "lower_back_kernel": 3.75e+08,
    "attention_back_kernel": 3.125e+08,
    "tokens_back_kernel": 2.5e+08,
    "layer_grads_kernel": 6.25e+08,
    "attention_grads_kernel": 3.125e+08,
    "add_kernel": 1.25e+08,
    "gate_kernel": 0,
    "total_kernel": 3.125e+07,
    "unpack_kernel": 3.125e+07,
    "collect_kernel": 1.25e+08,
    "stack_kernel": 3.125e+07,
    "pack_kernel": 3.125e+07,
    "finish_kernel": 3.125e+07,
    "sum_kernel": 3.125e+07,
}


def dot(left, right, dims=NN):
    return lax.dot_general(left, right, dims, preferred_element_type=F32)


def full_spec():
    return pl.BlockSpec(memory_space=pltpu.VMEM)


def any_spec():
    return pl.BlockSpec(memory_space=pl.ANY)


def smem_spec():
    return pl.BlockSpec(memory_space=pltpu.SMEM)


def row_spec(width, block=BLOCK):
    return pl.BlockSpec((block, width), lambda i: (i, 0))


def tall_spec(width):
    return row_spec(width, TALL)


def one_spec(rows, width):
    return pl.BlockSpec((rows, width), lambda i: (0, 0))


def shape(dims, dtype=BF16):
    return pltpu.HBM(dims, dtype)


def near(dims, dtype=BF16):
    return pltpu.VMEM(dims, dtype)


def loose(dims, dtype=BF16):
    return jax.ShapeDtypeStruct(dims, dtype)


class Near:
    def __init__(self, value):
        self.value = value


class Loose(Near):
    pass


def pinned(value):
    if isinstance(value, Loose):
        return value.value
    if isinstance(value, Near):
        return pltpu.with_memory_space_constraint(value.value, pltpu.VMEM)
    return pltpu.with_memory_space_constraint(value, pltpu.HBM)


def block_rows(step, block=TALL):
    return pl.ds(pl.multiple_of(step * block, block), block)


def limit(mib):
    return pltpu.CompilerParams(vmem_limit_bytes=mib * MIB)


def call(kernel, args, in_specs, out_shape, out_specs, mib, weight=0, grid=None, scratch=(), deps=(), **more):
    n_args, n_deps = len(args), len(deps)

    def body(*refs):
        kernel(*refs[:n_args], *refs[n_args + n_deps :])

    kwargs = dict(more)
    args = [a if spec.memory_space == pltpu.SMEM else pinned(a) for a, spec in zip(args, in_specs)]
    deps = [pinned(a) for a in deps]
    if grid is not None:
        kwargs["grid"] = grid
    return pl.pallas_call(
        body,
        out_shape=out_shape,
        in_specs=list(in_specs) + [any_spec()] * n_deps,
        out_specs=out_specs,
        scratch_shapes=list(scratch),
        cost_estimate=pl.CostEstimate(flops=int(weight or WEIGHTS.get(getattr(kernel, "func", kernel).__name__, 0)), bytes_accessed=0, transcendentals=0),
        name=getattr(kernel, "func", kernel).__name__,
        compiler_params=limit(24),
        **kwargs,
    )(*args, *deps)


def normalize(resid):
    centered = resid - jnp.mean(resid, axis=-1, keepdims=True)
    variance = jnp.mean(centered * centered, axis=-1, keepdims=True)
    scale = lax.rsqrt(variance + epsilon)
    return centered * scale, scale


def normalize_back(grad, norm, scale):
    mean_grad = jnp.mean(grad, axis=-1, keepdims=True)
    mean_both = jnp.mean(grad * norm, axis=-1, keepdims=True)
    return scale * (grad - mean_grad - norm * mean_both)


def column_sum(value):
    return jnp.sum(value.reshape(-1, 8, value.shape[1]), axis=0)


def add_rows(ref, step, *rows):
    total = jnp.concatenate(list(rows), axis=0)

    @pl.when(step == 0)
    def _():
        ref[...] = total

    @pl.when(step > 0)
    def _():
        ref[...] += total


def piece_copies(place, core, half, pieces, targets, sems):
    x, y = place[37], place[38]
    for q in range(4):
        r = (4 - q) % 4
        for n, (ref, at, first, width, blocks) in enumerate(targets):
            for j in range(blocks):
                inner = (j, slice(None), pl.ds(at, width)) if blocks > 1 else (slice(None), pl.ds(at, width))
                for p in range(2):
                    row = (p, (x + r) & 3, slice(None)) if half == 0 else (p, slice(None), (y + r) & 3)
                    pltpu.make_async_copy(
                        pieces[q].at[:, p, :, pl.ds(first + j * width, width)], ref.at[row + inner], sems.at[n]
                    ).start()


def all_piece_copies(place, pieces, targets, sems):
    for core in range(2):

        @pl.when(place[0] == core)
        def _(core=core):
            for half in range(2):
                mine = pieces[:4] if half == core else pieces[4:]
                into = [(ref, half * width, first, width, blocks) for ref, first, width, blocks in targets]
                piece_copies(place, core, half, mine, into, sems)


def flat(value):
    return value.reshape(-1, value.shape[-1])


ORDER = (2, 4, 4, HALF_UNIT)


def wait_whole(ref, sem):
    pltpu.make_async_copy(ref, ref, sem).wait()


def pair_masks():
    lane = lax.broadcasted_iota(jnp.int32, (128, 128), 1)
    return lane < HEAD_DIM


def both_heads(block, low):
    zero = jnp.zeros_like(block)
    return jnp.concatenate([jnp.where(low, block, zero), jnp.where(low, zero, block)], axis=0)


def upright(block):
    return jnp.concatenate([block[:, :128], block[:, 128:]], axis=0)


def attention_kernel(place, x_ref, *refs):
    pieces = refs[:8]
    qkv_ref, probs_ref, heads_ref, norm_ref, scale_ref, vec_ref, wout_hbm = refs[8:15]
    wqkv, wout, wvec, sems = refs[15:]
    step = pl.program_id(0)

    @pl.when(step == 0)
    def _():
        for core in range(2):

            @pl.when(place[0] == core)
            def _(core=core):
                for part in range(3):
                    for half in range(2):
                        first = max(768 * part, 1152 * half)
                        width = min(768 * part + 768, 1152 * half + 1152) - first
                        if width > 0:
                            mine = pieces[:4] if half == core else pieces[4:]
                            target = (wqkv, first, first - 1152 * half, width, 1)
                            piece_copies(place, core, half, mine, [target], sems.at[pl.ds(part, 1)])
                    if part == 0:
                        piece_copies(place, core, core, pieces[:4], [(wvec, 0, 1152, 128, 1)], sems.at[pl.ds(3, 1)])

        all_piece_copies(place, pieces, ((wout, 1280, 384, 1),), sems.at[pl.ds(4, 1)])
        wait_whole(wvec, sems.at[3])
        vec_ref[...] = flat(wvec[...]).astype(F32).T[:16]

    x = x_ref[...]
    for n in range(3):

        @pl.when(step == 0)
        def _():
            wait_whole(wqkv.at[:, :, :, :, pl.ds(n * WIDTH, WIDTH)], sems.at[n])

        part = dot(x, flat(wqkv[:, :, :, :, n * WIDTH : (n + 1) * WIDTH]))
        if n != 1:
            part = part + vec_ref[n // 2 : n // 2 + 1, :]
        qkv_ref[:, n * WIDTH : (n + 1) * WIDTH] = part.astype(BF16)
    low = pair_masks()
    for s in range(BLOCK // 128):
        rows = slice(128 * s, 128 * s + 128)
        for h in range(HEADS // 2):
            cols = slice(128 * h, 128 * h + 128)
            query = both_heads(qkv_ref[rows, 128 * h : 128 * h + 128] * BF16(0.125), low)
            keyed = qkv_ref[rows, WIDTH + 128 * h : WIDTH + 128 * h + 128]
            valued = qkv_ref[rows, 2 * WIDTH + 128 * h : 2 * WIDTH + 128 * h + 128]
            scores = dot(keyed, query, NT)
            weight = jnp.exp(scores - jnp.max(scores, axis=0, keepdims=True))
            probs = (weight * (1.0 / jnp.sum(weight, axis=0, keepdims=True))).astype(BF16)
            probs_ref[s, h] = probs
            heads_ref[rows, cols] = dot(upright(probs), both_heads(valued, low), TN).astype(BF16)

    @pl.when(step == 0)
    def _():
        wait_whole(wout, sems.at[4])
        pltpu.make_async_copy(wout, wout_hbm, sems.at[5]).start()

    attn = dot(heads_ref[...], flat(wout[...])) + vec_ref[2:3, :]
    norm, scale = normalize(x.astype(F32) + attn)
    norm_ref[...] = norm
    scale_ref[...] = jnp.broadcast_to(scale, scale_ref.shape)

    @pl.when(step == STEPS - 1)
    def _():
        pltpu.make_async_copy(wout, wout_hbm, sems.at[5]).wait()


def attention_forward(place, rows, pieces):
    return call(
        attention_kernel,
        [place, rows, *pieces],
        [smem_spec(), row_spec(WIDTH)] + [any_spec()] * 8,
        [
            shape((ROWS, 3 * WIDTH)),
            shape((ROWS // 128, HEADS // 2, 128, 256)),
            shape((ROWS, WIDTH)),
            shape((ROWS, WIDTH), F32),
            shape((ROWS, 128), F32),
            shape((16, WIDTH), F32),
            shape(ORDER + (WIDTH,)),
        ],
        [
            row_spec(3 * WIDTH),
            pl.BlockSpec((BLOCK // 128, HEADS // 2, 128, 256), lambda i: (i, 0, 0, 0)),
            row_spec(WIDTH),
            row_spec(WIDTH),
            row_spec(128),
            one_spec(16, WIDTH),
            any_spec(),
        ],
        20,
        grid=(STEPS,),
        scratch=[
            pltpu.VMEM(ORDER + (3 * WIDTH,), BF16),
            pltpu.VMEM(ORDER + (WIDTH,), BF16),
            pltpu.VMEM(ORDER + (128,), BF16),
            pltpu.SemaphoreType.DMA((6,)),
        ],
    )


def wide_scale(ref):
    return jnp.concatenate([ref[...]] * 6, axis=1)


def hidden_of(norm, vec_ref):
    return norm * vec_ref[3:4, :] + vec_ref[4:5, :]


def gelu_parts(upper):
    phi = 0.5 * (1.0 + lax.erf(upper * 0.7071067811865476))
    bell = jnp.exp(-0.5 * upper * upper) * 0.3989422804014327
    return upper * phi, phi + upper * bell


def contrast_kernel(first_ref, received_ref, keep_ref, partner_ref, dfirst_ref, dreceived_ref):
    first = first_ref[...]
    received = received_ref[...].astype(F32)
    logits = lax.dot_general(first, received, NT, precision=lax.Precision.HIGHEST, preferred_element_type=F32)
    logits = logits * logit_scale
    weight = jnp.exp(logits - jnp.max(logits, axis=-1, keepdims=True))
    soft = weight / jnp.sum(weight, axis=-1, keepdims=True)
    column = lax.broadcasted_iota(jnp.int32, (8, 8), 1)
    chosen = jnp.where(column == partner_ref[...], 1.0, 0.0)
    dlogits = (contrast_weight * logit_scale) * keep_ref[...] * (soft - chosen)
    high = lax.Precision.HIGHEST
    dfirst_ref[...] = lax.dot_general(dlogits, received, NN, precision=high, preferred_element_type=F32)
    dreceived_ref[...] = lax.dot_general(
        dlogits, first, TN, precision=high, preferred_element_type=F32
    ).astype(BF16)


def contrast_back(first, received, keep, partner, deps):
    return call(
        contrast_kernel,
        [Loose(first), Loose(received), Loose(keep), Loose(partner)],
        [full_spec()] * 4,
        [loose((8, WIDTH), F32), loose((8, WIDTH))],
        [full_spec()] * 2,
        4,
        deps=deps,
    )


CHUNK = 512
CHUNKS = INNER // CHUNK


def chunk(n):
    return slice(n * CHUNK, (n + 1) * CHUNK)


def feed_forward_rows(hidden, vec_ref, b_in_ref, size, win_part, wdown_part, put):
    hidden_low = hidden.astype(BF16)
    down, active = hidden + vec_ref[5:6, :], None
    after = dot(hidden_low, win_part(0))
    for n in range(INNER // size):
        upper = after + b_in_ref[:, n * size : (n + 1) * size]
        if (n + 1) * size < INNER:
            after = dot(hidden_low, win_part(n + 1))
        if n > 0:
            down = down + dot(active, wdown_part(n - 1))
        active, slope = gelu_parts(upper)
        active = active.astype(BF16)
        put(slice(n * size, (n + 1) * size), active, slope.astype(BF16))
    down = down + dot(active, wdown_part(INNER // size - 1))
    return normalize(down)


def put_norm(first_span, count, norm, scale, vec_ref, norm_two_ref, scale_ref, mixed_ref):
    norm_two_ref[...] = norm.astype(BF16)
    scale_ref[...] = jnp.broadcast_to(scale, scale_ref.shape)
    final = norm * vec_ref[6:7, :] + vec_ref[7:8, :]
    for s in range(norm.shape[0] // 128):
        rows = slice(128 * s, 128 * s + 128)
        live = jnp.where(first_span + s < count[0], 1.0, 0.0)
        mixed_ref[rows, :] = (final[rows] * live).astype(BF16)


def feed_forward_first_kernel(place, count, norm_ref, norm_hbm, vec_ref, b_in_ref, keep_ref, *refs):
    pieces = refs[:8]
    first_ref, sent_ref, win, wdown, hidden_ref, active_ref, slope_ref, norm_two_ref, scale_ref, mixed_ref = refs[8:18]
    tops, sems, tops_sem = refs[18:]
    for s in range(8):
        pltpu.make_async_copy(norm_hbm.at[pl.ds(128 * s, 8)], tops.at[pl.ds(8 * s, 8)], tops_sem).start()
    all_piece_copies(place, pieces, ((win, 0, 1536, 1),), sems)
    all_piece_copies(place, pieces, ((wdown, 1536, 384, 4),), sems.at[pl.ds(1, 1)])
    wait_whole(tops, tops_sem)
    top = hidden_of(jnp.concatenate([tops[8 * s : 8 * s + 1, :] for s in range(8)], axis=0), vec_ref)
    hidden = hidden_of(norm_ref[...], vec_ref)
    hidden_ref[:TALL, :] = hidden.astype(BF16)
    hidden = jnp.concatenate([hidden, top, jnp.zeros_like(top)], axis=0)
    wait_whole(win, sems.at[0])

    def win_part(n):
        return flat(win[:, :, :, :, n * WIDTH : (n + 1) * WIDTH])

    def wdown_part(n):
        if n == 0:
            wait_whole(wdown, sems.at[1])
        return flat(wdown[n // 2, 2 * (n % 2) : 2 * (n % 2) + 2])

    def put(cols, active, slope):
        active_ref[:TALL, cols] = active[:TALL]
        slope_ref[:TALL, cols] = slope[:TALL]

    norm, scale = feed_forward_rows(hidden, vec_ref, b_in_ref, WIDTH, win_part, wdown_part, put)
    put_norm(0, count, norm[:TALL], scale[:TALL], vec_ref, norm_two_ref, scale_ref, mixed_ref)
    final = norm[TALL : TALL + 8] * vec_ref[6:7, :] + vec_ref[7:8, :]
    first_ref[...] = final
    sent_ref[...] = (final.astype(BF16).astype(F32) * keep_ref[...]).astype(BF16)


def feed_forward_shapes():
    return [
        near((ROWS, WIDTH)),
        near((ROWS, INNER)),
        near((ROWS, INNER)),
        shape((ROWS, WIDTH)),
        shape((ROWS, 128), F32),
        shape((ROWS, WIDTH)),
    ]


def feed_forward_first(place, count, norm, vec, b_in, keep, pieces):
    def rows(width):
        return pl.BlockSpec((TALL, width), lambda i: (0, 0))

    return call(
        feed_forward_first_kernel,
        [place, count, norm, norm, vec, b_in, keep, *pieces],
        [smem_spec(), smem_spec(), rows(WIDTH), any_spec()] + [full_spec()] * 3 + [any_spec()] * 8,
        [
            shape((8, WIDTH), F32),
            loose((8, WIDTH)),
            near(ORDER + (INNER,)),
            near((2, 4, 4, 4, HALF_UNIT, WIDTH)),
        ]
        + feed_forward_shapes(),
        [full_spec()] * 7 + [rows(WIDTH), rows(128), rows(WIDTH)],
        24,
        grid=(1,),
        scratch=[
            pltpu.VMEM((64, WIDTH), F32),
            pltpu.SemaphoreType.DMA((2,)),
            pltpu.SemaphoreType.DMA,
        ],
    )


def feed_forward_kernel(index, count, norm_ref, vec_ref, b_in_ref, win, wdown, *refs):
    hidden_ref, active_ref, slope_ref, norm_two_ref, scale_ref, mixed_ref = refs[-6:]
    here = slice(index * BLOCK, (index + 1) * BLOCK)
    hidden = hidden_of(norm_ref[...], vec_ref)
    hidden_ref[here, :] = hidden.astype(BF16)

    def put(cols, active, slope):
        active_ref[here, cols] = active
        slope_ref[here, cols] = slope

    norm, scale = feed_forward_rows(
        hidden, vec_ref, b_in_ref, CHUNK, lambda n: win[:, chunk(n)], lambda n: wdown[chunk(n), :], put
    )
    put_norm(index * (BLOCK // 128), count, norm, scale, vec_ref, norm_two_ref, scale_ref, mixed_ref)


def feed_forward(index, count, norm, vec, b_in, win, wdown, so_far, deps=()):
    def rows(width):
        return pl.BlockSpec((BLOCK, width), lambda i: (index, 0))

    return call(
        functools.partial(feed_forward_kernel, index),
        [count, norm, vec, b_in, Near(win), Near(wdown)] + [Near(v) if n < 3 else v for n, v in enumerate(so_far)],
        [smem_spec(), rows(WIDTH)] + [full_spec()] * 7 + [any_spec()] * 3,
        feed_forward_shapes(),
        [full_spec()] * 3 + [rows(WIDTH), rows(128), rows(WIDTH)],
        20,
        grid=(1,),
        input_output_aliases={6 + n: n for n in range(6)},
        deps=deps,
    )


def feed_forward_back_kernel(
    count, cot_ref, dfirst_ref, back_ref, keep_ref, norm_ref, scale_ref, vec_ref, slope_ref, wdown, dres_ref, ddown_ref, dupper_ref, sums_ref, db_in_ref
):
    step = pl.program_id(0)
    dfirst = dfirst_ref[...] + back_ref[...].astype(F32) * keep_ref[...]
    slot = lax.broadcasted_iota(jnp.int32, (8, 1), 0)
    blocks = TALL // BLOCK

    def here(b):
        return pl.ds(pl.multiple_of(step * TALL + b * BLOCK, BLOCK), BLOCK)

    def norm_back(b):
        parts = []
        for s in range(BLOCK // 128):
            row = b * BLOCK + 128 * s
            span = step * (TALL // 128) + b * (BLOCK // 128) + s
            live = jnp.where(span < count[0], 1.0, 0.0)
            mine = jnp.sum(jnp.where(slot == span, dfirst, 0.0), axis=0, keepdims=True)
            cot = cot_ref[row : row + 128, :].astype(F32) * live
            top = cot[:8] + jnp.where(slot == 0, mine, 0.0)
            parts += [top, cot[8:]]
        dfinal = jnp.concatenate(parts, axis=0)
        rows = slice(b * BLOCK, (b + 1) * BLOCK)
        norm = norm_ref[rows, :].astype(F32)
        scale = jnp.concatenate([scale_ref[rows, :]] * 6, axis=1)
        dres = normalize_back(dfinal * vec_ref[6:7, :], norm, scale)
        dres_ref[here(b), :] = dres
        ddown = dres.astype(BF16)
        ddown_ref[here(b), :] = ddown
        return ddown, [column_sum(dfinal * norm), column_sum(dfinal), column_sum(dres)]

    jobs = [(b, n) for b in range(blocks) for n in range(CHUNKS)]
    ready, sums, sums_in = norm_back(0), [], [[] for _ in range(blocks)]
    sums.append(ready[1])
    ddown = ready[0]
    after = dot(ddown, wdown[chunk(0), :], NT)
    for k, (b, n) in enumerate(jobs):
        dactive = after
        if n == 0 and b + 1 < blocks:
            ready = norm_back(b + 1)
            sums.append(ready[1])
        if k + 1 < len(jobs):
            if n + 1 == CHUNKS:
                ddown = ready[0]
            after = dot(ddown, wdown[chunk(jobs[k + 1][1]), :], NT)
        dupper = dactive * slope_ref[here(b), chunk(n)].astype(F32)
        dupper_ref[here(b), chunk(n)] = dupper.astype(BF16)
        sums_in[b].append(column_sum(dupper))
    add_rows(sums_ref, step, *[sum(group) for group in zip(*sums)])
    add_rows(db_in_ref, step, sum(jnp.concatenate(parts, axis=1) for parts in sums_in))


def feed_forward_back(count, cotangent, dfirst, back, keep, norm, scale, vec, slope, wdown):
    return call(
        feed_forward_back_kernel,
        [count, cotangent, Loose(dfirst), Loose(back), Loose(keep), norm, scale, vec, Near(slope), Near(wdown)],
        [smem_spec(), tall_spec(WIDTH), full_spec(), full_spec(), full_spec(), tall_spec(WIDTH), tall_spec(128)]
        + [full_spec()] * 3,
        [
            near((ROWS, WIDTH), F32),
            near((ROWS, WIDTH)),
            near((ROWS, INNER)),
            shape((24, WIDTH), F32),
            shape((8, INNER), F32),
        ],
        [full_spec(), full_spec(), full_spec(), one_spec(24, WIDTH), one_spec(8, INNER)],
        20,
        grid=(ROWS // TALL,),
        input_output_aliases={8: 2},
    )


def hidden_back_kernel(
    dres_ref, dupper_ref, norm_ref, scale_ref, vec_ref, win, wout, dres_one_ref, dattn_ref, dheads_ref, sums_ref
):
    step = pl.program_id(0)
    count = TALL // BLOCK

    def here(n):
        return pl.ds(pl.multiple_of(step * TALL + n * BLOCK, BLOCK), BLOCK)

    def product(n):
        return dot(dupper_ref[here(n), :], win[...], NT)

    after, sums = product(0), []

    for n in range(count):
        rows = slice(n * BLOCK, (n + 1) * BLOCK)
        dhidden = dres_ref[here(n), :] + after
        if n + 1 < count:
            after = product(n + 1)
        norm = norm_ref[rows, :]
        scale = jnp.concatenate([scale_ref[rows, :]] * 6, axis=1)
        dres = normalize_back(dhidden * vec_ref[3:4, :], norm, scale)
        dres_one_ref[rows, :] = dres
        dattn = dres.astype(BF16)
        dattn_ref[rows, :] = dattn
        dheads_ref[rows, :] = dot(dattn, flat(wout[...]), NT).astype(BF16)
        sums.append([column_sum(dhidden * norm), column_sum(dhidden), column_sum(dres)])
    add_rows(sums_ref, step, *[sum(group) for group in zip(*sums)])


def hidden_back(dres, dupper, norm, scale, vec, win, wout, deps):
    return call(
        hidden_back_kernel,
        [Near(dres), Near(dupper), norm, scale, vec, Near(win), wout],
        [full_spec(), full_spec(), tall_spec(WIDTH), tall_spec(128)] + [full_spec()] * 3,
        [shape((ROWS, WIDTH), F32), shape((ROWS, WIDTH)), shape((ROWS, WIDTH)), shape((24, WIDTH), F32)],
        [tall_spec(WIDTH), tall_spec(WIDTH), tall_spec(WIDTH), one_spec(24, WIDTH)],
        22,
        grid=(ROWS // TALL,),
        deps=deps,
    )


def attention_back_kernel(qkv_ref, probs_ref, dheads_ref, dqkv_ref, near_ref, sums_ref):
    step = pl.program_id(0)
    low = pair_masks()
    for s in range(BLOCK // 128):
        rows = slice(128 * s, 128 * s + 128)
        for h in range(HEADS // 2):
            query = both_heads(qkv_ref[rows, 128 * h : 128 * h + 128] * BF16(0.125), low)
            keyed = qkv_ref[rows, WIDTH + 128 * h : WIDTH + 128 * h + 128]
            valued = qkv_ref[rows, 2 * WIDTH + 128 * h : 2 * WIDTH + 128 * h + 128]
            dheads = both_heads(dheads_ref[rows, 128 * h : 128 * h + 128], low)
            probs_low = probs_ref[s, h]
            probs = probs_low.astype(F32)
            dprobs = dot(valued, dheads, NT)
            inner = jnp.sum(probs * dprobs, axis=0, keepdims=True)
            dscores = (probs * (dprobs - inner)).astype(BF16)
            dquery = dot(upright(dscores), both_heads(keyed * BF16(0.125), low), TN)
            dqkv_ref[rows, 128 * h : 128 * h + 128] = dquery.astype(BF16)
            dqkv_ref[rows, WIDTH + 128 * h : WIDTH + 128 * h + 128] = dot(dscores, query).astype(BF16)
            dqkv_ref[rows, 2 * WIDTH + 128 * h : 2 * WIDTH + 128 * h + 128] = dot(probs_low, dheads).astype(BF16)
    near_ref[block_rows(step, BLOCK), :] = dqkv_ref[...]
    add_rows(
        sums_ref,
        step,
        column_sum(dqkv_ref[:, :WIDTH].astype(F32)),
        column_sum(dqkv_ref[:, 2 * WIDTH :].astype(F32)),
    )


def attention_back(qkv, probs, dheads, deps):
    return call(
        attention_back_kernel,
        [qkv, probs, dheads],
        [
            row_spec(3 * WIDTH),
            pl.BlockSpec((BLOCK // 128, HEADS // 2, 128, 256), lambda i: (i, 0, 0, 0)),
            row_spec(WIDTH),
        ],
        [shape((ROWS, 3 * WIDTH)), near((ROWS, 3 * WIDTH)), shape((16, WIDTH), F32)],
        [row_spec(3 * WIDTH), full_spec(), one_spec(16, WIDTH)],
        16,
        grid=(STEPS,),
        deps=deps,
    )


def tokens_back_kernel(place, dres_ref, dqkv_ref, *refs):
    pieces, (out_ref, wqkv, sems) = refs[:8], refs[8:]

    @pl.when(pl.program_id(0) == 0)
    def _():
        all_piece_copies(place, pieces, ((wqkv, 0, 1152, 1),), sems)
        wait_whole(wqkv, sems.at[0])

    out_ref[...] = (dres_ref[...] + dot(dqkv_ref[...], flat(wqkv[...]), NT)).astype(BF16)


def tokens_back(place, dres, dqkv, pieces, deps):
    return call(
        tokens_back_kernel,
        [place, dres, dqkv, *pieces],
        [smem_spec(), row_spec(WIDTH), row_spec(3 * WIDTH)] + [any_spec()] * 8,
        shape((ROWS, WIDTH)),
        row_spec(WIDTH),
        14,
        grid=(STEPS,),
        scratch=[pltpu.VMEM(ORDER + (3 * WIDTH,), BF16), pltpu.SemaphoreType.DMA((1,))],
        deps=deps,
    )


def put_unit(place, both, half, unit, p, cols, value):
    side = place[0] if half == 0 else 1 - place[0]
    both[side, place[1 + 16 * half + unit], p, :, cols] = value.astype(BF16)


def put_units(place, both, half, cols, value):
    for p in range(2):
        for unit in range(16):
            row = 384 * p + HALF_UNIT * unit
            put_unit(place, both, half, unit, p, cols, value[row : row + HALF_UNIT])


def write_half(place, both, half, outs, sem, cols):
    for core in range(2):

        @pl.when(place[0] == core)
        def _(side=half ^ core):
            pltpu.make_async_copy(both.at[side, :, :, :, cols], outs[side].at[:, :, :, cols], sem).start()


def run_ahead(jobs):
    after = jobs[0][0]()
    for n, (_, use) in enumerate(jobs):
        value = after
        if n + 1 < len(jobs):
            after = jobs[n + 1][0]()
        use(value)


def layer_grads_kernel(place, active_ref, ddown_ref, hidden_ref, dupper_ref, own, theirs, both, sem):
    outs = (own, theirs)

    def in_job(h, n):
        cols = slice(768 * n, 768 * n + 768)

        def product():
            first = 1536 * h + 768 * n
            return dot(hidden_ref[...], dupper_ref[:, first : first + 768], TN)

        return product, lambda value: put_units(place, both, h, cols, value)

    def down_job(n):
        def product():
            return dot(active_ref[:, WIDTH * n : WIDTH * n + WIDTH], ddown_ref[...], TN)

        def use(value):
            for h in range(2):
                for i in range(2):
                    for y in range(4):
                        for j in range(4):
                            row = 384 * i + 96 * y + HALF_UNIT * j
                            part = value[row : row + HALF_UNIT, 384 * h : 384 * h + 384]
                            cols = slice(1536 + 384 * j, 1536 + 384 * j + 384)
                            put_unit(place, both, h, 4 * (2 * (n % 2) + i) + y, n // 2, cols, part)

        return product, use

    def write(p, cols):
        for side in (1, 0):
            pltpu.make_async_copy(both.at[side, :, p, :, cols], outs[side].at[:, p, :, cols], sem).start()

    run_ahead([in_job(h, n) for h in range(2) for n in range(2)])
    write(0, slice(0, 1536))
    write(1, slice(0, 1536))
    run_ahead([down_job(n) for n in range(2)])
    write(0, slice(1536, 3072))
    run_ahead([down_job(n) for n in range(2, 4)])
    write(1, slice(1536, 3072))
    wait_whole(both, sem)


def layer_grads(place, active, ddown, hidden_low, dupper):
    return call(
        layer_grads_kernel,
        [place, Near(active), Near(ddown), Near(hidden_low), Near(dupper)],
        [smem_spec()] + [full_spec()] * 4,
        [shape((16, 2, HALF_UNIT, 3072)), loose((16, 2, HALF_UNIT, 3072))],
        [any_spec(), any_spec()],
        20,
        scratch=[pltpu.VMEM((2, 16, 2, HALF_UNIT, 3072), BF16), pltpu.SemaphoreType.DMA],
    )


def every_fourth(line, j):
    blocks = jnp.concatenate([line[:, 512 * n : 512 * n + 512] for n in range(6)] + [jnp.zeros((2, 512), F32)], axis=0)
    row = lax.broadcasted_iota(jnp.int32, (512, 128), 0)
    lane = lax.broadcasted_iota(jnp.int32, (512, 128), 1)
    pick = jnp.where(row == 4 * lane + j, 1.0, 0.0)
    picked = lax.dot_general(blocks, pick, NN, precision=lax.Precision.HIGHEST, preferred_element_type=F32)
    return jnp.concatenate([picked[n : n + 1] for n in range(6)], axis=1)


def attention_grads_kernel(
    place, x_hbm, dqkv_ref, heads_hbm, dattn_hbm, sums_qkv, sums_one, sums_two, db_in, own, theirs, both, x, heads, dattn, sems
):
    pairs = ((x_hbm, x), (heads_hbm, heads), (dattn_hbm, dattn))
    loads = [pltpu.make_async_copy(far, here, sems.at[n]) for n, (far, here) in enumerate(pairs)]
    for load in loads:
        load.start()
    outs, done = (own, theirs), sems.at[3]

    def total(ref, n):
        return jnp.sum(ref[8 * n : 8 * n + 8, :], axis=0, keepdims=True)

    rows = [total(sums_qkv, 0), total(sums_qkv, 1), total(sums_one, 2), total(sums_one, 0), total(sums_one, 1)]
    rows += [total(sums_two, 2), total(sums_two, 0), total(sums_two, 1)]
    rows += [every_fourth(total(db_in, 0), j) for j in range(4)] + [jnp.zeros((116, WIDTH), F32)]
    wide = jnp.concatenate(rows, axis=0).T
    put_units(place, both, 0, slice(1152, 1280), wide)
    put_units(place, both, 1, slice(1152, 1280), jnp.zeros_like(wide))
    loads[0].wait()

    def job(n):
        def product():
            return dot(x[...], dqkv_ref[:, 768 * n : 768 * n + 768], TN)

        def use(value):
            for m in range(2):
                first = 768 * n + 384 * m
                h, at = first // 1152, first % 1152
                put_units(place, both, h, slice(at, at + 384), value[:, 384 * m : 384 * m + 384])
                write_half(place, both, h, outs, done, slice(at, at + 384))

        return product, use

    def out_product():
        loads[1].wait()
        loads[2].wait()
        return dot(heads[...], dattn[...], TN)

    def out_use(value):
        for h in range(2):
            put_units(place, both, h, slice(1280, FIRST), value[:, 384 * h : 384 * h + 384])
            write_half(place, both, h, outs, done, slice(1152, FIRST))

    run_ahead([job(n) for n in range(3)] + [(out_product, out_use)])
    wait_whole(both, done)


def attention_grads(place, rows, dqkv, heads, dattn, sums, deps):
    sums_qkv, sums_one, sums_two, db_in = sums
    return call(
        attention_grads_kernel,
        [place, rows, Near(dqkv), heads, dattn, sums_qkv, sums_one, sums_two, db_in],
        [smem_spec(), any_spec(), full_spec(), any_spec(), any_spec()] + [full_spec()] * 4,
        [shape((16, 2, HALF_UNIT, FIRST)), loose((16, 2, HALF_UNIT, FIRST))],
        [any_spec(), any_spec()],
        20,
        scratch=[pltpu.VMEM((2, 16, 2, HALF_UNIT, FIRST), BF16)]
        + [pltpu.VMEM((ROWS, WIDTH), BF16)] * 3
        + [pltpu.SemaphoreType.DMA((4,))],
        deps=deps,
    )


def add_kernel(own_hbm, recv_hbm, *refs):
    outs, (own, recv, sems) = refs[:-3], refs[-3:]
    loads = []
    for r in range(4):
        part = pl.ds(4 * r, 4)
        pair = [
            pltpu.make_async_copy(own_hbm.at[part], own.at[part], sems.at[2 * r]),
            pltpu.make_async_copy(recv_hbm.at[part], recv.at[part], sems.at[2 * r + 1]),
        ]
        for load in pair:
            load.start()
        loads.append(pair)
    for r in range(4):
        for load in loads[r]:
            load.wait()
        for k in range(4):
            outs[r][k] = (own[4 * r + k].astype(F32) + recv[4 * r + k].astype(F32)).astype(BF16)


def add_theirs(own, recv, deps):
    width = recv.shape[3]
    buffer = pltpu.VMEM((16, 2, HALF_UNIT, width), BF16)
    return call(
        add_kernel,
        [own, Loose(recv)],
        [any_spec()] * 2,
        [loose((4, 2, HALF_UNIT, width))] * 4,
        [full_spec()] * 4,
        18,
        scratch=[buffer, buffer, pltpu.SemaphoreType.DMA((8,))],
        deps=deps,
    )


OCTET = FIRST + 1536 + 384


def pack_kernel(wqkv_hbm, wout_hbm, win_hbm, wdown_hbm, vec, mask, pick, out_ref, wqkv, wout, win, wdown, sems):
    loads = [
        pltpu.make_async_copy(far, here, sems.at[n])
        for n, (far, here) in enumerate(((wqkv_hbm, wqkv), (wout_hbm, wout), (win_hbm, win), (wdown_hbm, wdown)))
    ]
    for load in loads:
        load.start()
    column = dot((vec[...] * mask[...]).astype(BF16), pick[...])[:6].astype(BF16)
    for load in loads:
        load.wait()
    for h in range(2):
        out_ref[h] = jnp.zeros((8, OCTET), BF16)
        out_ref[h, :6, :1152] = wqkv[:, 1152 * h : 1152 * h + 1152]
        out_ref[h, :6, 1152:1280] = column
        out_ref[h, :6, 1280:FIRST] = wout[:, 384 * h : 384 * h + 384]
        out_ref[h, :6, FIRST : FIRST + 1536] = win[:, 1536 * h : 1536 * h + 1536]
        out_ref[h, :6, FIRST + 1536 :] = wdown[:6, 384 * h : 384 * h + 384]
        for q in range(18):
            row, at = 6 + q // 9, 384 * (q % 9)
            out_ref[h, row : row + 1, at : at + 384] = wdown[6 + q : 7 + q, 384 * h : 384 * h + 384]
    for k in range(2, 8):
        out_ref[k] = out_ref[k % 2]


def pack(wqkv, wout, win, wdown, vectors, b_in):
    vec = jnp.zeros((128,), F32)
    for n, v in enumerate(list(vectors) + [b_in]):
        vec = vec + lax.pad(v.astype(F32), jnp.zeros((), F32), [(6 * n, 128 - 6 * n - v.shape[0], 0)])
    j = np.arange(128)
    r = np.where(j < 48, j % 6, np.where(j < 72, (j - 48) // 4, -1))
    i = np.where(j < 48, j // 6, np.where(j < 72, 8 + (j - 48) % 4, -1))
    mask = (r[None, :] == np.arange(8)[:, None]).astype(np.float32)
    pick = (i[:, None] == np.arange(128)[None, :]).astype(ml_dtypes.bfloat16)
    return call(
        pack_kernel,
        [wqkv, wout, win, wdown, vec.reshape(1, 128), mask, pick],
        [any_spec()] * 4 + [full_spec()] * 3,
        loose((8, 8, OCTET)),
        full_spec(),
        6,
        scratch=[
            pltpu.VMEM((6, 2304), BF16),
            pltpu.VMEM((6, 768), BF16),
            pltpu.VMEM((6, 3072), BF16),
            pltpu.VMEM((24, 768), BF16),
            pltpu.SemaphoreType.DMA((4,)),
        ],
    )


def stack_kernel(cuts, place, *refs):
    parts, outs = refs[:4], refs[4:]
    for q in range(4):
        slot = place[33 + (4 - q) % 4]
        for n, (first, width) in enumerate(cuts):
            outs[n][slot] = parts[q][:, :, first : first + width]


def stack(place, parts, cuts):
    return call(
        functools.partial(stack_kernel, cuts),
        [place, *[Loose(p) for p in parts]],
        [smem_spec()] + [full_spec()] * 4,
        [loose((4, 2, HALF_UNIT, w)) for _, w in cuts],
        [full_spec()] * len(cuts),
        8,
    )


def gate_kernel(*refs):
    pass


def gate(values, deps):
    return call(
        gate_kernel,
        [Loose(v) for v in values],
        [any_spec()] * len(values),
        [loose(v.shape, v.dtype) for v in values],
        [any_spec()] * len(values),
        2,
        deps=deps,
        input_output_aliases={n: n for n in range(len(values))},
    )


def sum_kernel(sets, more, *refs):
    ins, rest, outs = refs[: 4 * sets], refs[4 * sets : 4 * sets + more], refs[4 * sets + more :]
    for r in range(4):
        first = 0
        for g in range(sets):
            part = ins[4 * g : 4 * g + 4]
            width = part[0].shape[3]
            total = part[0][r].astype(F32)
            for p in part[1:]:
                total = total + p[r].astype(F32)
            outs[r][:, :, first : first + width] = total.astype(BF16)
            first += width
        if more:
            outs[r][:, :, first:] = rest[r][...]


def sum_blocks(parts, more=(), deps=(), weight=0):
    width = parts[0].shape[3] + (more[0].shape[2] if more else 0)
    args = [Loose(p) for p in list(parts) + list(more)]
    return call(
        functools.partial(sum_kernel, 1, len(more)),
        args,
        [full_spec()] * len(args),
        [loose((2, HALF_UNIT, width))] * 4,
        [full_spec()] * 4,
        14,
        deps=deps,
        weight=weight,
    )


def finish_kernel(in_ref, dqkv, dout, din, ddown, *vectors):
    for h in range(2):
        total = in_ref[h].astype(F32)
        for k in range(h + 2, 8, 2):
            total = total + in_ref[k].astype(F32)
        dqkv[:, 1152 * h : 1152 * h + 1152] = total[:6, :1152]
        dout[:, 384 * h : 384 * h + 384] = total[:6, 1280:FIRST]
        din[:, 1536 * h : 1536 * h + 1536] = total[:6, FIRST : FIRST + 1536]
        ddown[:6, 384 * h : 384 * h + 384] = total[:6, FIRST + 1536 :]
        for q in range(18):
            row, at = 6 + q // 9, 384 * (q % 9)
            ddown[6 + q : 7 + q, 384 * h : 384 * h + 384] = total[row : row + 1, at : at + 384]
        if h == 0:
            wide = jnp.concatenate([total[:6, 1152:1280], jnp.zeros((122, 128), F32)], axis=0).T
    for n in range(8):
        vectors[n][...] = wide[n, :6]
    row = lax.broadcasted_iota(jnp.int32, (128, 128), 0)
    lane = lax.broadcasted_iota(jnp.int32, (128, 128), 1)
    b_in = jnp.zeros((8, 128), F32)
    for j in range(4):
        spread = jnp.where(lane == 4 * row + j, 1.0, 0.0)
        line = jnp.concatenate([wide[8 + j : 9 + j]] * 8, axis=0)
        b_in = b_in + lax.dot_general(line, spread, NN, precision=lax.Precision.HIGHEST, preferred_element_type=F32)
    vectors[8][...] = b_in[0, :24]


def finish(blocks):
    return call(
        finish_kernel,
        [Loose(blocks)],
        [full_spec()],
        [shape(d, F32) for d in ((6, 2304), (6, 768), (6, 3072), (24, 768)) + ((6,),) * 8 + ((24,),)],
        [full_spec()] * 13,
        6,
    )


def unpack_kernel(blocks, unit):
    for k in range(8):
        p, j = k // 4, k % 4
        at = FIRST + 1536 + 384 * j
        unit[p, 6 * j : 6 * j + 6, : FIRST + 1536] = blocks[k, :6, : FIRST + 1536]
        unit[p, :6, at : at + 384] = blocks[k, :6, FIRST + 1536 :]
        for q in range(18):
            row, first = 6 + q // 9, 384 * (q % 9)
            unit[p, 6 + q : 7 + q, at : at + 384] = blocks[k, row : row + 1, first : first + 384]


def unpack_octet(blocks):
    return call(
        unpack_kernel,
        [Loose(blocks)],
        [full_spec()],
        loose((2, HALF_UNIT, FIRST + 3072)),
        full_spec(),
        6,
    )


def total_kernel(*refs):
    out = refs[4]
    total = refs[0][...].astype(F32)
    for part in refs[1:4]:
        total = total + part[...].astype(F32)
    total = total.astype(BF16)
    for k in range(8):
        p, j = k // 4, k % 4
        at = FIRST + 1536 + 384 * j
        out[k] = jnp.zeros((8, OCTET), BF16)
        out[k, :6, : FIRST + 1536] = total[p, 6 * j : 6 * j + 6, : FIRST + 1536]
        out[k, :6, FIRST + 1536 :] = total[p, :6, at : at + 384]
        for q in range(18):
            row, first = 6 + q // 9, 384 * (q % 9)
            out[k, row : row + 1, first : first + 384] = total[p, 6 + q : 7 + q, at : at + 384]


def total_blocks(parts):
    return call(
        total_kernel, [Loose(p) for p in parts], [full_spec()] * 4, loose((8, 8, OCTET)), full_spec(), 6
    )


def per_device(
    tokens,
    cotangent,
    span_counts,
    single_flags,
    partner_slots,
    w_qkv,
    b_query,
    b_value,
    w_out,
    b_out,
    gain_attn,
    shift_attn,
    w_in,
    b_in,
    w_down,
    b_down,
    gain_ffn,
    shift_ffn,
):
    place = my_place()
    packed = pack(
        w_qkv, w_out, w_in, w_down, [b_query, b_value, b_out, gain_attn, shift_attn, b_down, gain_ffn, shift_ffn], b_in
    )
    rows48 = exchange_octet(packed)
    unit = unpack_octet(rows48)
    one_early, two_early = stack(place, gather(unit, 0), ((0, FIRST), (FIRST, 3072)))
    one_late = gather(one_early, 1)
    one_pieces = one_late + [to_core(piece) for piece in one_late]
    two_late = gather(two_early, 1)

    count = span_counts[0]
    live = (jnp.arange(8, dtype=jnp.int32) < count).astype(F32)
    keep = (live * (1.0 - single_flags[0].astype(F32)))[:, None]
    partner = partner_slots[0][:, None]
    rows = tokens.reshape(ROWS, WIDTH)

    qkv, probs, heads, norm_one, scale_one, vec, wout = attention_forward(place, rows, one_pieces)
    full_b_in = vec[8:12].T.reshape(1, INNER)
    two_late = [two_late[0], *gate(two_late[1:], [vec])]
    first, sent, win, wdown, *so_far = feed_forward_first(
        place, count, norm_one, vec, full_b_in, keep, two_late + [to_core(piece) for piece in two_late]
    )
    win, wdown = win.reshape(WIDTH, INNER), wdown.reshape(INNER, WIDTH)
    partners = [(d, d ^ 64) for d in range(128)]
    received = send(sent, partners)
    so_far = feed_forward(2, count, norm_one, vec, full_b_in, win, wdown, so_far)
    dfirst, dreceived = contrast_back(first, received, keep, partner, [so_far[4]])
    returned = send(dreceived, partners)
    hidden_low, active, slope, norm_two, scale_two, mixed = feed_forward(
        3, count, norm_one, vec, full_b_in, win, wdown, so_far, [Loose(dreceived)]
    )
    dres_two, ddown, dupper, sums_two, db_in = feed_forward_back(
        count, cotangent.reshape(ROWS, WIDTH), dfirst, returned, keep, norm_two, scale_two, vec, slope, wdown
    )
    two_mine, two_out = layer_grads(place, active, ddown, hidden_low, dupper)
    two_recv = to_core(two_out)
    dres_one, dattn, dheads, sums_one = hidden_back(
        dres_two, dupper, norm_one, scale_one, vec, win, wout, [Loose(two_out)]
    )
    two_own = add_theirs(two_mine, two_recv, [sums_one])
    two_parts = scatter_sends(two_own, 1)
    dqkv, dqkv_near, sums_qkv = attention_back(qkv, probs, dheads, [Loose(two_own[0])])
    sums = (sums_qkv, sums_one, sums_two, db_in)
    one_mine, one_out = attention_grads(place, rows, dqkv_near, heads, dattn, sums, [])
    one_recv = to_core(one_out)
    late = sum_blocks(two_parts, deps=[one_mine], weight=3e10)
    one_own = add_theirs(one_mine, one_recv, [Loose(late[0])])
    one_parts = scatter_sends(one_own, 1)
    grad_tokens = tokens_back(place, dres_one, dqkv, one_pieces, [Loose(one_own[0])])
    back = total_blocks(scatter_sends(sum_blocks(one_parts, late, deps=[grad_tokens]), 0))
    dqkv_own, dout_own, din_own, ddown_own, *vectors = finish(exchange_octet(back))
    return (
        mixed.reshape(tokens.shape),
        grad_tokens.reshape(tokens.shape),
        dqkv_own,
        vectors[0],
        vectors[1],
        dout_own,
        vectors[2],
        vectors[3],
        vectors[4],
        din_own,
        vectors[8],
        ddown_own,
        vectors[5],
        vectors[6],
        vectors[7],
    )


def solution(mesh):
    return jax.shard_map(
        per_device,
        mesh=mesh,
        in_specs=(
            P("pair", "dp", None, None),
            P("pair", "dp", None, None),
            P("pair", "dp"),
            P("pair", "dp"),
            P("pair", "dp"),
            P(("pair", "dp"), None),
            P(("pair", "dp")),
            P(("pair", "dp")),
            P(("pair", "dp"), None),
            P(("pair", "dp")),
            P(("pair", "dp")),
            P(("pair", "dp")),
            P(("pair", "dp"), None),
            P(("pair", "dp")),
            P(("pair", "dp"), None),
            P(("pair", "dp")),
            P(("pair", "dp")),
            P(("pair", "dp")),
        ),
        out_specs=(
            P("pair", "dp", None, None),
            P("pair", "dp", None, None),
            P(("pair", "dp"), None),
            P(("pair", "dp")),
            P(("pair", "dp")),
            P(("pair", "dp"), None),
            P(("pair", "dp")),
            P(("pair", "dp")),
            P(("pair", "dp")),
            P(("pair", "dp"), None),
            P(("pair", "dp")),
            P(("pair", "dp"), None),
            P(("pair", "dp")),
            P(("pair", "dp")),
            P(("pair", "dp")),
        ),
        check_vma=False,
    )
```

```python
import functools

import jax
import jax.numpy as jnp
import ml_dtypes
import numpy as np
from jax import lax
from jax.experimental import pallas as pl
from jax.experimental.pallas import tpu as pltpu
from jax.sharding import PartitionSpec as P

HEADS = 12
HEAD_DIM = 64


epsilon = 1e-12
contrast_weight = 8.0
logit_scale = 0.0625


AXES = ("pair", "dp")
PIECES = (0, 3, 1, 2)
HALF_UNIT = 24


def device_index(p, x, y, z, c):
    return (((p * 4 + x) * 4 + y) * 2 + z) * 2 + c


def all_places():
    return [(p, x, y, z, c) for p in range(2) for x in range(4) for y in range(4) for z in range(2) for c in range(2)]


def moved(place, stage, r):
    p, x, y, z, c = place
    if (stage == 0) == (c == 0):
        return (p, x, (y + r) % 4, z, c)
    return (p, (x + r) % 4, y, z, c)


def stage_pairs(stage, r, back=False):
    pairs = [(device_index(*moved(q, stage, r)), device_index(*q)) for q in all_places()]
    return [(t, s) for s, t in pairs] if back else pairs


def core_pairs():
    return [(d, d ^ 1) for d in range(128)]


def octets():
    return [
        [device_index(p, x, y, z, c) for p in range(2) for z in range(2) for c in range(2)]
        for x in range(4)
        for y in range(4)
    ]


def send(value, pairs):
    return lax.ppermute(value, AXES, pairs)


def exchange_octet(value):
    return lax.all_to_all(value, AXES, 0, 0, axis_index_groups=octets(), tiled=True)


def my_place():
    dp = lax.axis_index("dp")
    c, y, x = dp & 1, (dp >> 2) & 3, (dp >> 4) & 3
    i = jnp.arange(16, dtype=jnp.int32)
    far_x, far_y = ((i >> 2) - x) & 3, ((i & 3) - y) & 3
    r = jnp.arange(4, dtype=jnp.int32)
    slots = jnp.where(c == 0, y + r, x + r) & 3
    parts = [c[None], 4 * far_x + far_y, 4 * far_y + far_x, slots, x[None], y[None]]
    return jnp.concatenate(parts).astype(jnp.int32)


WIDE = (1152, 128, 384)
FIRST = sum(WIDE)
SECOND = 3072


def gather(block, stage):
    return [block] + [send(block, stage_pairs(stage, r)) for r in PIECES[1:]]


def to_core(value):
    return send(value, core_pairs())


def scatter_sends(blocks, stage):
    return [blocks[0]] + [send(blocks[r], stage_pairs(stage, r, True)) for r in (1, 2, 3)]


F32 = jnp.float32
BF16 = jnp.bfloat16
NN = (((1,), (0,)), ((), ()))
NT = (((1,), (1,)), ((), ()))
TN = (((0,), (0,)), ((), ()))
ROWS = 1024
BLOCK = 256
STEPS = ROWS // BLOCK
TALL = 512
WIDTH = 768
INNER = 3072
MIB = 2**20
WEIGHTS = {
    "attention_kernel": 0,
    "feed_forward_first_kernel": 3.75e+08,
    "contrast_kernel": 6.25e+06,
    "feed_forward_kernel": 1.875e+08,
    "feed_forward_back_kernel": 3.125e+08,
    "hidden_back_kernel": 3.75e+08,
    "upper_back_kernel": 3.75e+08,
    "lower_back_kernel": 3.75e+08,
    "attention_back_kernel": 3.125e+08,
    "tokens_back_kernel": 2.5e+08,
    "layer_grads_kernel": 6.25e+08,
    "attention_grads_kernel": 3.125e+08,
    "add_kernel": 1.25e+08,
    "gate_kernel": 0,
    "total_kernel": 3.125e+07,
    "unpack_kernel": 3.125e+07,
    "collect_kernel": 1.25e+08,
    "stack_kernel": 3.125e+07,
    "pack_kernel": 3.125e+07,
    "finish_kernel": 3.125e+07,
    "sum_kernel": 3.125e+07,
}


def dot(left, right, dims=NN):
    return lax.dot_general(left, right, dims, preferred_element_type=F32)


def full_spec():
    return pl.BlockSpec(memory_space=pltpu.VMEM)


def any_spec():
    return pl.BlockSpec(memory_space=pl.ANY)


def smem_spec():
    return pl.BlockSpec(memory_space=pltpu.SMEM)


def row_spec(width, block=BLOCK):
    return pl.BlockSpec((block, width), lambda i: (i, 0))


def tall_spec(width):
    return row_spec(width, TALL)


def one_spec(rows, width):
    return pl.BlockSpec((rows, width), lambda i: (0, 0))


def shape(dims, dtype=BF16):
    return pltpu.HBM(dims, dtype)


def near(dims, dtype=BF16):
    return pltpu.VMEM(dims, dtype)


def loose(dims, dtype=BF16):
    return jax.ShapeDtypeStruct(dims, dtype)


class Near:
    def __init__(self, value):
        self.value = value


class Loose(Near):
    pass


def pinned(value):
    if isinstance(value, Loose):
        return value.value
    if isinstance(value, Near):
        return pltpu.with_memory_space_constraint(value.value, pltpu.VMEM)
    return pltpu.with_memory_space_constraint(value, pltpu.HBM)


def block_rows(step, block=TALL):
    return pl.ds(pl.multiple_of(step * block, block), block)


def limit(mib):
    return pltpu.CompilerParams(vmem_limit_bytes=mib * MIB)


def call(kernel, args, in_specs, out_shape, out_specs, mib, weight=0, grid=None, scratch=(), deps=(), **more):
    n_args, n_deps = len(args), len(deps)

    def body(*refs):
        kernel(*refs[:n_args], *refs[n_args + n_deps :])

    kwargs = dict(more)
    args = [a if spec.memory_space == pltpu.SMEM else pinned(a) for a, spec in zip(args, in_specs)]
    deps = [pinned(a) for a in deps]
    if grid is not None:
        kwargs["grid"] = grid
    return pl.pallas_call(
        body,
        out_shape=out_shape,
        in_specs=list(in_specs) + [any_spec()] * n_deps,
        out_specs=out_specs,
        scratch_shapes=list(scratch),
        cost_estimate=pl.CostEstimate(flops=int(weight or WEIGHTS.get(getattr(kernel, "func", kernel).__name__, 0)), bytes_accessed=0, transcendentals=0),
        name=getattr(kernel, "func", kernel).__name__,
        compiler_params=limit(24),
        **kwargs,
    )(*args, *deps)


def normalize(resid):
    centered = resid - jnp.mean(resid, axis=-1, keepdims=True)
    variance = jnp.mean(centered * centered, axis=-1, keepdims=True)
    scale = lax.rsqrt(variance + epsilon)
    return centered * scale, scale


def normalize_back(grad, norm, scale):
    mean_grad = jnp.mean(grad, axis=-1, keepdims=True)
    mean_both = jnp.mean(grad * norm, axis=-1, keepdims=True)
    return scale * (grad - mean_grad - norm * mean_both)


def column_sum(value):
    return jnp.sum(value.reshape(-1, 8, value.shape[1]), axis=0)


def add_rows(ref, step, *rows):
    total = jnp.concatenate(list(rows), axis=0)

    @pl.when(step == 0)
    def _():
        ref[...] = total

    @pl.when(step > 0)
    def _():
        ref[...] += total


def piece_copies(place, core, half, pieces, targets, sems):
    x, y = place[37], place[38]
    for q in range(4):
        r = PIECES[q]
        for n, (ref, at, first, width, blocks) in enumerate(targets):
            for j in range(blocks):
                inner = (j, slice(None), pl.ds(at, width)) if blocks > 1 else (slice(None), pl.ds(at, width))
                for p in range(2):
                    row = (p, (x + r) & 3, slice(None)) if half == 0 else (p, slice(None), (y + r) & 3)
                    pltpu.make_async_copy(
                        pieces[q].at[:, p, :, pl.ds(first + j * width, width)], ref.at[row + inner], sems.at[n]
                    ).start()


def all_piece_copies(place, pieces, targets, sems):
    for core in range(2):

        @pl.when(place[0] == core)
        def _(core=core):
            for half in range(2):
                mine = pieces[:4] if half == core else pieces[4:]
                into = [(ref, half * width, first, width, blocks) for ref, first, width, blocks in targets]
                piece_copies(place, core, half, mine, into, sems)


def flat(value):
    return value.reshape(-1, value.shape[-1])


ORDER = (2, 4, 4, HALF_UNIT)


def wait_whole(ref, sem):
    pltpu.make_async_copy(ref, ref, sem).wait()


def pair_masks():
    lane = lax.broadcasted_iota(jnp.int32, (128, 128), 1)
    return lane < HEAD_DIM


def both_heads(block, low):
    zero = jnp.zeros_like(block)
    return jnp.concatenate([jnp.where(low, block, zero), jnp.where(low, zero, block)], axis=0)


def upright(block):
    return jnp.concatenate([block[:, :128], block[:, 128:]], axis=0)


def attention_kernel(place, x_ref, *refs):
    pieces = refs[:8]
    qkv_ref, probs_ref, heads_ref, norm_ref, scale_ref, vec_ref, wout_hbm = refs[8:15]
    wqkv, wout, wvec, sems = refs[15:]
    step = pl.program_id(0)

    @pl.when(step == 0)
    def _():
        for core in range(2):

            @pl.when(place[0] == core)
            def _(core=core):
                for part in range(3):
                    for half in range(2):
                        first = max(768 * part, 1152 * half)
                        width = min(768 * part + 768, 1152 * half + 1152) - first
                        if width > 0:
                            mine = pieces[:4] if half == core else pieces[4:]
                            target = (wqkv, first, first - 1152 * half, width, 1)
                            piece_copies(place, core, half, mine, [target], sems.at[pl.ds(part, 1)])
                    if part == 0:
                        piece_copies(place, core, core, pieces[:4], [(wvec, 0, 1152, 128, 1)], sems.at[pl.ds(3, 1)])

        all_piece_copies(place, pieces, ((wout, 1280, 384, 1),), sems.at[pl.ds(4, 1)])
        wait_whole(wvec, sems.at[3])
        vec_ref[...] = flat(wvec[...]).astype(F32).T[:16]

    x = x_ref[...]
    for n in range(3):

        @pl.when(step == 0)
        def _():
            wait_whole(wqkv.at[:, :, :, :, pl.ds(n * WIDTH, WIDTH)], sems.at[n])

        part = dot(x, flat(wqkv[:, :, :, :, n * WIDTH : (n + 1) * WIDTH]))
        if n != 1:
            part = part + vec_ref[n // 2 : n // 2 + 1, :]
        qkv_ref[:, n * WIDTH : (n + 1) * WIDTH] = part.astype(BF16)
    low = pair_masks()
    for s in range(BLOCK // 128):
        rows = slice(128 * s, 128 * s + 128)
        for h in range(HEADS // 2):
            cols = slice(128 * h, 128 * h + 128)
            query = both_heads(qkv_ref[rows, 128 * h : 128 * h + 128] * BF16(0.125), low)
            keyed = qkv_ref[rows, WIDTH + 128 * h : WIDTH + 128 * h + 128]
            valued = qkv_ref[rows, 2 * WIDTH + 128 * h : 2 * WIDTH + 128 * h + 128]
            scores = dot(keyed, query, NT)
            weight = jnp.exp(scores - jnp.max(scores, axis=0, keepdims=True))
            probs = (weight * (1.0 / jnp.sum(weight, axis=0, keepdims=True))).astype(BF16)
            probs_ref[s, h] = probs
            heads_ref[rows, cols] = dot(upright(probs), both_heads(valued, low), TN).astype(BF16)

    @pl.when(step == 0)
    def _():
        wait_whole(wout, sems.at[4])
        pltpu.make_async_copy(wout, wout_hbm, sems.at[5]).start()

    attn = dot(heads_ref[...], flat(wout[...])) + vec_ref[2:3, :]
    norm, scale = normalize(x.astype(F32) + attn)
    norm_ref[...] = norm
    scale_ref[...] = jnp.broadcast_to(scale, scale_ref.shape)

    @pl.when(step == STEPS - 1)
    def _():
        pltpu.make_async_copy(wout, wout_hbm, sems.at[5]).wait()


def attention_forward(place, rows, pieces):
    return call(
        attention_kernel,
        [place, rows, *pieces],
        [smem_spec(), row_spec(WIDTH)] + [any_spec()] * 8,
        [
            shape((ROWS, 3 * WIDTH)),
            shape((ROWS // 128, HEADS // 2, 128, 256)),
            shape((ROWS, WIDTH)),
            shape((ROWS, WIDTH), F32),
            shape((ROWS, 128), F32),
            shape((16, WIDTH), F32),
            shape(ORDER + (WIDTH,)),
        ],
        [
            row_spec(3 * WIDTH),
            pl.BlockSpec((BLOCK // 128, HEADS // 2, 128, 256), lambda i: (i, 0, 0, 0)),
            row_spec(WIDTH),
            row_spec(WIDTH),
            row_spec(128),
            one_spec(16, WIDTH),
            any_spec(),
        ],
        20,
        grid=(STEPS,),
        scratch=[
            pltpu.VMEM(ORDER + (3 * WIDTH,), BF16),
            pltpu.VMEM(ORDER + (WIDTH,), BF16),
            pltpu.VMEM(ORDER + (128,), BF16),
            pltpu.SemaphoreType.DMA((6,)),
        ],
    )


def wide_scale(ref):
    return jnp.concatenate([ref[...]] * 6, axis=1)


def hidden_of(norm, vec_ref):
    return norm * vec_ref[3:4, :] + vec_ref[4:5, :]


def gelu_parts(upper):
    phi = 0.5 * (1.0 + lax.erf(upper * 0.7071067811865476))
    bell = jnp.exp(-0.5 * upper * upper) * 0.3989422804014327
    return upper * phi, phi + upper * bell


def contrast_kernel(first_ref, received_ref, keep_ref, partner_ref, dfirst_ref, dreceived_ref):
    first = first_ref[...]
    received = received_ref[...].astype(F32)
    logits = lax.dot_general(first, received, NT, precision=lax.Precision.HIGHEST, preferred_element_type=F32)
    logits = logits * logit_scale
    weight = jnp.exp(logits - jnp.max(logits, axis=-1, keepdims=True))
    soft = weight / jnp.sum(weight, axis=-1, keepdims=True)
    column = lax.broadcasted_iota(jnp.int32, (8, 8), 1)
    chosen = jnp.where(column == partner_ref[...], 1.0, 0.0)
    dlogits = (contrast_weight * logit_scale) * keep_ref[...] * (soft - chosen)
    high = lax.Precision.HIGHEST
    dfirst_ref[...] = lax.dot_general(dlogits, received, NN, precision=high, preferred_element_type=F32)
    dreceived_ref[...] = lax.dot_general(
        dlogits, first, TN, precision=high, preferred_element_type=F32
    ).astype(BF16)


def contrast_back(first, received, keep, partner, deps):
    return call(
        contrast_kernel,
        [Loose(first), Loose(received), Loose(keep), Loose(partner)],
        [full_spec()] * 4,
        [loose((8, WIDTH), F32), loose((8, WIDTH))],
        [full_spec()] * 2,
        4,
        deps=deps,
    )


CHUNK = 512
CHUNKS = INNER // CHUNK


def chunk(n):
    return slice(n * CHUNK, (n + 1) * CHUNK)


def feed_forward_rows(hidden, vec_ref, b_in_ref, size, win_part, wdown_part, put):
    hidden_low = hidden.astype(BF16)
    down, active = hidden + vec_ref[5:6, :], None
    after = dot(hidden_low, win_part(0))
    for n in range(INNER // size):
        upper = after + b_in_ref[:, n * size : (n + 1) * size]
        if (n + 1) * size < INNER:
            after = dot(hidden_low, win_part(n + 1))
        if n > 0:
            down = down + dot(active, wdown_part(n - 1))
        active, slope = gelu_parts(upper)
        active = active.astype(BF16)
        put(slice(n * size, (n + 1) * size), active, slope.astype(BF16))
    down = down + dot(active, wdown_part(INNER // size - 1))
    return normalize(down)


def put_norm(first_span, count, norm, scale, vec_ref, norm_two_ref, scale_ref, mixed_ref):
    norm_two_ref[...] = norm.astype(BF16)
    scale_ref[...] = jnp.broadcast_to(scale, scale_ref.shape)
    final = norm * vec_ref[6:7, :] + vec_ref[7:8, :]
    for s in range(norm.shape[0] // 128):
        rows = slice(128 * s, 128 * s + 128)
        live = jnp.where(first_span + s < count[0], 1.0, 0.0)
        mixed_ref[rows, :] = (final[rows] * live).astype(BF16)


def feed_forward_first_kernel(place, count, norm_ref, norm_hbm, vec_ref, b_in_ref, keep_ref, *refs):
    pieces = refs[:8]
    first_ref, sent_ref, win, wdown, hidden_ref, active_ref, slope_ref, norm_two_ref, scale_ref, mixed_ref = refs[8:18]
    tops, sems, tops_sem = refs[18:]
    for s in range(8):
        pltpu.make_async_copy(norm_hbm.at[pl.ds(128 * s, 8)], tops.at[pl.ds(8 * s, 8)], tops_sem).start()
    all_piece_copies(place, pieces, ((win, 0, 1536, 1),), sems)
    all_piece_copies(place, pieces, ((wdown, 1536, 384, 4),), sems.at[pl.ds(1, 1)])
    wait_whole(tops, tops_sem)
    top = hidden_of(jnp.concatenate([tops[8 * s : 8 * s + 1, :] for s in range(8)], axis=0), vec_ref)
    hidden = hidden_of(norm_ref[...], vec_ref)
    hidden_ref[:TALL, :] = hidden.astype(BF16)
    hidden = jnp.concatenate([hidden, top, jnp.zeros_like(top)], axis=0)
    wait_whole(win, sems.at[0])

    def win_part(n):
        return flat(win[:, :, :, :, n * WIDTH : (n + 1) * WIDTH])

    def wdown_part(n):
        if n == 0:
            wait_whole(wdown, sems.at[1])
        return flat(wdown[n // 2, 2 * (n % 2) : 2 * (n % 2) + 2])

    def put(cols, active, slope):
        active_ref[:TALL, cols] = active[:TALL]
        slope_ref[:TALL, cols] = slope[:TALL]

    norm, scale = feed_forward_rows(hidden, vec_ref, b_in_ref, WIDTH, win_part, wdown_part, put)
    put_norm(0, count, norm[:TALL], scale[:TALL], vec_ref, norm_two_ref, scale_ref, mixed_ref)
    final = norm[TALL : TALL + 8] * vec_ref[6:7, :] + vec_ref[7:8, :]
    first_ref[...] = final
    sent_ref[...] = (final.astype(BF16).astype(F32) * keep_ref[...]).astype(BF16)


def feed_forward_shapes():
    return [
        near((ROWS, WIDTH)),
        near((ROWS, INNER)),
        near((ROWS, INNER)),
        shape((ROWS, WIDTH)),
        shape((ROWS, 128), F32),
        shape((ROWS, WIDTH)),
    ]


def feed_forward_first(place, count, norm, vec, b_in, keep, pieces):
    def rows(width):
        return pl.BlockSpec((TALL, width), lambda i: (0, 0))

    return call(
        feed_forward_first_kernel,
        [place, count, norm, norm, vec, b_in, keep, *pieces],
        [smem_spec(), smem_spec(), rows(WIDTH), any_spec()] + [full_spec()] * 3 + [any_spec()] * 8,
        [
            shape((8, WIDTH), F32),
            loose((8, WIDTH)),
            near(ORDER + (INNER,)),
            near((2, 4, 4, 4, HALF_UNIT, WIDTH)),
        ]
        + feed_forward_shapes(),
        [full_spec()] * 7 + [rows(WIDTH), rows(128), rows(WIDTH)],
        24,
        grid=(1,),
        scratch=[
            pltpu.VMEM((64, WIDTH), F32),
            pltpu.SemaphoreType.DMA((2,)),
            pltpu.SemaphoreType.DMA,
        ],
    )


def feed_forward_kernel(index, count, norm_ref, vec_ref, b_in_ref, win, wdown, *refs):
    hidden_ref, active_ref, slope_ref, norm_two_ref, scale_ref, mixed_ref = refs[-6:]
    here = slice(index * BLOCK, (index + 1) * BLOCK)
    hidden = hidden_of(norm_ref[...], vec_ref)
    hidden_ref[here, :] = hidden.astype(BF16)

    def put(cols, active, slope):
        active_ref[here, cols] = active
        slope_ref[here, cols] = slope

    norm, scale = feed_forward_rows(
        hidden, vec_ref, b_in_ref, CHUNK, lambda n: win[:, chunk(n)], lambda n: wdown[chunk(n), :], put
    )
    put_norm(index * (BLOCK // 128), count, norm, scale, vec_ref, norm_two_ref, scale_ref, mixed_ref)


def feed_forward(index, count, norm, vec, b_in, win, wdown, so_far, deps=()):
    def rows(width):
        return pl.BlockSpec((BLOCK, width), lambda i: (index, 0))

    return call(
        functools.partial(feed_forward_kernel, index),
        [count, norm, vec, b_in, Near(win), Near(wdown)] + [Near(v) if n < 3 else v for n, v in enumerate(so_far)],
        [smem_spec(), rows(WIDTH)] + [full_spec()] * 7 + [any_spec()] * 3,
        feed_forward_shapes(),
        [full_spec()] * 3 + [rows(WIDTH), rows(128), rows(WIDTH)],
        20,
        grid=(1,),
        input_output_aliases={6 + n: n for n in range(6)},
        deps=deps,
    )


def feed_forward_back_kernel(
    count, cot_ref, dfirst_ref, back_ref, keep_ref, norm_ref, scale_ref, vec_ref, slope_ref, wdown, dres_ref, ddown_ref, dupper_ref, sums_ref, db_in_ref
):
    step = pl.program_id(0)
    dfirst = dfirst_ref[...] + back_ref[...].astype(F32) * keep_ref[...]
    slot = lax.broadcasted_iota(jnp.int32, (8, 1), 0)
    blocks = TALL // BLOCK

    def here(b):
        return pl.ds(pl.multiple_of(step * TALL + b * BLOCK, BLOCK), BLOCK)

    def norm_back(b):
        parts = []
        for s in range(BLOCK // 128):
            row = b * BLOCK + 128 * s
            span = step * (TALL // 128) + b * (BLOCK // 128) + s
            live = jnp.where(span < count[0], 1.0, 0.0)
            mine = jnp.sum(jnp.where(slot == span, dfirst, 0.0), axis=0, keepdims=True)
            cot = cot_ref[row : row + 128, :].astype(F32) * live
            top = cot[:8] + jnp.where(slot == 0, mine, 0.0)
            parts += [top, cot[8:]]
        dfinal = jnp.concatenate(parts, axis=0)
        rows = slice(b * BLOCK, (b + 1) * BLOCK)
        norm = norm_ref[rows, :].astype(F32)
        scale = jnp.concatenate([scale_ref[rows, :]] * 6, axis=1)
        dres = normalize_back(dfinal * vec_ref[6:7, :], norm, scale)
        dres_ref[here(b), :] = dres
        ddown = dres.astype(BF16)
        ddown_ref[here(b), :] = ddown
        return ddown, [column_sum(dfinal * norm), column_sum(dfinal), column_sum(dres)]

    jobs = [(b, n) for b in range(blocks) for n in range(CHUNKS)]
    ready, sums, sums_in = norm_back(0), [], [[] for _ in range(blocks)]
    sums.append(ready[1])
    ddown = ready[0]
    after = dot(ddown, wdown[chunk(0), :], NT)
    for k, (b, n) in enumerate(jobs):
        dactive = after
        if n == 0 and b + 1 < blocks:
            ready = norm_back(b + 1)
            sums.append(ready[1])
        if k + 1 < len(jobs):
            if n + 1 == CHUNKS:
                ddown = ready[0]
            after = dot(ddown, wdown[chunk(jobs[k + 1][1]), :], NT)
        dupper = dactive * slope_ref[here(b), chunk(n)].astype(F32)
        dupper_ref[here(b), chunk(n)] = dupper.astype(BF16)
        sums_in[b].append(column_sum(dupper))
    add_rows(sums_ref, step, *[sum(group) for group in zip(*sums)])
    add_rows(db_in_ref, step, sum(jnp.concatenate(parts, axis=1) for parts in sums_in))


def feed_forward_back(count, cotangent, dfirst, back, keep, norm, scale, vec, slope, wdown):
    return call(
        feed_forward_back_kernel,
        [count, cotangent, Loose(dfirst), Loose(back), Loose(keep), norm, scale, vec, Near(slope), Near(wdown)],
        [smem_spec(), tall_spec(WIDTH), full_spec(), full_spec(), full_spec(), tall_spec(WIDTH), tall_spec(128)]
        + [full_spec()] * 3,
        [
            near((ROWS, WIDTH), F32),
            near((ROWS, WIDTH)),
            near((ROWS, INNER)),
            shape((24, WIDTH), F32),
            shape((8, INNER), F32),
        ],
        [full_spec(), full_spec(), full_spec(), one_spec(24, WIDTH), one_spec(8, INNER)],
        20,
        grid=(ROWS // TALL,),
        input_output_aliases={8: 2},
    )


def hidden_back_kernel(
    dres_ref, dupper_ref, norm_ref, scale_ref, vec_ref, win, wout, dres_one_ref, dattn_ref, dheads_ref, sums_ref
):
    step = pl.program_id(0)
    count = TALL // BLOCK

    def here(n):
        return pl.ds(pl.multiple_of(step * TALL + n * BLOCK, BLOCK), BLOCK)

    def product(n):
        return dot(dupper_ref[here(n), :], win[...], NT)

    after, sums = product(0), []

    for n in range(count):
        rows = slice(n * BLOCK, (n + 1) * BLOCK)
        dhidden = dres_ref[here(n), :] + after
        if n + 1 < count:
            after = product(n + 1)
        norm = norm_ref[rows, :]
        scale = jnp.concatenate([scale_ref[rows, :]] * 6, axis=1)
        dres = normalize_back(dhidden * vec_ref[3:4, :], norm, scale)
        dres_one_ref[rows, :] = dres
        dattn = dres.astype(BF16)
        dattn_ref[rows, :] = dattn
        dheads_ref[rows, :] = dot(dattn, flat(wout[...]), NT).astype(BF16)
        sums.append([column_sum(dhidden * norm), column_sum(dhidden), column_sum(dres)])
    add_rows(sums_ref, step, *[sum(group) for group in zip(*sums)])


def hidden_back(dres, dupper, norm, scale, vec, win, wout, deps):
    return call(
        hidden_back_kernel,
        [Near(dres), Near(dupper), norm, scale, vec, Near(win), wout],
        [full_spec(), full_spec(), tall_spec(WIDTH), tall_spec(128)] + [full_spec()] * 3,
        [shape((ROWS, WIDTH), F32), shape((ROWS, WIDTH)), shape((ROWS, WIDTH)), shape((24, WIDTH), F32)],
        [tall_spec(WIDTH), tall_spec(WIDTH), tall_spec(WIDTH), one_spec(24, WIDTH)],
        22,
        grid=(ROWS // TALL,),
        deps=deps,
    )


def attention_back_kernel(qkv_ref, probs_ref, dheads_ref, dqkv_ref, near_ref, sums_ref):
    step = pl.program_id(0)
    low = pair_masks()
    for s in range(BLOCK // 128):
        rows = slice(128 * s, 128 * s + 128)
        for h in range(HEADS // 2):
            query = both_heads(qkv_ref[rows, 128 * h : 128 * h + 128] * BF16(0.125), low)
            keyed = qkv_ref[rows, WIDTH + 128 * h : WIDTH + 128 * h + 128]
            valued = qkv_ref[rows, 2 * WIDTH + 128 * h : 2 * WIDTH + 128 * h + 128]
            dheads = both_heads(dheads_ref[rows, 128 * h : 128 * h + 128], low)
            probs_low = probs_ref[s, h]
            probs = probs_low.astype(F32)
            dprobs = dot(valued, dheads, NT)
            inner = jnp.sum(probs * dprobs, axis=0, keepdims=True)
            dscores = (probs * (dprobs - inner)).astype(BF16)
            dquery = dot(upright(dscores), both_heads(keyed * BF16(0.125), low), TN)
            dqkv_ref[rows, 128 * h : 128 * h + 128] = dquery.astype(BF16)
            dqkv_ref[rows, WIDTH + 128 * h : WIDTH + 128 * h + 128] = dot(dscores, query).astype(BF16)
            dqkv_ref[rows, 2 * WIDTH + 128 * h : 2 * WIDTH + 128 * h + 128] = dot(probs_low, dheads).astype(BF16)
    near_ref[block_rows(step, BLOCK), :] = dqkv_ref[...]
    add_rows(
        sums_ref,
        step,
        column_sum(dqkv_ref[:, :WIDTH].astype(F32)),
        column_sum(dqkv_ref[:, 2 * WIDTH :].astype(F32)),
    )


def attention_back(qkv, probs, dheads, deps):
    return call(
        attention_back_kernel,
        [qkv, probs, dheads],
        [
            row_spec(3 * WIDTH),
            pl.BlockSpec((BLOCK // 128, HEADS // 2, 128, 256), lambda i: (i, 0, 0, 0)),
            row_spec(WIDTH),
        ],
        [shape((ROWS, 3 * WIDTH)), near((ROWS, 3 * WIDTH)), shape((16, WIDTH), F32)],
        [row_spec(3 * WIDTH), full_spec(), one_spec(16, WIDTH)],
        16,
        grid=(STEPS,),
        deps=deps,
    )


def tokens_back_kernel(place, dres_ref, dqkv_ref, *refs):
    pieces, (out_ref, wqkv, sems) = refs[:8], refs[8:]

    @pl.when(pl.program_id(0) == 0)
    def _():
        all_piece_copies(place, pieces, ((wqkv, 0, 1152, 1),), sems)
        wait_whole(wqkv, sems.at[0])

    out_ref[...] = (dres_ref[...] + dot(dqkv_ref[...], flat(wqkv[...]), NT)).astype(BF16)


def tokens_back(place, dres, dqkv, pieces, deps):
    return call(
        tokens_back_kernel,
        [place, dres, dqkv, *pieces],
        [smem_spec(), row_spec(WIDTH), row_spec(3 * WIDTH)] + [any_spec()] * 8,
        shape((ROWS, WIDTH)),
        row_spec(WIDTH),
        14,
        grid=(STEPS,),
        scratch=[pltpu.VMEM(ORDER + (3 * WIDTH,), BF16), pltpu.SemaphoreType.DMA((1,))],
        deps=deps,
    )


def put_unit(place, both, half, unit, p, cols, value):
    side = place[0] if half == 0 else 1 - place[0]
    both[side, place[1 + 16 * half + unit], p, :, cols] = value.astype(BF16)


def put_units(place, both, half, cols, value):
    for p in range(2):
        for unit in range(16):
            row = 384 * p + HALF_UNIT * unit
            put_unit(place, both, half, unit, p, cols, value[row : row + HALF_UNIT])


def write_half(place, both, half, outs, sem, cols):
    for core in range(2):

        @pl.when(place[0] == core)
        def _(side=half ^ core):
            pltpu.make_async_copy(both.at[side, :, :, :, cols], outs[side].at[:, :, :, cols], sem).start()


def run_ahead(jobs):
    after = jobs[0][0]()
    for n, (_, use) in enumerate(jobs):
        value = after
        if n + 1 < len(jobs):
            after = jobs[n + 1][0]()
        use(value)


def layer_grads_kernel(place, active_ref, ddown_ref, hidden_ref, dupper_ref, own, theirs, both, sem):
    outs = (own, theirs)

    def in_job(h, n):
        cols = slice(768 * n, 768 * n + 768)

        def product():
            first = 1536 * h + 768 * n
            return dot(hidden_ref[...], dupper_ref[:, first : first + 768], TN)

        return product, lambda value: put_units(place, both, h, cols, value)

    def down_job(n):
        def product():
            return dot(active_ref[:, WIDTH * n : WIDTH * n + WIDTH], ddown_ref[...], TN)

        def use(value):
            for h in range(2):
                for i in range(2):
                    for y in range(4):
                        for j in range(4):
                            row = 384 * i + 96 * y + HALF_UNIT * j
                            part = value[row : row + HALF_UNIT, 384 * h : 384 * h + 384]
                            cols = slice(1536 + 384 * j, 1536 + 384 * j + 384)
                            put_unit(place, both, h, 4 * (2 * (n % 2) + i) + y, n // 2, cols, part)

        return product, use

    def write(p, cols):
        for side in (1, 0):
            pltpu.make_async_copy(both.at[side, :, p, :, cols], outs[side].at[:, p, :, cols], sem).start()

    run_ahead([in_job(h, n) for h in range(2) for n in range(2)])
    write(0, slice(0, 1536))
    write(1, slice(0, 1536))
    run_ahead([down_job(n) for n in range(2)])
    write(0, slice(1536, 3072))
    run_ahead([down_job(n) for n in range(2, 4)])
    write(1, slice(1536, 3072))
    wait_whole(both, sem)


def layer_grads(place, active, ddown, hidden_low, dupper):
    return call(
        layer_grads_kernel,
        [place, Near(active), Near(ddown), Near(hidden_low), Near(dupper)],
        [smem_spec()] + [full_spec()] * 4,
        [shape((16, 2, HALF_UNIT, 3072)), loose((16, 2, HALF_UNIT, 3072))],
        [any_spec(), any_spec()],
        20,
        scratch=[pltpu.VMEM((2, 16, 2, HALF_UNIT, 3072), BF16), pltpu.SemaphoreType.DMA],
    )


def every_fourth(line, j):
    blocks = jnp.concatenate([line[:, 512 * n : 512 * n + 512] for n in range(6)] + [jnp.zeros((2, 512), F32)], axis=0)
    row = lax.broadcasted_iota(jnp.int32, (512, 128), 0)
    lane = lax.broadcasted_iota(jnp.int32, (512, 128), 1)
    pick = jnp.where(row == 4 * lane + j, 1.0, 0.0)
    picked = lax.dot_general(blocks, pick, NN, precision=lax.Precision.HIGHEST, preferred_element_type=F32)
    return jnp.concatenate([picked[n : n + 1] for n in range(6)], axis=1)


def attention_grads_kernel(
    place, x_hbm, dqkv_ref, heads_hbm, dattn_hbm, sums_qkv, sums_one, sums_two, db_in, own, theirs, both, x, heads, dattn, sems
):
    pairs = ((x_hbm, x), (heads_hbm, heads), (dattn_hbm, dattn))
    loads = [pltpu.make_async_copy(far, here, sems.at[n]) for n, (far, here) in enumerate(pairs)]
    for load in loads:
        load.start()
    outs, done = (own, theirs), sems.at[3]

    def total(ref, n):
        return jnp.sum(ref[8 * n : 8 * n + 8, :], axis=0, keepdims=True)

    rows = [total(sums_qkv, 0), total(sums_qkv, 1), total(sums_one, 2), total(sums_one, 0), total(sums_one, 1)]
    rows += [total(sums_two, 2), total(sums_two, 0), total(sums_two, 1)]
    rows += [every_fourth(total(db_in, 0), j) for j in range(4)] + [jnp.zeros((116, WIDTH), F32)]
    wide = jnp.concatenate(rows, axis=0).T
    put_units(place, both, 0, slice(1152, 1280), wide)
    put_units(place, both, 1, slice(1152, 1280), jnp.zeros_like(wide))
    loads[0].wait()

    def job(n):
        def product():
            return dot(x[...], dqkv_ref[:, 768 * n : 768 * n + 768], TN)

        def use(value):
            for m in range(2):
                first = 768 * n + 384 * m
                h, at = first // 1152, first % 1152
                put_units(place, both, h, slice(at, at + 384), value[:, 384 * m : 384 * m + 384])
                write_half(place, both, h, outs, done, slice(at, at + 384))

        return product, use

    def out_product():
        loads[1].wait()
        loads[2].wait()
        return dot(heads[...], dattn[...], TN)

    def out_use(value):
        for h in range(2):
            put_units(place, both, h, slice(1280, FIRST), value[:, 384 * h : 384 * h + 384])
            write_half(place, both, h, outs, done, slice(1152, FIRST))

    run_ahead([job(n) for n in range(3)] + [(out_product, out_use)])
    wait_whole(both, done)


def attention_grads(place, rows, dqkv, heads, dattn, sums, deps):
    sums_qkv, sums_one, sums_two, db_in = sums
    return call(
        attention_grads_kernel,
        [place, rows, Near(dqkv), heads, dattn, sums_qkv, sums_one, sums_two, db_in],
        [smem_spec(), any_spec(), full_spec(), any_spec(), any_spec()] + [full_spec()] * 4,
        [shape((16, 2, HALF_UNIT, FIRST)), loose((16, 2, HALF_UNIT, FIRST))],
        [any_spec(), any_spec()],
        20,
        scratch=[pltpu.VMEM((2, 16, 2, HALF_UNIT, FIRST), BF16)]
        + [pltpu.VMEM((ROWS, WIDTH), BF16)] * 3
        + [pltpu.SemaphoreType.DMA((4,))],
        deps=deps,
    )


def add_kernel(own_hbm, recv_hbm, *refs):
    outs, (own, recv, sems) = refs[:-3], refs[-3:]
    loads = []
    for r in range(4):
        part = pl.ds(4 * r, 4)
        pair = [
            pltpu.make_async_copy(own_hbm.at[part], own.at[part], sems.at[2 * r]),
            pltpu.make_async_copy(recv_hbm.at[part], recv.at[part], sems.at[2 * r + 1]),
        ]
        for load in pair:
            load.start()
        loads.append(pair)
    for r in range(4):
        for load in loads[r]:
            load.wait()
        for k in range(4):
            outs[r][k] = (own[4 * r + k].astype(F32) + recv[4 * r + k].astype(F32)).astype(BF16)


def add_theirs(own, recv, deps):
    width = recv.shape[3]
    buffer = pltpu.VMEM((16, 2, HALF_UNIT, width), BF16)
    return call(
        add_kernel,
        [own, Loose(recv)],
        [any_spec()] * 2,
        [loose((4, 2, HALF_UNIT, width))] * 4,
        [full_spec()] * 4,
        18,
        scratch=[buffer, buffer, pltpu.SemaphoreType.DMA((8,))],
        deps=deps,
    )


OCTET = FIRST + 1536 + 384


def pack_kernel(wqkv_hbm, wout_hbm, win_hbm, wdown_hbm, vec, mask, pick, out_ref, wqkv, wout, win, wdown, sems):
    loads = [
        pltpu.make_async_copy(far, here, sems.at[n])
        for n, (far, here) in enumerate(((wqkv_hbm, wqkv), (wout_hbm, wout), (win_hbm, win), (wdown_hbm, wdown)))
    ]
    for load in loads:
        load.start()
    column = dot((vec[...] * mask[...]).astype(BF16), pick[...])[:6].astype(BF16)
    for load in loads:
        load.wait()
    for h in range(2):
        out_ref[h] = jnp.zeros((8, OCTET), BF16)
        out_ref[h, :6, :1152] = wqkv[:, 1152 * h : 1152 * h + 1152]
        out_ref[h, :6, 1152:1280] = column
        out_ref[h, :6, 1280:FIRST] = wout[:, 384 * h : 384 * h + 384]
        out_ref[h, :6, FIRST : FIRST + 1536] = win[:, 1536 * h : 1536 * h + 1536]
        out_ref[h, :6, FIRST + 1536 :] = wdown[:6, 384 * h : 384 * h + 384]
        for q in range(18):
            row, at = 6 + q // 9, 384 * (q % 9)
            out_ref[h, row : row + 1, at : at + 384] = wdown[6 + q : 7 + q, 384 * h : 384 * h + 384]
    for k in range(2, 8):
        out_ref[k] = out_ref[k % 2]


def pack(wqkv, wout, win, wdown, vectors, b_in):
    vec = jnp.zeros((128,), F32)
    for n, v in enumerate(list(vectors) + [b_in]):
        vec = vec + lax.pad(v.astype(F32), jnp.zeros((), F32), [(6 * n, 128 - 6 * n - v.shape[0], 0)])
    j = np.arange(128)
    r = np.where(j < 48, j % 6, np.where(j < 72, (j - 48) // 4, -1))
    i = np.where(j < 48, j // 6, np.where(j < 72, 8 + (j - 48) % 4, -1))
    mask = (r[None, :] == np.arange(8)[:, None]).astype(np.float32)
    pick = (i[:, None] == np.arange(128)[None, :]).astype(ml_dtypes.bfloat16)
    return call(
        pack_kernel,
        [wqkv, wout, win, wdown, vec.reshape(1, 128), mask, pick],
        [any_spec()] * 4 + [full_spec()] * 3,
        loose((8, 8, OCTET)),
        full_spec(),
        6,
        scratch=[
            pltpu.VMEM((6, 2304), BF16),
            pltpu.VMEM((6, 768), BF16),
            pltpu.VMEM((6, 3072), BF16),
            pltpu.VMEM((24, 768), BF16),
            pltpu.SemaphoreType.DMA((4,)),
        ],
    )


def stack_kernel(cuts, place, *refs):
    parts, outs = refs[:4], refs[4:]
    for q in range(4):
        slot = place[33 + PIECES[q]]
        for n, (first, width) in enumerate(cuts):
            outs[n][slot] = parts[q][:, :, first : first + width]


def stack(place, parts, cuts):
    return call(
        functools.partial(stack_kernel, cuts),
        [place, *[Loose(p) for p in parts]],
        [smem_spec()] + [full_spec()] * 4,
        [loose((4, 2, HALF_UNIT, w)) for _, w in cuts],
        [full_spec()] * len(cuts),
        8,
    )


def gate_kernel(*refs):
    pass


def gate(values, deps):
    return call(
        gate_kernel,
        [Loose(v) for v in values],
        [any_spec()] * len(values),
        [loose(v.shape, v.dtype) for v in values],
        [any_spec()] * len(values),
        2,
        deps=deps,
        input_output_aliases={n: n for n in range(len(values))},
    )


def sum_kernel(sets, more, *refs):
    ins, rest, outs = refs[: 4 * sets], refs[4 * sets : 4 * sets + more], refs[4 * sets + more :]
    for r in range(4):
        first = 0
        for g in range(sets):
            part = ins[4 * g : 4 * g + 4]
            width = part[0].shape[3]
            total = part[0][r].astype(F32)
            for p in part[1:]:
                total = total + p[r].astype(F32)
            outs[r][:, :, first : first + width] = total.astype(BF16)
            first += width
        if more:
            outs[r][:, :, first:] = rest[r][...]


def sum_blocks(parts, more=(), deps=(), weight=0):
    width = parts[0].shape[3] + (more[0].shape[2] if more else 0)
    args = [Loose(p) for p in list(parts) + list(more)]
    return call(
        functools.partial(sum_kernel, 1, len(more)),
        args,
        [full_spec()] * len(args),
        [loose((2, HALF_UNIT, width))] * 4,
        [full_spec()] * 4,
        14,
        deps=deps,
        weight=weight,
    )


def finish_kernel(in_ref, dqkv, dout, din, ddown, *vectors):
    for h in range(2):
        total = in_ref[h].astype(F32)
        for k in range(h + 2, 8, 2):
            total = total + in_ref[k].astype(F32)
        dqkv[:, 1152 * h : 1152 * h + 1152] = total[:6, :1152]
        dout[:, 384 * h : 384 * h + 384] = total[:6, 1280:FIRST]
        din[:, 1536 * h : 1536 * h + 1536] = total[:6, FIRST : FIRST + 1536]
        ddown[:6, 384 * h : 384 * h + 384] = total[:6, FIRST + 1536 :]
        for q in range(18):
            row, at = 6 + q // 9, 384 * (q % 9)
            ddown[6 + q : 7 + q, 384 * h : 384 * h + 384] = total[row : row + 1, at : at + 384]
        if h == 0:
            wide = jnp.concatenate([total[:6, 1152:1280], jnp.zeros((122, 128), F32)], axis=0).T
    for n in range(8):
        vectors[n][...] = wide[n, :6]
    row = lax.broadcasted_iota(jnp.int32, (128, 128), 0)
    lane = lax.broadcasted_iota(jnp.int32, (128, 128), 1)
    b_in = jnp.zeros((8, 128), F32)
    for j in range(4):
        spread = jnp.where(lane == 4 * row + j, 1.0, 0.0)
        line = jnp.concatenate([wide[8 + j : 9 + j]] * 8, axis=0)
        b_in = b_in + lax.dot_general(line, spread, NN, precision=lax.Precision.HIGHEST, preferred_element_type=F32)
    vectors[8][...] = b_in[0, :24]


def finish(blocks):
    return call(
        finish_kernel,
        [Loose(blocks)],
        [full_spec()],
        [shape(d, F32) for d in ((6, 2304), (6, 768), (6, 3072), (24, 768)) + ((6,),) * 8 + ((24,),)],
        [full_spec()] * 13,
        6,
    )


def unpack_kernel(blocks, unit):
    for k in range(8):
        p, j = k // 4, k % 4
        at = FIRST + 1536 + 384 * j
        unit[p, 6 * j : 6 * j + 6, : FIRST + 1536] = blocks[k, :6, : FIRST + 1536]
        unit[p, :6, at : at + 384] = blocks[k, :6, FIRST + 1536 :]
        for q in range(18):
            row, first = 6 + q // 9, 384 * (q % 9)
            unit[p, 6 + q : 7 + q, at : at + 384] = blocks[k, row : row + 1, first : first + 384]


def unpack_octet(blocks):
    return call(
        unpack_kernel,
        [Loose(blocks)],
        [full_spec()],
        loose((2, HALF_UNIT, FIRST + 3072)),
        full_spec(),
        6,
    )


def total_kernel(*refs):
    out = refs[4]
    total = refs[0][...].astype(F32)
    for part in refs[1:4]:
        total = total + part[...].astype(F32)
    total = total.astype(BF16)
    for k in range(8):
        p, j = k // 4, k % 4
        at = FIRST + 1536 + 384 * j
        out[k] = jnp.zeros((8, OCTET), BF16)
        out[k, :6, : FIRST + 1536] = total[p, 6 * j : 6 * j + 6, : FIRST + 1536]
        out[k, :6, FIRST + 1536 :] = total[p, :6, at : at + 384]
        for q in range(18):
            row, first = 6 + q // 9, 384 * (q % 9)
            out[k, row : row + 1, first : first + 384] = total[p, 6 + q : 7 + q, at : at + 384]


def total_blocks(parts):
    return call(
        total_kernel, [Loose(p) for p in parts], [full_spec()] * 4, loose((8, 8, OCTET)), full_spec(), 6
    )


def per_device(
    tokens,
    cotangent,
    span_counts,
    single_flags,
    partner_slots,
    w_qkv,
    b_query,
    b_value,
    w_out,
    b_out,
    gain_attn,
    shift_attn,
    w_in,
    b_in,
    w_down,
    b_down,
    gain_ffn,
    shift_ffn,
):
    place = my_place()
    packed = pack(
        w_qkv, w_out, w_in, w_down, [b_query, b_value, b_out, gain_attn, shift_attn, b_down, gain_ffn, shift_ffn], b_in
    )
    rows48 = exchange_octet(packed)
    unit = unpack_octet(rows48)
    one_early, two_early = stack(place, gather(unit, 0), ((0, FIRST), (FIRST, 3072)))
    one_late = gather(one_early, 1)
    one_pieces = one_late + [to_core(piece) for piece in one_late]
    two_late = gather(two_early, 1)

    count = span_counts[0]
    live = (jnp.arange(8, dtype=jnp.int32) < count).astype(F32)
    keep = (live * (1.0 - single_flags[0].astype(F32)))[:, None]
    partner = partner_slots[0][:, None]
    rows = tokens.reshape(ROWS, WIDTH)

    qkv, probs, heads, norm_one, scale_one, vec, wout = attention_forward(place, rows, one_pieces)
    full_b_in = vec[8:12].T.reshape(1, INNER)
    two_late = [two_late[0], *gate(two_late[1:], [vec])]
    first, sent, win, wdown, *so_far = feed_forward_first(
        place, count, norm_one, vec, full_b_in, keep, two_late + [to_core(piece) for piece in two_late]
    )
    win, wdown = win.reshape(WIDTH, INNER), wdown.reshape(INNER, WIDTH)
    partners = [(d, d ^ 64) for d in range(128)]
    received = send(sent, partners)
    so_far = feed_forward(2, count, norm_one, vec, full_b_in, win, wdown, so_far)
    dfirst, dreceived = contrast_back(first, received, keep, partner, [so_far[4]])
    returned = send(dreceived, partners)
    hidden_low, active, slope, norm_two, scale_two, mixed = feed_forward(
        3, count, norm_one, vec, full_b_in, win, wdown, so_far, [Loose(dreceived)]
    )
    dres_two, ddown, dupper, sums_two, db_in = feed_forward_back(
        count, cotangent.reshape(ROWS, WIDTH), dfirst, returned, keep, norm_two, scale_two, vec, slope, wdown
    )
    two_mine, two_out = layer_grads(place, active, ddown, hidden_low, dupper)
    two_recv = to_core(two_out)
    dres_one, dattn, dheads, sums_one = hidden_back(
        dres_two, dupper, norm_one, scale_one, vec, win, wout, [Loose(two_out)]
    )
    two_own = add_theirs(two_mine, two_recv, [sums_one])
    two_parts = scatter_sends(two_own, 1)
    dqkv, dqkv_near, sums_qkv = attention_back(qkv, probs, dheads, [Loose(two_own[0])])
    sums = (sums_qkv, sums_one, sums_two, db_in)
    one_mine, one_out = attention_grads(place, rows, dqkv_near, heads, dattn, sums, [])
    one_recv = to_core(one_out)
    late = sum_blocks(two_parts, deps=[one_mine], weight=3e10)
    one_own = add_theirs(one_mine, one_recv, [Loose(late[0])])
    one_parts = scatter_sends(one_own, 1)
    grad_tokens = tokens_back(place, dres_one, dqkv, one_pieces, [Loose(one_own[0])])
    back = total_blocks(scatter_sends(sum_blocks(one_parts, late, deps=[grad_tokens]), 0))
    dqkv_own, dout_own, din_own, ddown_own, *vectors = finish(exchange_octet(back))
    return (
        mixed.reshape(tokens.shape),
        grad_tokens.reshape(tokens.shape),
        dqkv_own,
        vectors[0],
        vectors[1],
        dout_own,
        vectors[2],
        vectors[3],
        vectors[4],
        din_own,
        vectors[8],
        ddown_own,
        vectors[5],
        vectors[6],
        vectors[7],
    )


def solution(mesh):
    return jax.shard_map(
        per_device,
        mesh=mesh,
        in_specs=(
            P("pair", "dp", None, None),
            P("pair", "dp", None, None),
            P("pair", "dp"),
            P("pair", "dp"),
            P("pair", "dp"),
            P(("pair", "dp"), None),
            P(("pair", "dp")),
            P(("pair", "dp")),
            P(("pair", "dp"), None),
            P(("pair", "dp")),
            P(("pair", "dp")),
            P(("pair", "dp")),
            P(("pair", "dp"), None),
            P(("pair", "dp")),
            P(("pair", "dp"), None),
            P(("pair", "dp")),
            P(("pair", "dp")),
            P(("pair", "dp")),
        ),
        out_specs=(
            P("pair", "dp", None, None),
            P("pair", "dp", None, None),
            P(("pair", "dp"), None),
            P(("pair", "dp")),
            P(("pair", "dp")),
            P(("pair", "dp"), None),
            P(("pair", "dp")),
            P(("pair", "dp")),
            P(("pair", "dp")),
            P(("pair", "dp"), None),
            P(("pair", "dp")),
            P(("pair", "dp"), None),
            P(("pair", "dp")),
            P(("pair", "dp")),
            P(("pair", "dp")),
        ),
        check_vma=False,
    )
```
